32 devices in a mesh: groups: 2 (over x), row: 16 (over z, y, core).
Axes of the slice: x: 2, y: 2, z: 4, core: 2. Of those that a mesh axis runs over, the one named last changes fastest.
Arguments:
- pair_acts: bfloat16 [96, 48, 128], P(('groups', 'row')), parts along dimension 0, may hold values from -6 to 6
- res_mask: int32 [96], P('groups'), parts along dimension 0, may hold values 0 or 1
- chain_id: int32 [96], P('groups'), parts along dimension 0, may hold values from 0 to 3, never falling along the last dimension, each value on 1 to 24 neighbouring positions
- in_gain: float32 [128], replicated, may hold values from 0.1 to 1.9
- w_left: bfloat16 [128, 256], replicated, may hold values from -0.5 to 0.5
- w_right: bfloat16 [128, 256], replicated, may hold values from -0.5 to 0.5
- w_mult_gate: bfloat16 [128, 128], replicated, may hold values from -0.5 to 0.5
- mult_gain: float32 [128], replicated, may hold values from 0.1 to 1.9
- w_mult_out: bfloat16 [128, 128], replicated, may hold values from -0.5 to 0.5
- att_gain: float32 [128], replicated, may hold values from 0.1 to 1.9
- w_att: bfloat16 [128, 512], replicated, may hold values from -0.5 to 0.5
- w_pair_bias: bfloat16 [128, 4], replicated, may hold values from -0.5 to 0.5
- cross_bias: float32 [4], replicated, may hold values from -2 to 2
- w_att_out: bfloat16 [128, 128], replicated, may hold values from -0.5 to 0.5
Outputs:
- pair_out: bfloat16 [96, 48, 128], P(('groups', 'row')), parts along dimension 0
The draws below stay inside these ranges and needn't reach their ends.
There are 2 independent parts, one for each index of `groups`. The reference program is written for one: setup_inputs(seed, part) draws one part's arguments, and reference() takes and returns one part's arrays. A program takes and returns all parts, laid end to end along the dimension named above; an argument that names none is the same for every part. Nothing has to cross between parts.
Inputs may be any that keep to these rules, and one draw needn't show every extreme that they name: `res_mask`: 1 marks a residue that is present, 0 a padded or missing one. `chain_id`: chains are contiguous runs of residues numbered from 0 in order; each has 1 to 24 residues and every number below 4 occurs.
All inputs are finite; a program needn't handle non-finite values.
Results may differ from the reference program's by a relative error of at most 0.0085.
Values may be sent and summed in bfloat16 or wider, within the bound.
No kernel may reach another device: no remote copies, remote signals or barrier semaphores. Data moves between devices by JAX's collectives and lax.ppermute only.
A program may use at most 64 MiB of HBM per device.

```python
import math
import jax
import jax.numpy as jnp
import numpy as np
from jax import lax

C = 128
CM = 128
H = 4
DH = 32
CHAINS = 4
NRES = 48


def with_ends(drawn, key, least, high):
    spot = [jax.random.randint(jax.random.fold_in(key, axis), (), 0, length) for axis, length in enumerate(drawn.shape)]
    main_axis = drawn.shape.index(max(drawn.shape))
    beside = spot[:main_axis] + [(spot[main_axis] + 1) % drawn.shape[main_axis]] + spot[main_axis + 1:]
    return drawn.at[tuple(spot)].set(least).at[tuple(beside)].set(high)


def block_scale(own_key, shape, split, low, largest):
    def one(dim, parts):
        heights = jax.random.uniform(jax.random.fold_in(jax.random.fold_in(own_key, 6), dim), (parts,), jnp.float32, low / len(split), largest / len(split))
        return jnp.repeat(jnp.exp(heights), shape[dim] // parts).reshape((-1,) + (1,) * (len(shape) - dim - 1))

    factor_of = one(*split[0])
    for cut in split[1:]:
        factor_of = factor_of * one(*cut)
    return factor_of


def profile(count, total, limit, skew):
    portions = [(1 << 20) // math.isqrt(rank ** skew) + 1 for rank in range(2, count + 1)]
    spare, counts = total - limit - (count - 1), [1] * (count - 1)
    while spare > 0:
        movable = [i for i in range(count - 1) if counts[i] < limit]
        mass, left = sum([portions[i] for i in movable]), spare
        for i in movable:
            more = min(limit - counts[i], max(1, left * portions[i] // mass), spare)
            counts[i] = counts[i] + more
            spare = spare - more
    return np.array([limit] + counts)


def uneven(own_key, count, total, bound, skew):
    if count == 2:
        one = jax.random.randint(own_key, (), max(1, total - bound), min(bound, total - 1) + 1)
        return jnp.stack([one, total - one])
    tallies = jnp.asarray(profile(count, total, bound, skew), jnp.int32)
    twos = (count - 1) // 2
    donor, taker = tallies[1:1 + 2 * twos:2], tallies[2:2 + 2 * twos:2]
    room = jnp.minimum(donor - 1, bound - taker)
    moved = jax.random.randint(jax.random.fold_in(own_key, 1), (twos,), 0, 1 << 20) % (room + 1)
    tallies = tallies.at[1:1 + 2 * twos:2].set(donor - moved).at[2:2 + 2 * twos:2].set(taker + moved)
    return tallies[jax.random.permutation(jax.random.fold_in(own_key, 2), count)]


def gaussian(rng, dims, deviation, limit, pieces=(), held_as=jnp.bfloat16):
    array = deviation * jax.random.normal(rng, dims, jnp.float32)
    if pieces:
        array = array * block_scale(rng, dims, pieces, -0.22, 0.18)
    return jnp.clip(array, -limit, limit).astype(held_as)


def setup_inputs(seed: int = 0, part: int = 0) -> dict:
    arg_keys = jax.random.split(jax.random.key(seed), 15)
    part_keys = jax.random.split(jax.random.fold_in(arg_keys[14], part), 15)
    return {
        "pair_acts": gaussian(part_keys[0], (NRES, NRES, C), 1.0, 6.0, ((0, 16),)),
        "res_mask": with_ends((jax.random.randint(part_keys[1], (NRES,), 0, 8) < 7).astype(jnp.int32), jax.random.fold_in(part_keys[1], 1), 0, 1),
        "chain_id": jnp.searchsorted(jnp.cumsum(uneven(part_keys[2], CHAINS, NRES, NRES // 2, 0)), jnp.arange(NRES), side="right").astype(jnp.int32),
        "in_gain": jnp.clip(1.0 + 0.18 * jax.random.normal(arg_keys[3], (C,), jnp.float32), 0.1, 1.9),
        "w_left": gaussian(arg_keys[4], (C, 2 * CM), C ** -0.5, 0.5),
        "w_right": gaussian(arg_keys[5], (C, 2 * CM), C ** -0.5, 0.5),
        "w_mult_gate": gaussian(arg_keys[6], (C, C), C ** -0.5, 0.5),
        "mult_gain": jnp.clip(1.0 + 0.18 * jax.random.normal(arg_keys[7], (CM,), jnp.float32), 0.1, 1.9),
        "w_mult_out": gaussian(arg_keys[8], (CM, C), CM ** -0.5, 0.5),
        "att_gain": jnp.clip(1.0 + 0.18 * jax.random.normal(arg_keys[9], (C,), jnp.float32), 0.1, 1.9),
        "w_att": gaussian(arg_keys[10], (C, 4 * H * DH), C ** -0.5, 0.5),
        "w_pair_bias": gaussian(arg_keys[11], (C, H), C ** -0.5, 0.5),
        "cross_bias": jnp.clip(jax.random.uniform(arg_keys[12], (H,), jnp.float32, -2.0, 2.0), -2.0, 2.0),
        "w_att_out": gaussian(arg_keys[13], (H * DH, C), (H * DH) ** -0.5, 0.5),
    }


norm_eps = 1e-05

def layer_norm(tensor, norm_axis):
    tensor = tensor.astype(jnp.float32)
    average = lax.optimization_barrier(jnp.mean(tensor, axis=norm_axis, keepdims=True))
    spread = lax.optimization_barrier(jnp.mean(jnp.square(tensor - average), axis=norm_axis, keepdims=True))
    return (tensor - average) * lax.rsqrt(spread + norm_eps)

def project_f32(normed, weight, form):
    return jnp.einsum(form, normed.astype(jnp.float32), weight.astype(jnp.float32))

def edges_of(normed, weight, pair_mask, mult_width):
    gate_part = project_f32(normed, weight[:, :mult_width], 'ikc,cm->mik')
    value_part = project_f32(normed, weight[:, mult_width:], 'ikc,cm->mik')
    return (pair_mask[None] * jax.nn.sigmoid(gate_part) * value_part).astype(jnp.bfloat16)

def reference(pair_acts, res_mask, chain_id, in_gain, w_left, w_right, w_mult_gate, mult_gain, w_mult_out, att_gain, w_att, w_pair_bias, cross_bias, w_att_out):
    mult_width = w_left.shape[1] // 2
    residues = pair_acts.shape[0]
    mask_float = res_mask.astype(jnp.float32)
    pair_mask = mask_float[:, None] * mask_float[None, :]
    normed = (layer_norm(pair_acts, -1) * in_gain).astype(jnp.bfloat16)
    left_edges = edges_of(normed, w_left, pair_mask, mult_width)
    right_edges = edges_of(normed, w_right, pair_mask, mult_width)
    product = jnp.einsum('cik,cjk->cij', left_edges.astype(jnp.float32), right_edges.astype(jnp.float32)).astype(jnp.bfloat16)
    product_norm = (layer_norm(product, 0) * mult_gain[:, None, None]).astype(jnp.bfloat16)
    gate_mult = jax.nn.sigmoid(project_f32(normed, w_mult_gate, 'ijc,cd->ijd'))
    update = project_f32(product_norm, w_mult_out, 'mij,mc->ijc')
    pair_mid = (pair_acts.astype(jnp.float32) + gate_mult * update).astype(jnp.bfloat16)
    normed_mid = (layer_norm(pair_mid, -1) * att_gain).astype(jnp.bfloat16)
    inner_dim = w_att.shape[1] // 4
    head_count = cross_bias.shape[0]
    head_dim = inner_dim // head_count

    def heads_of(slot_idx):
        return project_f32(normed_mid, w_att[:, slot_idx * inner_dim:(slot_idx + 1) * inner_dim], 'ijc,ce->ije')
    query_all = (heads_of(0) * head_dim ** (-0.5)).astype(jnp.bfloat16).reshape(residues, residues, head_count, head_dim)
    key_all = heads_of(1).astype(jnp.bfloat16).reshape(residues, residues, head_count, head_dim)
    value_all = heads_of(2).astype(jnp.bfloat16).reshape(residues, residues, head_count, head_dim)
    gate_att = jax.nn.sigmoid(heads_of(3))
    pair_bias = project_f32(normed_mid, w_pair_bias, 'kic,ch->hki').astype(jnp.bfloat16)
    crossing = (chain_id[:, None] != chain_id[None, :]).astype(jnp.float32)
    extra = pair_bias.astype(jnp.float32) + cross_bias[:, None, None] * crossing[None]

    def column(col_index):
        query = query_all[:, col_index].astype(jnp.float32)
        key_col = key_all[:, col_index].astype(jnp.float32)
        value_col = value_all[:, col_index].astype(jnp.float32)
        scores = jnp.einsum('ihd,khd->hki', query, key_col) + extra
        key_live = mask_float * mask_float[col_index] > 0
        scores = jnp.where(key_live[None, :, None], scores, -1000000000.0)
        weights = jax.nn.softmax(scores, axis=1).astype(jnp.bfloat16)
        return jnp.einsum('hki,khd->ihd', weights.astype(jnp.float32), value_col)
    outputs = lax.map(column, jnp.arange(residues, dtype=jnp.int32))
    outputs = jnp.transpose(outputs, (1, 0, 2, 3)).reshape(residues, residues, inner_dim)
    gated = (outputs * gate_att).astype(jnp.bfloat16)
    pair_out = pair_mid.astype(jnp.float32) + project_f32(gated, w_att_out, 'ije,ec->ijc')
    return pair_out.astype(jnp.bfloat16)
```

```python
import functools

import jax
import jax.numpy as jnp
from jax import lax
from jax.experimental import pallas as pl
from jax.experimental.pallas import tpu as pltpu
from jax.sharding import PartitionSpec as P

norm_eps = 1e-05
vmem_share = 4 * 2**20


def layer_norm(tensor, norm_axis):
    tensor = tensor.astype(jnp.float32)
    average = jnp.mean(tensor, axis=norm_axis, keepdims=True)
    spread = jnp.mean(jnp.square(tensor - average), axis=norm_axis, keepdims=True)
    return (tensor - average) * lax.rsqrt(spread + norm_eps)


def edges_of(normed, weight, row_mask, mult_width):
    gate_part = jnp.einsum(
        "ikc,cm->mik", normed, weight[:, :mult_width], preferred_element_type=jnp.float32
    )
    value_part = jnp.einsum(
        "ikc,cm->mik", normed, weight[:, mult_width:], preferred_element_type=jnp.float32
    )
    return (row_mask[None] * jax.nn.sigmoid(gate_part) * value_part).astype(jnp.bfloat16)


def attend(normed_cols, bias_table, mask_float, chain_id, cross_bias, w_att, first_col):
    residues, col_count, _ = normed_cols.shape
    inner_dim = w_att.shape[1] // 4
    head_count = cross_bias.shape[0]
    head_dim = inner_dim // head_count

    def project(slot_idx):
        return jnp.einsum(
            "ijc,ce->ije",
            normed_cols,
            w_att[:, slot_idx * inner_dim : (slot_idx + 1) * inner_dim],
            preferred_element_type=jnp.float32,
        )

    query_all = (
        (project(0) * head_dim ** (-0.5))
        .astype(jnp.bfloat16)
        .reshape(residues, col_count, head_count, head_dim)
    )
    key_all = project(1).astype(jnp.bfloat16).reshape(residues, col_count, head_count, head_dim)
    value_all = project(2).astype(jnp.bfloat16).reshape(residues, col_count, head_count, head_dim)
    gate_att = jax.nn.sigmoid(project(3))
    crossing = (chain_id[:, None] != chain_id[None, :]).astype(jnp.float32)
    half_rows = residues // 2

    def column(col_index):
        query = lax.dynamic_index_in_dim(query_all, col_index, 1, keepdims=False)
        key_col = lax.dynamic_index_in_dim(key_all, col_index, 1, keepdims=False)
        value_col = lax.dynamic_index_in_dim(value_all, col_index, 1, keepdims=False)
        own_live = lax.dynamic_index_in_dim(mask_float, first_col + col_index, 0, keepdims=False)
        key_live = mask_float * own_live > 0
        pieces_out = []
        for block_idx in range(2):
            lower_row = block_idx * half_rows
            query_block = query[lower_row : lower_row + half_rows]
            scores = jnp.einsum(
                "ihd,khd->hki", query_block, key_col, preferred_element_type=jnp.float32
            )
            scores = scores + (
                bias_table[:, :, lower_row : lower_row + half_rows].astype(jnp.float32)
                + cross_bias[:, None, None] * crossing[None, :, lower_row : lower_row + half_rows]
            )
            scores = jnp.where(key_live[None, :, None], scores, -1000000000.0)
            weights = jax.nn.softmax(scores, axis=1).astype(jnp.bfloat16)
            pieces_out.append(
                jnp.einsum("hki,khd->ihd", weights, value_col, preferred_element_type=jnp.float32)
            )
        return jnp.concatenate(pieces_out, 0)

    outputs = lax.map(column, jnp.arange(col_count, dtype=jnp.int32))
    outputs = jnp.transpose(outputs, (1, 0, 2, 3)).reshape(residues, col_count, inner_dim)
    return (outputs * gate_att).astype(jnp.bfloat16)


def shards(
    pair_acts,
    res_mask,
    chain_id,
    in_gain,
    w_left,
    w_right,
    w_mult_gate,
    mult_gain,
    w_mult_out,
    att_gain,
    w_att,
    w_pair_bias,
    cross_bias,
    w_att_out,
):
    row_count = pair_acts.shape[0]
    mult_width = w_left.shape[1] // 2
    first_row = lax.axis_index("row") * row_count
    mask_float = res_mask.astype(jnp.float32)
    own_mask = lax.dynamic_slice_in_dim(mask_float, first_row, row_count)
    row_mask = own_mask[:, None] * mask_float[None, :]
    normed = (layer_norm(pair_acts, -1) * in_gain).astype(jnp.bfloat16)
    left_edges = edges_of(normed, w_left, row_mask, mult_width)
    right_edges = edges_of(normed, w_right, row_mask, mult_width)
    left_chan, right_chan = (
        lax.all_to_all(left_edges, "row", split_axis=0, concat_axis=1, tiled=True),
        lax.all_to_all(right_edges, "row", split_axis=0, concat_axis=1, tiled=True),
    )
    product = jnp.einsum(
        "cik,cjk->cij", left_chan, right_chan, preferred_element_type=jnp.float32
    ).astype(jnp.bfloat16)
    product_own = lax.all_to_all(product, "row", split_axis=1, concat_axis=0, tiled=True)
    product_norm = (layer_norm(product_own, 0) * mult_gain[:, None, None]).astype(jnp.bfloat16)
    gate_mult = jax.nn.sigmoid(
        jnp.einsum("ijc,cd->ijd", normed, w_mult_gate, preferred_element_type=jnp.float32)
    )
    update = jnp.einsum("mij,mc->ijc", product_norm, w_mult_out, preferred_element_type=jnp.float32)
    pair_mid = (pair_acts.astype(jnp.float32) + gate_mult * update).astype(jnp.bfloat16)
    normed_mid = (layer_norm(pair_mid, -1) * att_gain).astype(jnp.bfloat16)
    bias_piece = jnp.einsum(
        "kic,ch->hki", normed_mid, w_pair_bias, preferred_element_type=jnp.float32
    ).astype(jnp.bfloat16)
    bias_table = lax.all_gather(bias_piece, "row", axis=1, tiled=True)
    normed_cols = lax.all_to_all(normed_mid, "row", split_axis=1, concat_axis=0, tiled=True)
    gated = attend(normed_cols, bias_table, mask_float, chain_id, cross_bias, w_att, first_row)
    gated_rows = lax.all_to_all(gated, "row", split_axis=0, concat_axis=1, tiled=True)
    pair_out = pair_mid.astype(jnp.float32) + jnp.einsum(
        "ije,ec->ijc", gated_rows, w_att_out, preferred_element_type=jnp.float32
    )
    return pair_out.astype(jnp.bfloat16)


def dot(a, b):
    return jnp.dot(a, b, preferred_element_type=jnp.float32)


def dot_t(a, b):
    return lax.dot_general(a, b, (((1,), (1,)), ((), ())), preferred_element_type=jnp.float32)


def sigmoid(x):
    return 1.0 / (1.0 + jnp.exp(-x))


def norm_rows(x, gain):
    average = jnp.mean(x, axis=-1, keepdims=True)
    centred = x - average
    spread = jnp.mean(centred * centred, axis=-1, keepdims=True)
    return centred * lax.rsqrt(spread + norm_eps) * gain


def right_kernel(offsets, row_count, me_ref, live_ref, held_ref, come_ref, gain_ref, w_ref, acts_ref, normed_ref, right_ref):
    residues = come_ref.shape[1]
    width = w_ref.shape[1] // 2
    pieces = len(offsets) // 2
    for t, offset in enumerate(offsets):
        source, at = (held_ref, t) if t < pieces else (come_ref, t - pieces)
        place = jnp.bitwise_xor(me_ref[0], offset) // 2
        acts_ref[pl.ds(place * row_count, row_count)] = source[at * row_count : (at + 1) * row_count]

    own_count = acts_ref.shape[0]
    step_rows = row_count
    core = me_ref[0] % 2
    live_all = live_ref[...]
    for chip in range(own_count // row_count):
        lower = chip * row_count
        x = acts_ref[lower : lower + row_count].astype(jnp.float32)
        normed = norm_rows(x, gain_ref[...])
        rows = []
        for r in range(row_count):
            live = me_ref[1 + (2 * chip + core) * row_count + r].astype(jnp.float32)
            rows.append(normed[r] * (live_all * live))
        normed = jnp.concatenate(rows, 0).astype(jnp.bfloat16)
        normed_ref[lower * residues : (lower + row_count) * residues] = normed
        both = dot(normed, w_ref[...])
        edges = (sigmoid(both[:, :width]) * both[:, width:]).astype(jnp.bfloat16)
        right_ref[lower * residues : (lower + row_count) * residues] = edges


def left_kernel(step_rows, normed_ref, w_left_ref, w_gate_ref, left_ref, gate_ref):
    width = w_left_ref.shape[1] // 2
    for lower in range(0, normed_ref.shape[0], step_rows):
        normed = normed_ref[lower : lower + step_rows]
        both = dot(normed, w_left_ref[...])
        edges = sigmoid(both[:, :width]) * both[:, width:]
        left_ref[lower : lower + step_rows] = edges.astype(jnp.bfloat16).astype(jnp.float32)
        gate_ref[lower : lower + step_rows] = sigmoid(dot(normed, w_gate_ref[...]))


def product_kernel(
    row_count,
    me_ref,
    left_ref,
    right_ref,
    other_ref,
    gate_ref,
    acts_ref,
    mult_gain_ref,
    w_out_ref,
    att_gain_ref,
    mid_ref,
    normed_mid_ref,
    turned_ref,
    product_ref,
):
    own_count, residues, _ = acts_ref.shape
    core = me_ref[0] % 2
    for source, side in ((right_ref, core), (other_ref, 1 - core)):
        for local in range(own_count):
            spot = (2 * (local // row_count) + side) * row_count + local % row_count
            turned_ref[pl.ds(spot, residues, stride=residues), :] = source[
                local * residues : (local + 1) * residues
            ].astype(jnp.float32)

    row_block, tile = 4, 8
    tiles = residues // tile

    def rows_of(block, carry):
        first = block * row_block

        def add(k, totals):
            ahead = [
                turned_ref[pl.ds(pl.multiple_of(k * residues + t * tile, tile), tile), :]
                for t in range(tiles)
            ]
            out = []
            for a in range(row_block):
                one = left_ref[pl.ds((first + a) * residues + k, 1), :]
                out.extend(totals[a * tiles + t] + one * ahead[t] for t in range(tiles))
            return tuple(out)

        totals = lax.fori_loop(
            0,
            residues,
            add,
            tuple(jnp.zeros((tile, left_ref.shape[1]), jnp.float32) for _ in range(row_block * tiles)),
            unroll=8,
        )
        for a in range(row_block):
            for t in range(tiles):
                product_ref[pl.ds(pl.multiple_of((first + a) * residues + t * tile, tile), tile), :] = (
                    totals[a * tiles + t]
                )
        return carry

    lax.fori_loop(0, own_count // row_block, rows_of, 0)

    for local in range(0, own_count, row_count):
        at = slice(local * residues, (local + row_count) * residues)
        product = product_ref[at].astype(jnp.bfloat16).astype(jnp.float32)
        product = norm_rows(product, mult_gain_ref[...]).astype(jnp.bfloat16)
        update = gate_ref[at] * dot(product, w_out_ref[...])
        acts = acts_ref[local : local + row_count].astype(jnp.float32).reshape(update.shape)
        mid = (acts + update).astype(jnp.bfloat16)
        mid_ref[at] = mid
        normed_mid_ref[at] = norm_rows(mid.astype(jnp.float32), att_gain_ref[...]).astype(jnp.bfloat16)


def attend_kernel(
    row_count,
    me_ref,
    cross_ref,
    mid_ref,
    own_ref,
    other_ref,
    crossing_ref,
    keep_ref,
    w_att_ref,
    w_bias_ref,
    w_out_ref,
    out_ref,
    pair_ref,
    query_ref,
    context_ref,
):
    residues = pair_ref.shape[1]
    heads = w_bias_ref.shape[0]
    inner = w_out_ref.shape[0]
    head_dim = inner // heads
    channels = pair_ref.shape[2]
    core = me_ref[0] % 2
    chip = me_ref[0] // 2
    own_count = residues // 2
    for source, side in ((own_ref, core), (other_ref, 1 - core)):
        for local in range(own_count):
            spot = (2 * (local // row_count) + side) * row_count + local % row_count
            pair_ref[pl.ds(spot, 1)] = source[local * residues : (local + 1) * residues].astype(jnp.float32)[None]

    first = me_ref[0] * row_count
    mine = pair_ref[pl.ds(first, row_count)].reshape(row_count * residues, channels).astype(jnp.bfloat16)
    query = (dot(mine, w_att_ref[:, :inner]) * head_dim ** (-0.5)).astype(jnp.bfloat16)
    gate = sigmoid(dot(mine, w_att_ref[:, 3 * inner :]))
    head_of = lax.broadcasted_iota(jnp.int32, (1, inner), 1) // head_dim
    for h in range(heads):
        w_key = jnp.where(head_of == h, w_att_ref[:, inner : 2 * inner], 0)
        query_ref[h] = dot_t(query, w_key).reshape(row_count, residues, channels)

    tile = 8
    wide = residues * tile
    pieces = []
    for i in range(row_count):
        column = pair_ref[:, pl.ds(first + i, 1), :]
        spread = jnp.broadcast_to(column, (residues, tile, channels)).reshape(wide, channels)
        bias = dot_t(w_bias_ref[...], spread.astype(jnp.bfloat16)).astype(jnp.bfloat16).astype(jnp.float32)
        crossing = crossing_ref[i : i + 1, :]
        pieces.append([bias[h : h + 1] + cross_ref[h] * crossing for h in range(heads)])
    extra = jnp.concatenate(
        [jnp.broadcast_to(pieces[i][h], (tile, wide)) for h in range(heads) for i in range(row_count)], 0
    )
    total_rows = heads * row_count * tile
    same = (
        lax.broadcasted_iota(jnp.int32, (total_rows, wide), 0) % tile
        == lax.broadcasted_iota(jnp.int32, (total_rows, wide), 1) % tile
    )
    for g in range(residues // tile):
        keys = pair_ref[:, g * tile : (g + 1) * tile, :].reshape(wide, channels).astype(jnp.bfloat16)
        asked = query_ref[:, :, g * tile : (g + 1) * tile, :].reshape(total_rows, channels).astype(jnp.bfloat16)
        scores = dot_t(asked, keys) + extra
        scores = jnp.where(keep_ref[g : g + 1, :] > 0, scores, -1000000000.0)
        scores = jnp.where(same, scores, -1e30)
        scores = jnp.exp(scores - jnp.max(scores, axis=-1, keepdims=True))
        weights = (scores / jnp.sum(scores, axis=-1, keepdims=True)).astype(jnp.bfloat16)
        context_ref[:, :, g * tile : (g + 1) * tile, :] = dot(weights, keys).reshape(
            heads, row_count, tile, channels
        )

    values = jnp.zeros((row_count * residues, inner), jnp.float32)
    for h in range(heads):
        w_value = jnp.where(head_of == h, w_att_ref[:, 2 * inner : 3 * inner], 0)
        context = context_ref[h].reshape(row_count * residues, channels).astype(jnp.bfloat16)
        values = values + dot(context, w_value)
    gated = (values * gate).astype(jnp.bfloat16)
    mid = mid_ref[pl.ds(chip * row_count, row_count)].astype(jnp.float32)
    update = dot(gated, w_out_ref[...]).reshape(mid.shape)
    out_ref[...] = (mid + update).astype(jnp.bfloat16)


def call(body, args, scalars, outs, scratch, flops, name):
    return pl.pallas_call(
        body,
        out_shape=[jax.ShapeDtypeStruct(shape, dtype) for shape, dtype in outs],
        in_specs=[pl.BlockSpec(memory_space=pltpu.SMEM)] * len(scalars)
        + [pl.BlockSpec(memory_space=pltpu.VMEM)] * len(args),
        out_specs=[pl.BlockSpec(memory_space=pltpu.VMEM)] * len(outs),
        scratch_shapes=scratch,
        compiler_params=pltpu.CompilerParams(vmem_limit_bytes=24 * 2**20),
        cost_estimate=pl.CostEstimate(flops=flops, bytes_accessed=2**20, transcendentals=2**18),
        name=name,
    )(*scalars, *args)


def gathered(
    row_devices,
    pair_acts,
    res_mask,
    chain_id,
    in_gain,
    w_left,
    w_right,
    w_mult_gate,
    mult_gain,
    w_mult_out,
    att_gain,
    w_att,
    w_pair_bias,
    cross_bias,
    w_att_out,
):
    row_count, residues, channels = pair_acts.shape
    width = w_left.shape[1] // 2
    heads = w_pair_bias.shape[1]
    own_count = residues // 2
    pairs = own_count * residues
    me = lax.axis_index("row")
    tile = 8

    def swap(x, shift):
        return lax.ppermute(x, "row", [(i, i ^ shift) for i in range(row_devices)])

    held, offsets, shift = pair_acts, [0], row_devices // 2
    while shift > 2:
        held = jnp.concatenate([held, swap(held, shift)], 0)
        offsets = offsets + [o ^ shift for o in offsets]
        shift //= 2
    come = swap(held, 2)
    offsets = offsets + [o ^ 2 for o in offsets]

    place = jnp.concatenate([me[None].astype(jnp.int32), res_mask])
    mask_float = res_mask.astype(jnp.float32)
    live = jnp.broadcast_to(mask_float[:, None], (residues, channels))
    own_chain = lax.dynamic_slice_in_dim(chain_id, me * row_count, row_count)
    crossing = (own_chain[:, None] != jnp.repeat(chain_id, tile)[None, :]).astype(jnp.float32)
    keep = (mask_float.reshape(-1, 1, tile) * mask_float[None, :, None]).reshape(-1, residues * tile)

    bf16, f32 = jnp.bfloat16, jnp.float32
    acts, normed, right = call(
        functools.partial(right_kernel, offsets, row_count),
        [live, held, come, in_gain[None], w_right],
        [place],
        [((own_count, residues, channels), bf16), ((pairs, channels), bf16), ((pairs, width), bf16)],
        [],
        2 * pairs * channels * 2 * width,
        "right_edges",
    )
    other = swap(right, 1)
    left, gate = call(
        functools.partial(left_kernel, row_count * residues),
        [normed, w_left, w_mult_gate],
        [],
        [((pairs, width), f32), ((pairs, channels), f32)],
        [],
        2 * pairs * channels * 3 * width,
        "left_edges",
    )
    mid, normed_mid = call(
        functools.partial(product_kernel, row_count),
        [left, right, other, gate, acts, mult_gain[None], w_mult_out, att_gain[None]],
        [place],
        [((pairs, channels), bf16), ((pairs, channels), bf16)],
        [pltpu.VMEM((residues * residues, width), f32), pltpu.VMEM((pairs, width), f32)],
        2 * pairs * residues * width,
        "product",
    )
    normed_other = swap(normed_mid, 1)
    (out,) = call(
        functools.partial(attend_kernel, row_count),
        [
            mid.reshape(own_count, residues, channels),
            normed_mid,
            normed_other,
            crossing,
            keep,
            w_att,
            w_pair_bias.T,
            w_att_out,
        ],
        [place, cross_bias],
        [((row_count, residues, channels), bf16)],
        [
            pltpu.VMEM((residues, residues, channels), f32),
            pltpu.VMEM((heads, row_count, residues, channels), f32),
            pltpu.VMEM((heads, row_count, residues, channels), f32),
        ],
        2 * pairs * channels * 4 * channels,
        "attend",
    )
    return out


def solution(mesh):
    placed = (
        P(("groups", "row"), None, None),
        P("groups"),
        P("groups"),
        P(),
        P(),
        P(),
        P(),
        P(),
        P(),
        P(),
        P(),
        P(),
        P(),
        P(),
    )
    row_devices = mesh.shape["row"]

    def whole(pair_acts, *others):
        row_count, residues, channels = pair_acts.shape
        in_vmem = 4 * residues * residues * channels <= vmem_share
        paired = row_devices >= 4 and row_devices & (row_devices - 1) == 0 and residues % 8 == 0
        if in_vmem and paired:
            return gathered(row_devices, pair_acts, *others)
        return shards(pair_acts, *others)

    return jax.shard_map(
        whole,
        mesh=mesh,
        in_specs=placed,
        out_specs=P(("groups", "row"), None, None),
        check_vma=False,
    )
```

```python
import functools

import jax
import jax.numpy as jnp
from jax import lax
from jax.experimental import pallas as pl
from jax.experimental.pallas import tpu as pltpu
from jax.sharding import PartitionSpec as P

norm_eps = 1e-05
vmem_share = 4 * 2**20


def layer_norm(tensor, norm_axis):
    tensor = tensor.astype(jnp.float32)
    average = jnp.mean(tensor, axis=norm_axis, keepdims=True)
    spread = jnp.mean(jnp.square(tensor - average), axis=norm_axis, keepdims=True)
    return (tensor - average) * lax.rsqrt(spread + norm_eps)


def edges_of(normed, weight, row_mask, mult_width):
    gate_part = jnp.einsum(
        "ikc,cm->mik", normed, weight[:, :mult_width], preferred_element_type=jnp.float32
    )
    value_part = jnp.einsum(
        "ikc,cm->mik", normed, weight[:, mult_width:], preferred_element_type=jnp.float32
    )
    return (row_mask[None] * jax.nn.sigmoid(gate_part) * value_part).astype(jnp.bfloat16)


def attend(normed_cols, bias_table, mask_float, chain_id, cross_bias, w_att, first_col):
    residues, col_count, _ = normed_cols.shape
    inner_dim = w_att.shape[1] // 4
    head_count = cross_bias.shape[0]
    head_dim = inner_dim // head_count

    def project(slot_idx):
        return jnp.einsum(
            "ijc,ce->ije",
            normed_cols,
            w_att[:, slot_idx * inner_dim : (slot_idx + 1) * inner_dim],
            preferred_element_type=jnp.float32,
        )

    query_all = (
        (project(0) * head_dim ** (-0.5))
        .astype(jnp.bfloat16)
        .reshape(residues, col_count, head_count, head_dim)
    )
    key_all = project(1).astype(jnp.bfloat16).reshape(residues, col_count, head_count, head_dim)
    value_all = project(2).astype(jnp.bfloat16).reshape(residues, col_count, head_count, head_dim)
    gate_att = jax.nn.sigmoid(project(3))
    crossing = (chain_id[:, None] != chain_id[None, :]).astype(jnp.float32)
    half_rows = residues // 2

    def column(col_index):
        query = lax.dynamic_index_in_dim(query_all, col_index, 1, keepdims=False)
        key_col = lax.dynamic_index_in_dim(key_all, col_index, 1, keepdims=False)
        value_col = lax.dynamic_index_in_dim(value_all, col_index, 1, keepdims=False)
        own_live = lax.dynamic_index_in_dim(mask_float, first_col + col_index, 0, keepdims=False)
        key_live = mask_float * own_live > 0
        pieces_out = []
        for block_idx in range(2):
            lower_row = block_idx * half_rows
            query_block = query[lower_row : lower_row + half_rows]
            scores = jnp.einsum(
                "ihd,khd->hki", query_block, key_col, preferred_element_type=jnp.float32
            )
            scores = scores + (
                bias_table[:, :, lower_row : lower_row + half_rows].astype(jnp.float32)
                + cross_bias[:, None, None] * crossing[None, :, lower_row : lower_row + half_rows]
            )
            scores = jnp.where(key_live[None, :, None], scores, -1000000000.0)
            weights = jax.nn.softmax(scores, axis=1).astype(jnp.bfloat16)
            pieces_out.append(
                jnp.einsum("hki,khd->ihd", weights, value_col, preferred_element_type=jnp.float32)
            )
        return jnp.concatenate(pieces_out, 0)

    outputs = lax.map(column, jnp.arange(col_count, dtype=jnp.int32))
    outputs = jnp.transpose(outputs, (1, 0, 2, 3)).reshape(residues, col_count, inner_dim)
    return (outputs * gate_att).astype(jnp.bfloat16)


def shards(
    pair_acts,
    res_mask,
    chain_id,
    in_gain,
    w_left,
    w_right,
    w_mult_gate,
    mult_gain,
    w_mult_out,
    att_gain,
    w_att,
    w_pair_bias,
    cross_bias,
    w_att_out,
):
    row_count = pair_acts.shape[0]
    mult_width = w_left.shape[1] // 2
    first_row = lax.axis_index("row") * row_count
    mask_float = res_mask.astype(jnp.float32)
    own_mask = lax.dynamic_slice_in_dim(mask_float, first_row, row_count)
    row_mask = own_mask[:, None] * mask_float[None, :]
    normed = (layer_norm(pair_acts, -1) * in_gain).astype(jnp.bfloat16)
    left_edges = edges_of(normed, w_left, row_mask, mult_width)
    right_edges = edges_of(normed, w_right, row_mask, mult_width)
    left_chan, right_chan = (
        lax.all_to_all(left_edges, "row", split_axis=0, concat_axis=1, tiled=True),
        lax.all_to_all(right_edges, "row", split_axis=0, concat_axis=1, tiled=True),
    )
    product = jnp.einsum(
        "cik,cjk->cij", left_chan, right_chan, preferred_element_type=jnp.float32
    ).astype(jnp.bfloat16)
    product_own = lax.all_to_all(product, "row", split_axis=1, concat_axis=0, tiled=True)
    product_norm = (layer_norm(product_own, 0) * mult_gain[:, None, None]).astype(jnp.bfloat16)
    gate_mult = jax.nn.sigmoid(
        jnp.einsum("ijc,cd->ijd", normed, w_mult_gate, preferred_element_type=jnp.float32)
    )
    update = jnp.einsum("mij,mc->ijc", product_norm, w_mult_out, preferred_element_type=jnp.float32)
    pair_mid = (pair_acts.astype(jnp.float32) + gate_mult * update).astype(jnp.bfloat16)
    normed_mid = (layer_norm(pair_mid, -1) * att_gain).astype(jnp.bfloat16)
    bias_piece = jnp.einsum(
        "kic,ch->hki", normed_mid, w_pair_bias, preferred_element_type=jnp.float32
    ).astype(jnp.bfloat16)
    bias_table = lax.all_gather(bias_piece, "row", axis=1, tiled=True)
    normed_cols = lax.all_to_all(normed_mid, "row", split_axis=1, concat_axis=0, tiled=True)
    gated = attend(normed_cols, bias_table, mask_float, chain_id, cross_bias, w_att, first_row)
    gated_rows = lax.all_to_all(gated, "row", split_axis=0, concat_axis=1, tiled=True)
    pair_out = pair_mid.astype(jnp.float32) + jnp.einsum(
        "ije,ec->ijc", gated_rows, w_att_out, preferred_element_type=jnp.float32
    )
    return pair_out.astype(jnp.bfloat16)


def dot(a, b):
    return jnp.dot(a, b, preferred_element_type=jnp.float32)


def dot_t(a, b):
    return lax.dot_general(a, b, (((1,), (1,)), ((), ())), preferred_element_type=jnp.float32)


def sigmoid(x):
    return 0.5 * jnp.tanh(0.5 * x) + 0.5


def norm_rows(x, gain):
    average = jnp.mean(x, axis=-1, keepdims=True)
    centred = x - average
    spread = jnp.mean(centred * centred, axis=-1, keepdims=True)
    return centred * lax.rsqrt(spread + norm_eps) * gain


def gated_edges(normed, weight):
    both = dot(normed, weight)
    width = both.shape[1] // 2
    return (sigmoid(both[:, :width]) * both[:, width:]).astype(jnp.bfloat16)


def stage_kernel(copied, *refs):
    sources, refs = refs[: copied + 4], refs[copied + 4 :]
    (live_ref, crossing_ref, keep_ref), copies = refs[:3], refs[3 : copied + 3]
    *early, done = refs[copied + 3 :]
    cross_ref, chain_ref, mask_row_ref, chain_row_ref = early
    moves = [
        pltpu.make_async_copy(source, target, done.at[at])
        for at, (source, target) in enumerate(zip(sources, (*early, *copies), strict=True))
    ]
    for move in moves:
        move.start()
    for move in moves[: len(early)]:
        move.wait()
    residues = live_ref.shape[0]
    blocks, wide = keep_ref.shape
    tile = wide // residues
    heads = cross_ref.shape[0]
    row_count = crossing_ref.shape[0] // heads
    mask_row = mask_row_ref[...].astype(jnp.float32)
    chain_row = chain_row_ref[...].astype(jnp.float32)

    line = lax.broadcasted_iota(jnp.int32, (residues, residues), 0)
    spot = lax.broadcasted_iota(jnp.int32, (residues, residues), 1)
    diagonal = jnp.where(line == spot, mask_row, 0.0)
    live_ref[...] = dot(diagonal, jnp.ones((residues, live_ref.shape[1]), jnp.float32))

    line = lax.broadcasted_iota(jnp.int32, (residues, wide), 0)
    lane = lax.broadcasted_iota(jnp.int32, (residues, wide), 1)
    by_key = (lane // tile == line).astype(jnp.float32)
    by_column = (lane % tile == line % tile).astype(jnp.float32)
    block = lax.broadcasted_iota(jnp.int32, (blocks, residues), 0)
    spot = lax.broadcasted_iota(jnp.int32, (blocks, residues), 1)
    column_mask = jnp.where(spot // tile == block, mask_row, 0.0)
    keep_ref[...] = dot(column_mask, by_column) * dot(mask_row, by_key)

    chain_wide = dot(chain_row, by_key)
    first = lax.axis_index("row") * row_count
    for i in range(row_count):
        crossing = (chain_wide != chain_ref[first + i].astype(jnp.float32)).astype(jnp.float32)
        for h in range(heads):
            crossing_ref[h * row_count + i : h * row_count + i + 1, :] = cross_ref[h] * crossing
    for move in moves[len(early) :]:
        move.wait()


def spot_of(block_rows, place):
    return pl.ds(pl.multiple_of(place * block_rows, block_rows), block_rows)


def take_blocks(pieces, offsets, row_count, residues, live_ref, gain_ref):
    me = lax.axis_index("row")
    block_rows = row_count * residues
    blocks = [(ref, at) for ref in pieces for at in range(ref.shape[0] // row_count)]
    for (ref, at), offset in zip(blocks, offsets, strict=True):
        device = jnp.bitwise_xor(me, offset)
        acts = ref[at * row_count : (at + 1) * row_count]
        normed = norm_rows(acts.astype(jnp.float32), gain_ref[0:1])
        live_all = live_ref[...]
        rows = [normed[r] * (live_all * live_ref[pl.ds(device * row_count + r, 1), :]) for r in range(row_count)]
        normed = jnp.concatenate(rows, 0).astype(jnp.bfloat16)
        yield spot_of(block_rows, device // 2), acts.reshape(block_rows, acts.shape[-1]), normed


def early_kernel(offsets, row_count, live_ref, gain_ref, w_right_ref, w_left_ref, w_gate_ref, *refs):
    pieces, (acts_ref, right_ref, left_ref, gate_ref) = refs[:-4], refs[-4:]
    residues = live_ref.shape[0]
    for spot, acts, normed in take_blocks(pieces, offsets, row_count, residues, live_ref, gain_ref):
        acts_ref[spot] = acts
        right_ref[spot] = gated_edges(normed, w_right_ref[...])
        left_ref[spot] = gated_edges(normed, w_left_ref[...]).astype(jnp.float32)
        gate_ref[spot] = sigmoid(dot(normed, w_gate_ref[...]))


def right_kernel(offsets, row_count, live_ref, gain_ref, w_right_ref, *refs):
    pieces, (_, _, acts_ref, right_ref, normed_ref) = refs[:-5], refs[-5:]
    residues = live_ref.shape[0]
    block_rows = row_count * residues
    blocks = take_blocks(pieces, offsets, row_count, residues, live_ref, gain_ref)
    for t, (spot, acts, normed) in enumerate(blocks):
        acts_ref[spot] = acts
        right_ref[spot] = gated_edges(normed, w_right_ref[...])
        normed_ref[t * block_rows : (t + 1) * block_rows] = normed


def turn(source, turned_ref, row_count, residues):
    chips = source.shape[0] // (row_count * residues)
    own_count = chips * row_count
    for chip in range(chips):
        for r in range(row_count):
            lower = (chip * row_count + r) * residues
            turned_ref[pl.ds(r * chips + chip, residues, stride=own_count), :] = source[
                lower : lower + residues
            ].astype(jnp.float32)


def multiply(left_ref, turned_ref, residues, store):
    row_block, tile = 8, 8
    count = turned_ref.shape[0] // residues
    own_count = left_ref.shape[0] // residues
    tiles = count // tile

    def rows_of(block, carry):
        first = block * row_block

        def add(k, totals):
            ahead = [
                turned_ref[pl.ds(pl.multiple_of(k * count + t * tile, tile), tile), :] for t in range(tiles)
            ]
            out = []
            for a in range(row_block):
                one = left_ref[pl.ds((first + a) * residues + k, 1), :]
                out.extend(totals[a * tiles + t] + one * ahead[t] for t in range(tiles))
            return tuple(out)

        zeros = tuple(jnp.zeros((tile, left_ref.shape[1]), jnp.float32) for _ in range(row_block * tiles))
        totals = lax.fori_loop(0, residues, add, zeros, unroll=8)
        for a in range(row_block):
            for t in range(tiles):
                store(first + a, t, totals[a * tiles + t])
        return carry

    lax.fori_loop(0, own_count // row_block, rows_of, 0)


def left_kernel(
    offsets, row_count, residues, normed_ref, right_ref, w_left_ref, w_gate_ref, _, __, left_ref, gate_ref, near_ref, turned_ref
):
    me = lax.axis_index("row")
    block_rows = row_count * residues
    for t, offset in enumerate(offsets):
        spot = spot_of(block_rows, jnp.bitwise_xor(me, offset) // 2)
        normed = normed_ref[t * block_rows : (t + 1) * block_rows]
        left_ref[spot] = gated_edges(normed, w_left_ref[...]).astype(jnp.float32)
        gate_ref[spot] = sigmoid(dot(normed, w_gate_ref[...]))
    turn(right_ref, turned_ref, row_count, residues)
    count = turned_ref.shape[0] // residues

    def store(i, t, values):
        near_ref[pl.ds(pl.multiple_of(i * count + t * 8, 8), 8), :] = values

    multiply(left_ref, turned_ref, residues, store)


def product_kernel(
    row_count,
    residues,
    left_ref,
    other_ref,
    near_ref,
    gate_ref,
    acts_ref,
    gain_ref,
    w_out_ref,
    mid_ref,
    normed_mid_ref,
    turned_ref,
    product_ref,
):
    core = lax.axis_index("row") % 2
    turn(other_ref, turned_ref, row_count, residues)
    count = turned_ref.shape[0] // residues
    chips = count // row_count
    part = chips // 8

    def place(i, t, side):
        r, eighth = t // part, t % part
        start = i * residues + (eighth * 16 + side) * row_count + r
        return pl.ds(start, 8, stride=2 * row_count)

    def store(i, t, values):
        product_ref[place(i, t, 1 - core), :] = values
        product_ref[place(i, t, core), :] = near_ref[pl.ds(pl.multiple_of(i * count + t * 8, 8), 8), :]

    multiply(left_ref, turned_ref, residues, store)

    block_rows = row_count * residues
    for lower in range(0, acts_ref.shape[0], block_rows):
        at = slice(lower, lower + block_rows)
        product = product_ref[at].astype(jnp.bfloat16).astype(jnp.float32)
        product = norm_rows(product, gain_ref[1:2]).astype(jnp.bfloat16)
        update = gate_ref[at] * dot(product, w_out_ref[...])
        mid = (acts_ref[at].astype(jnp.float32) + update).astype(jnp.bfloat16)
        mid_ref[at] = mid
        normed_mid_ref[at] = norm_rows(mid.astype(jnp.float32), gain_ref[2:3]).astype(jnp.bfloat16)


def query_kernel(row_count, residues, heads, own_ref, w_att_ref, asked_ref, gate_ref):
    block_rows = row_count * residues
    inner = w_att_ref.shape[1] // 4
    head_dim = inner // heads
    tile = 8
    mine = own_ref[spot_of(block_rows, lax.axis_index("row") // 2)]
    query = (dot(mine, w_att_ref[:, :inner]) * head_dim ** (-0.5)).astype(jnp.bfloat16)
    gate_ref[...] = sigmoid(dot(mine, w_att_ref[:, 3 * inner :]))
    head_of = lax.broadcasted_iota(jnp.int32, (1, inner), 1) // head_dim
    asked = [
        dot_t(query, jnp.where(head_of == h, w_att_ref[:, inner : 2 * inner], 0)) for h in range(heads)
    ]
    for g in range(residues // tile):
        rows = [
            asked[h][i * residues + g * tile : i * residues + (g + 1) * tile]
            for h in range(heads)
            for i in range(row_count)
        ]
        asked_ref[g] = jnp.concatenate(rows, 0).astype(jnp.bfloat16)


def attend_kernel(
    row_count,
    own_ref,
    other_ref,
    mid_ref,
    asked_ref,
    gate_ref,
    crossing_ref,
    keep_ref,
    w_att_ref,
    w_bias_ref,
    w_out_ref,
    out_ref,
    pair_ref,
):
    residues, _, channels = pair_ref.shape
    heads = w_bias_ref.shape[0]
    inner = w_out_ref.shape[0]
    head_dim = inner // heads
    me = lax.axis_index("row")
    core = me % 2
    block_rows = row_count * residues
    for source, side in ((own_ref, core), (other_ref, 1 - core)):
        for local in range(residues // 2):
            spot = (2 * (local // row_count) + side) * row_count + local % row_count
            pair_ref[pl.ds(spot, 1)] = source[local * residues : (local + 1) * residues].astype(jnp.float32)[None]

    tile = 8
    wide = residues * tile
    first = me * row_count
    pieces = []
    for i in range(row_count):
        column = pair_ref[:, pl.ds(first + i, 1), :]
        spread = jnp.broadcast_to(column, (residues, tile, channels)).reshape(wide, channels)
        pieces.append(dot_t(w_bias_ref[...], spread.astype(jnp.bfloat16)).astype(jnp.bfloat16).astype(jnp.float32))
    extra = jnp.concatenate(
        [
            jnp.broadcast_to(pieces[i][h : h + 1] + crossing_ref[h * row_count + i : h * row_count + i + 1], (tile, wide))
            for h in range(heads)
            for i in range(row_count)
        ],
        0,
    )
    total_rows = heads * row_count * tile
    same = (
        lax.broadcasted_iota(jnp.int32, (total_rows, wide), 0) % tile
        == lax.broadcasted_iota(jnp.int32, (total_rows, wide), 1) % tile
    )
    low = jnp.where(same, -1000000000.0, -1e30)
    groups = range(residues // tile)
    keys = [
        pair_ref[:, g * tile : (g + 1) * tile, :].reshape(wide, channels).astype(jnp.bfloat16) for g in groups
    ]
    scores = [dot_t(asked_ref[g], keys[g]) for g in groups]
    scores = [
        jnp.where(jnp.logical_and(same, keep_ref[g : g + 1, :] > 0), scores[g] + extra, low) for g in groups
    ]
    scores = [jnp.exp(s - jnp.max(s, axis=-1, keepdims=True)) for s in scores]
    weights = [(s * (1.0 / jnp.sum(s, axis=-1, keepdims=True))).astype(jnp.bfloat16) for s in scores]
    context = [dot(weights[g], keys[g]) for g in groups]

    head_of = lax.broadcasted_iota(jnp.int32, (1, inner), 1) // head_dim
    values = jnp.zeros((block_rows, inner), jnp.float32)
    for h in range(heads):
        w_value = jnp.where(head_of == h, w_att_ref[:, 2 * inner : 3 * inner], 0)
        rows = [
            context[g][(h * row_count + i) * tile : (h * row_count + i + 1) * tile]
            for i in range(row_count)
            for g in groups
        ]
        values = values + dot(jnp.concatenate(rows, 0).astype(jnp.bfloat16), w_value)
    gated = (values * gate_ref[...]).astype(jnp.bfloat16)
    mid = mid_ref[spot_of(block_rows, me // 2)].astype(jnp.float32)
    out_ref[...] = (mid + dot(gated, w_out_ref[...])).astype(jnp.bfloat16).reshape(out_ref.shape)


def call(body, args, outs, cost_us, name, scratch=(), aliases=None, space=pltpu.VMEM):
    return pl.pallas_call(
        body,
        out_shape=[jax.ShapeDtypeStruct(shape, dtype) for shape, dtype in outs],
        in_specs=[pl.BlockSpec(memory_space=space)] * len(args),
        out_specs=[pl.BlockSpec(memory_space=pltpu.VMEM)] * len(outs),
        scratch_shapes=list(scratch),
        input_output_aliases=aliases or {},
        compiler_params=pltpu.CompilerParams(vmem_limit_bytes=24 * 2**20),
        cost_estimate=pl.CostEstimate(flops=int(cost_us * 1e9), bytes_accessed=2**18, transcendentals=0),
        name=name,
    )(*args)


def gathered(
    row_devices,
    pair_acts,
    res_mask,
    chain_id,
    in_gain,
    w_left,
    w_right,
    w_mult_gate,
    mult_gain,
    w_mult_out,
    att_gain,
    w_att,
    w_pair_bias,
    cross_bias,
    w_att_out,
):
    row_count, residues, channels = pair_acts.shape
    width = w_left.shape[1] // 2
    heads = w_pair_bias.shape[1]
    own_count = residues // 2
    pairs = own_count * residues
    block_rows = row_count * residues
    tile = 8
    wide = residues * tile
    bf16, f32 = jnp.bfloat16, jnp.float32

    def swap(x, shift):
        return lax.ppermute(x, "row", [(i, i ^ shift) for i in range(row_devices)])

    base, held = [0], pair_acts
    far, near, side = 8, 4, 2

    def spread(shifts):
        return [o ^ s for s in shifts for o in base]

    shift = row_devices // 2
    while shift > far:
        held = jnp.concatenate([held, swap(held, shift)], 0)
        base = base + [o ^ shift for o in base]
        shift //= 2
    from_far = swap(held, far)
    from_side = swap(held, side)

    weights = [
        in_gain[None],
        mult_gain[None],
        att_gain[None],
        w_right,
        w_left,
        w_mult_gate,
        w_mult_out,
        w_att,
        w_pair_bias.T,
        w_att_out,
        held,
    ]
    live, crossing, keep, in_g, mult_g, att_g, w_r, w_l, w_g, w_m, w_a, w_b, w_o, held = call(
        functools.partial(stage_kernel, len(weights)),
        [
            pltpu.with_memory_space_constraint(x, pltpu.HBM)
            for x in (cross_bias, chain_id, res_mask[None], chain_id[None], *weights)
        ],
        [((residues, channels), f32), ((heads * row_count, wide), f32), ((residues // tile, wide), f32)]
        + [(w.shape, w.dtype) for w in weights],
        2.0,
        "stage",
        [
            pltpu.SMEM((heads,), f32),
            pltpu.SMEM((residues,), jnp.int32),
            pltpu.VMEM((1, residues), jnp.int32),
            pltpu.VMEM((1, residues), jnp.int32),
            pltpu.SemaphoreType.DMA((len(weights) + 4,)),
        ],
        space=pltpu.HBM,
    )
    pair = jnp.concatenate([held, from_far], 0)
    from_near = swap(pair, near)
    from_far_side = swap(from_far, side)
    from_corner = swap(pair, near ^ side)

    sizes = [((pairs, channels), bf16), ((pairs, width), bf16), ((pairs, width), f32), ((pairs, channels), f32)]
    acts, right, left, gate = call(
        functools.partial(early_kernel, spread([0, far, side]), row_count),
        [live, in_g, w_r, w_l, w_g, pair, from_side],
        sizes,
        0.6,
        "early_edges",
    )
    late = spread([near, near ^ far, far ^ side, near ^ side, near ^ far ^ side])
    acts, right, normed = call(
        functools.partial(right_kernel, late, row_count),
        [live, in_g, w_r, from_near, from_far_side, from_corner, acts, right],
        [*sizes[:2], ((len(late) * block_rows, channels), bf16)],
        0.5,
        "right_edges",
        aliases={6: 0, 7: 1},
    )
    other = swap(right, 1)
    left, gate, near_product = call(
        functools.partial(left_kernel, late, row_count, residues),
        [normed, right, w_l, w_g, left, gate],
        [*sizes[2:], ((own_count * own_count, width), f32)],
        1.5,
        "left_edges",
        scratch=[pltpu.VMEM((pairs, width), f32)],
        aliases={4: 0, 5: 1},
    )
    mid, normed_mid = call(
        functools.partial(product_kernel, row_count, residues),
        [left, other, near_product, gate, acts, jnp.concatenate([in_g, mult_g, att_g], 0), w_m],
        [((pairs, channels), bf16), ((pairs, channels), bf16)],
        2.4,
        "product",
        scratch=[pltpu.VMEM((pairs, width), f32), pltpu.VMEM((pairs, width), f32)],
    )
    normed_other = swap(normed_mid, 1)
    asked, gate_att = call(
        functools.partial(query_kernel, row_count, residues, heads),
        [normed_mid, w_a],
        [((residues // tile, heads * row_count * tile, channels), bf16), ((block_rows, w_o.shape[0]), f32)],
        0.4,
        "queries",
    )
    (out,) = call(
        functools.partial(attend_kernel, row_count),
        [normed_mid, normed_other, mid, asked, gate_att, crossing, keep, w_a, w_b, w_o],
        [((row_count, residues, channels), bf16)],
        2.0,
        "attend",
        scratch=[pltpu.VMEM((residues, residues, channels), f32)],
    )
    return out


def solution(mesh):
    placed = (
        P(("groups", "row"), None, None),
        P("groups"),
        P("groups"),
        P(),
        P(),
        P(),
        P(),
        P(),
        P(),
        P(),
        P(),
        P(),
        P(),
        P(),
    )
    row_devices = mesh.shape["row"]

    def whole(pair_acts, *others):
        row_count, residues, channels = pair_acts.shape
        in_vmem = 4 * residues * residues * channels <= vmem_share
        paired = row_devices % 16 == 0 and row_devices & (row_devices - 1) == 0 and residues % 8 == 0
        if in_vmem and paired:
            return gathered(row_devices, pair_acts, *others)
        return shards(pair_acts, *others)

    return jax.shard_map(
        whole,
        mesh=mesh,
        in_specs=placed,
        out_specs=P(("groups", "row"), None, None),
        check_vma=False,
    )
```

```python
import functools

import jax
import jax.numpy as jnp
from jax import lax
from jax.experimental import pallas as pl
from jax.experimental.pallas import tpu as pltpu
from jax.sharding import PartitionSpec as P

norm_eps = 1e-05
vmem_share = 4 * 2**20


def layer_norm(tensor, norm_axis):
    tensor = tensor.astype(jnp.float32)
    average = jnp.mean(tensor, axis=norm_axis, keepdims=True)
    spread = jnp.mean(jnp.square(tensor - average), axis=norm_axis, keepdims=True)
    return (tensor - average) * lax.rsqrt(spread + norm_eps)


def edges_of(normed, weight, row_mask, mult_width):
    gate_part = jnp.einsum(
        "ikc,cm->mik", normed, weight[:, :mult_width], preferred_element_type=jnp.float32
    )
    value_part = jnp.einsum(
        "ikc,cm->mik", normed, weight[:, mult_width:], preferred_element_type=jnp.float32
    )
    return (row_mask[None] * jax.nn.sigmoid(gate_part) * value_part).astype(jnp.bfloat16)


def attend(normed_cols, bias_table, mask_float, chain_id, cross_bias, w_att, first_col):
    residues, col_count, _ = normed_cols.shape
    inner_dim = w_att.shape[1] // 4
    head_count = cross_bias.shape[0]
    head_dim = inner_dim // head_count

    def project(slot_idx):
        return jnp.einsum(
            "ijc,ce->ije",
            normed_cols,
            w_att[:, slot_idx * inner_dim : (slot_idx + 1) * inner_dim],
            preferred_element_type=jnp.float32,
        )

    query_all = (
        (project(0) * head_dim ** (-0.5))
        .astype(jnp.bfloat16)
        .reshape(residues, col_count, head_count, head_dim)
    )
    key_all = project(1).astype(jnp.bfloat16).reshape(residues, col_count, head_count, head_dim)
    value_all = project(2).astype(jnp.bfloat16).reshape(residues, col_count, head_count, head_dim)
    gate_att = jax.nn.sigmoid(project(3))
    crossing = (chain_id[:, None] != chain_id[None, :]).astype(jnp.float32)
    half_rows = residues // 2

    def column(col_index):
        query = lax.dynamic_index_in_dim(query_all, col_index, 1, keepdims=False)
        key_col = lax.dynamic_index_in_dim(key_all, col_index, 1, keepdims=False)
        value_col = lax.dynamic_index_in_dim(value_all, col_index, 1, keepdims=False)
        own_live = lax.dynamic_index_in_dim(mask_float, first_col + col_index, 0, keepdims=False)
        key_live = mask_float * own_live > 0
        pieces_out = []
        for block_idx in range(2):
            lower_row = block_idx * half_rows
            query_block = query[lower_row : lower_row + half_rows]
            scores = jnp.einsum(
                "ihd,khd->hki", query_block, key_col, preferred_element_type=jnp.float32
            )
            scores = scores + (
                bias_table[:, :, lower_row : lower_row + half_rows].astype(jnp.float32)
                + cross_bias[:, None, None] * crossing[None, :, lower_row : lower_row + half_rows]
            )
            scores = jnp.where(key_live[None, :, None], scores, -1000000000.0)
            weights = jax.nn.softmax(scores, axis=1).astype(jnp.bfloat16)
            pieces_out.append(
                jnp.einsum("hki,khd->ihd", weights, value_col, preferred_element_type=jnp.float32)
            )
        return jnp.concatenate(pieces_out, 0)

    outputs = lax.map(column, jnp.arange(col_count, dtype=jnp.int32))
    outputs = jnp.transpose(outputs, (1, 0, 2, 3)).reshape(residues, col_count, inner_dim)
    return (outputs * gate_att).astype(jnp.bfloat16)


def shards(
    pair_acts,
    res_mask,
    chain_id,
    in_gain,
    w_left,
    w_right,
    w_mult_gate,
    mult_gain,
    w_mult_out,
    att_gain,
    w_att,
    w_pair_bias,
    cross_bias,
    w_att_out,
):
    row_count = pair_acts.shape[0]
    mult_width = w_left.shape[1] // 2
    first_row = lax.axis_index("row") * row_count
    mask_float = res_mask.astype(jnp.float32)
    own_mask = lax.dynamic_slice_in_dim(mask_float, first_row, row_count)
    row_mask = own_mask[:, None] * mask_float[None, :]
    normed = (layer_norm(pair_acts, -1) * in_gain).astype(jnp.bfloat16)
    left_edges = edges_of(normed, w_left, row_mask, mult_width)
    right_edges = edges_of(normed, w_right, row_mask, mult_width)
    left_chan, right_chan = (
        lax.all_to_all(left_edges, "row", split_axis=0, concat_axis=1, tiled=True),
        lax.all_to_all(right_edges, "row", split_axis=0, concat_axis=1, tiled=True),
    )
    product = jnp.einsum(
        "cik,cjk->cij", left_chan, right_chan, preferred_element_type=jnp.float32
    ).astype(jnp.bfloat16)
    product_own = lax.all_to_all(product, "row", split_axis=1, concat_axis=0, tiled=True)
    product_norm = (layer_norm(product_own, 0) * mult_gain[:, None, None]).astype(jnp.bfloat16)
    gate_mult = jax.nn.sigmoid(
        jnp.einsum("ijc,cd->ijd", normed, w_mult_gate, preferred_element_type=jnp.float32)
    )
    update = jnp.einsum("mij,mc->ijc", product_norm, w_mult_out, preferred_element_type=jnp.float32)
    pair_mid = (pair_acts.astype(jnp.float32) + gate_mult * update).astype(jnp.bfloat16)
    normed_mid = (layer_norm(pair_mid, -1) * att_gain).astype(jnp.bfloat16)
    bias_piece = jnp.einsum(
        "kic,ch->hki", normed_mid, w_pair_bias, preferred_element_type=jnp.float32
    ).astype(jnp.bfloat16)
    bias_table = lax.all_gather(bias_piece, "row", axis=1, tiled=True)
    normed_cols = lax.all_to_all(normed_mid, "row", split_axis=1, concat_axis=0, tiled=True)
    gated = attend(normed_cols, bias_table, mask_float, chain_id, cross_bias, w_att, first_row)
    gated_rows = lax.all_to_all(gated, "row", split_axis=0, concat_axis=1, tiled=True)
    pair_out = pair_mid.astype(jnp.float32) + jnp.einsum(
        "ije,ec->ijc", gated_rows, w_att_out, preferred_element_type=jnp.float32
    )
    return pair_out.astype(jnp.bfloat16)


def dot(a, b):
    return jnp.dot(a, b, preferred_element_type=jnp.float32)


def dot_t(a, b):
    return lax.dot_general(a, b, (((1,), (1,)), ((), ())), preferred_element_type=jnp.float32)


def sigmoid(x):
    return 0.5 * jnp.tanh(0.5 * x) + 0.5


def norm_rows(x, gain):
    average = jnp.mean(x, axis=-1, keepdims=True)
    centred = x - average
    spread = jnp.mean(centred * centred, axis=-1, keepdims=True)
    return centred * lax.rsqrt(spread + norm_eps) * gain


def gated_edges(normed, weight):
    both = dot(normed, weight)
    width = both.shape[1] // 2
    return (sigmoid(both[:, :width]) * both[:, width:]).astype(jnp.bfloat16)


def odd_bits(number):
    return bin(number).count("1") % 2


def parity(number):
    bits = lax.axis_size("row").bit_length() - 1
    return functools.reduce(jnp.bitwise_xor, [number >> b for b in range(bits)]) & 1


def own_side():
    return parity(lax.axis_index("row"))


def stage_kernel(copied, *refs):
    sources, refs = refs[: copied + 4], refs[copied + 4 :]
    (live_ref, *half_refs), copies = refs[:5], refs[5 : copied + 5]
    *early, done = refs[copied + 5 :]
    cross_ref, chain_ref, mask_row_ref, chain_row_ref = early
    moves = [
        pltpu.make_async_copy(source, target, done.at[at])
        for at, (source, target) in enumerate(zip(sources, (*early, *copies), strict=True))
    ]
    for move in moves:
        move.start()
    for move in moves[: len(early)]:
        move.wait()
    residues = live_ref.shape[0]
    blocks, wide = half_refs[1].shape
    tile = 2 * wide // residues
    heads = cross_ref.shape[0]
    row_count = half_refs[0].shape[0] // heads
    mask_row = mask_row_ref[...].astype(jnp.float32)
    chain_row = chain_row_ref[...].astype(jnp.float32)

    line = lax.broadcasted_iota(jnp.int32, (residues, residues), 0)
    spot = lax.broadcasted_iota(jnp.int32, (residues, residues), 1)
    diagonal = jnp.where(line == spot, mask_row, 0.0)
    live_ref[...] = dot(diagonal, jnp.ones((residues, live_ref.shape[1]), jnp.float32))

    line = lax.broadcasted_iota(jnp.int32, (residues, wide), 0)
    lane = lax.broadcasted_iota(jnp.int32, (residues, wide), 1)
    by_column = (lane % tile == line % tile).astype(jnp.float32)
    local = lane // tile
    chip = local // row_count
    block = lax.broadcasted_iota(jnp.int32, (blocks, residues), 0)
    spot = lax.broadcasted_iota(jnp.int32, (blocks, residues), 1)
    column_mask = dot(jnp.where(spot // tile == block, mask_row, 0.0), by_column)
    first = lax.axis_index("row") * row_count
    for half, side in enumerate((own_side(), 1 - own_side())):
        key = (2 * chip + jnp.bitwise_xor(parity(chip), side)) * row_count + local % row_count
        by_key = (key == line).astype(jnp.float32)
        crossing_ref, keep_ref = half_refs[2 * half : 2 * half + 2]
        keep_ref[...] = column_mask * dot(mask_row, by_key)
        chain_wide = dot(chain_row, by_key)
        for i in range(row_count):
            crossing = (chain_wide != chain_ref[first + i].astype(jnp.float32)).astype(jnp.float32)
            for h in range(heads):
                crossing_ref[h * row_count + i : h * row_count + i + 1, :] = cross_ref[h] * crossing
    for move in moves[len(early) :]:
        move.wait()


def spot_of(block_rows, place):
    return pl.ds(pl.multiple_of(place * block_rows, block_rows), block_rows)


def take_blocks(pieces, offsets, row_count, residues, live_ref, gain_ref):
    me = lax.axis_index("row")
    block_rows = row_count * residues
    blocks = [(ref, at) for ref in pieces for at in range(ref.shape[0] // row_count)]
    for (ref, at), offset in zip(blocks, offsets, strict=True):
        device = jnp.bitwise_xor(me, offset)
        acts = ref[at * row_count : (at + 1) * row_count]
        normed = norm_rows(acts.astype(jnp.float32), gain_ref[0:1])
        live_all = live_ref[...]
        rows = [normed[r] * (live_all * live_ref[pl.ds(device * row_count + r, 1), :]) for r in range(row_count)]
        normed = jnp.concatenate(rows, 0).astype(jnp.bfloat16)
        yield spot_of(block_rows, device // 2), acts.reshape(block_rows, acts.shape[-1]), normed


def early_kernel(offsets, row_count, live_ref, gain_ref, w_right_ref, w_left_ref, w_gate_ref, *refs):
    pieces, (acts_ref, right_ref, left_ref, gate_ref) = refs[:-4], refs[-4:]
    residues = live_ref.shape[0]
    for spot, acts, normed in take_blocks(pieces, offsets, row_count, residues, live_ref, gain_ref):
        acts_ref[spot] = acts
        right_ref[spot] = gated_edges(normed, w_right_ref[...])
        left_ref[spot] = gated_edges(normed, w_left_ref[...]).astype(jnp.float32)
        gate_ref[spot] = sigmoid(dot(normed, w_gate_ref[...]))


def right_kernel(offsets, row_count, live_ref, gain_ref, w_right_ref, *refs):
    pieces, (_, _, acts_ref, right_ref, normed_ref) = refs[:-5], refs[-5:]
    residues = live_ref.shape[0]
    block_rows = row_count * residues
    blocks = take_blocks(pieces, offsets, row_count, residues, live_ref, gain_ref)
    for t, (spot, acts, normed) in enumerate(blocks):
        acts_ref[spot] = acts
        right_ref[spot] = gated_edges(normed, w_right_ref[...])
        normed_ref[t * block_rows : (t + 1) * block_rows] = normed


def turn(source, turned_ref, row_count, residues):
    chips = source.shape[0] // (row_count * residues)
    own_count = chips * row_count
    for chip in range(chips):
        for r in range(row_count):
            lower = (chip * row_count + r) * residues
            turned_ref[pl.ds(r * chips + chip, residues, stride=own_count), :] = source[
                lower : lower + residues
            ].astype(jnp.float32)


def multiply(left_ref, turned_ref, residues, store):
    row_block, tile = 8, 8
    count = turned_ref.shape[0] // residues
    own_count = left_ref.shape[0] // residues
    tiles = count // tile

    def rows_of(block, carry):
        first = block * row_block

        def add(k, totals):
            ahead = [
                turned_ref[pl.ds(pl.multiple_of(k * count + t * tile, tile), tile), :] for t in range(tiles)
            ]
            out = []
            for a in range(row_block):
                one = left_ref[pl.ds((first + a) * residues + k, 1), :]
                out.extend(totals[a * tiles + t] + one * ahead[t] for t in range(tiles))
            return tuple(out)

        zeros = tuple(jnp.zeros((tile, left_ref.shape[1]), jnp.float32) for _ in range(row_block * tiles))
        totals = lax.fori_loop(0, residues, add, zeros, unroll=16)
        for a in range(row_block):
            for t in range(tiles):
                store(first + a, t, totals[a * tiles + t])
        return carry

    lax.fori_loop(0, own_count // row_block, rows_of, 0)


def left_kernel(
    offsets, row_count, residues, normed_ref, right_ref, w_left_ref, w_gate_ref, _, __, left_ref, gate_ref, near_ref, turned_ref
):
    me = lax.axis_index("row")
    block_rows = row_count * residues
    for t, offset in enumerate(offsets):
        spot = spot_of(block_rows, jnp.bitwise_xor(me, offset) // 2)
        normed = normed_ref[t * block_rows : (t + 1) * block_rows]
        left_ref[spot] = gated_edges(normed, w_left_ref[...]).astype(jnp.float32)
        gate_ref[spot] = sigmoid(dot(normed, w_gate_ref[...]))
    turn(right_ref, turned_ref, row_count, residues)
    count = turned_ref.shape[0] // residues

    def store(i, t, values):
        near_ref[pl.ds(pl.multiple_of(i * count + t * 8, 8), 8), :] = values

    multiply(left_ref, turned_ref, residues, store)


def product_kernel(
    row_count,
    residues,
    left_ref,
    other_ref,
    near_ref,
    gate_ref,
    acts_ref,
    gain_ref,
    w_out_ref,
    mid_ref,
    normed_mid_ref,
    turned_ref,
    product_ref,
):
    core = own_side()
    turn(other_ref, turned_ref, row_count, residues)
    count = turned_ref.shape[0] // residues
    chips = count // row_count
    part = chips // 8

    line = lax.broadcasted_iota(jnp.int32, (8, 1), 0)
    odd_line = (line ^ (line >> 1) ^ (line >> 2)) & 1

    def store(i, t, values):
        r, eighth = t // part, t % part
        near = near_ref[pl.ds(pl.multiple_of(i * count + t * 8, 8), 8), :]
        near_first = odd_line == (core ^ odd_bits(eighth))
        for side, rows in ((0, jnp.where(near_first, near, values)), (1, jnp.where(near_first, values, near))):
            start = i * residues + (eighth * 16 + side) * row_count + r
            product_ref[pl.ds(start, 8, stride=2 * row_count), :] = rows

    multiply(left_ref, turned_ref, residues, store)

    block_rows = row_count * residues
    for lower in range(0, acts_ref.shape[0], block_rows):
        at = slice(lower, lower + block_rows)
        product = product_ref[at].astype(jnp.bfloat16).astype(jnp.float32)
        product = norm_rows(product, gain_ref[1:2]).astype(jnp.bfloat16)
        update = gate_ref[at] * dot(product, w_out_ref[...])
        mid = (acts_ref[at].astype(jnp.float32) + update).astype(jnp.bfloat16)
        mid_ref[at] = mid
        normed_mid_ref[at] = norm_rows(mid.astype(jnp.float32), gain_ref[2:3]).astype(jnp.bfloat16)


def half_attention(rows_ref, pair_ref, asked, w_bias, crossing_ref, keep_ref):
    count, residues, channels = pair_ref.shape
    heads = w_bias.shape[0]
    row_count = crossing_ref.shape[0] // heads
    tile = 8
    wide = count * tile
    for local in range(count):
        pair_ref[local] = rows_ref[local * residues : (local + 1) * residues].astype(jnp.float32)
    first = lax.axis_index("row") * row_count
    pieces = []
    for i in range(row_count):
        column = pair_ref[:, pl.ds(first + i, 1), :]
        spread = jnp.broadcast_to(column, (count, tile, channels)).reshape(wide, channels)
        pieces.append(dot_t(w_bias, spread.astype(jnp.bfloat16)).astype(jnp.bfloat16).astype(jnp.float32))
    extra = jnp.concatenate(
        [
            jnp.broadcast_to(pieces[i][h : h + 1] + crossing_ref[h * row_count + i : h * row_count + i + 1], (tile, wide))
            for h in range(heads)
            for i in range(row_count)
        ],
        0,
    )
    shape = extra.shape
    same = lax.broadcasted_iota(jnp.int32, shape, 0) % tile == lax.broadcasted_iota(jnp.int32, shape, 1) % tile
    low = jnp.where(same, -1000000000.0, -1e30)
    groups = range(residues // tile)
    keys = [
        pair_ref[:, g * tile : (g + 1) * tile, :].reshape(wide, channels).astype(jnp.bfloat16) for g in groups
    ]
    scores = [dot_t(asked[g], keys[g]) for g in groups]
    scores = [
        jnp.where(jnp.logical_and(same, keep_ref[g : g + 1, :] > 0), scores[g] + extra, low) for g in groups
    ]
    return scores, keys


def near_attend_kernel(
    row_count, residues, own_ref, w_att_ref, w_bias_ref, crossing_ref, keep_ref, asked_ref, gate_ref, top_ref, total_ref, context_ref, pair_ref
):
    block_rows = row_count * residues
    heads = w_bias_ref.shape[0]
    inner = w_att_ref.shape[1] // 4
    head_dim = inner // heads
    tile = 8
    groups = range(residues // tile)
    mine = own_ref[spot_of(block_rows, lax.axis_index("row") // 2)]
    query = (dot(mine, w_att_ref[:, :inner]) * head_dim ** (-0.5)).astype(jnp.bfloat16)
    gate_ref[...] = sigmoid(dot(mine, w_att_ref[:, 3 * inner :]))
    head_of = lax.broadcasted_iota(jnp.int32, (1, inner), 1) // head_dim
    by_head = [
        dot_t(query, jnp.where(head_of == h, w_att_ref[:, inner : 2 * inner], 0)) for h in range(heads)
    ]
    asked = [
        jnp.concatenate(
            [
                by_head[h][i * residues + g * tile : i * residues + (g + 1) * tile]
                for h in range(heads)
                for i in range(row_count)
            ],
            0,
        ).astype(jnp.bfloat16)
        for g in groups
    ]
    for g in groups:
        asked_ref[g] = asked[g]
    scores, keys = half_attention(own_ref, pair_ref, asked, w_bias_ref[...], crossing_ref, keep_ref)
    tops = [jnp.max(s, axis=-1, keepdims=True) for s in scores]
    scores = [jnp.exp(s - top) for s, top in zip(scores, tops, strict=True)]
    totals = [jnp.sum(s, axis=-1, keepdims=True) for s in scores]
    for g in groups:
        context_ref[g] = dot(scores[g].astype(jnp.bfloat16), keys[g])
        top_ref[g] = jnp.broadcast_to(tops[g], top_ref.shape[1:])
        total_ref[g] = jnp.broadcast_to(totals[g], total_ref.shape[1:])


def attend_kernel(
    row_count,
    other_ref,
    mid_ref,
    asked_ref,
    gate_ref,
    top_ref,
    total_ref,
    context_ref,
    crossing_ref,
    keep_ref,
    w_att_ref,
    w_bias_ref,
    w_out_ref,
    out_ref,
    pair_ref,
):
    residues = pair_ref.shape[1]
    heads = w_bias_ref.shape[0]
    inner = w_out_ref.shape[0]
    head_dim = inner // heads
    block_rows = row_count * residues
    tile = 8
    groups = range(residues // tile)
    asked = [asked_ref[g] for g in groups]
    scores, keys = half_attention(other_ref, pair_ref, asked, w_bias_ref[...], crossing_ref, keep_ref)
    tops = [jnp.maximum(jnp.max(scores[g], axis=-1, keepdims=True), top_ref[g]) for g in groups]
    scales = [jnp.exp(top_ref[g] - tops[g]) for g in groups]
    scores = [jnp.exp(scores[g] - tops[g][:, :1]) for g in groups]
    totals = [jnp.sum(scores[g], axis=-1, keepdims=True) + total_ref[g] * scales[g] for g in groups]
    context = [dot(scores[g].astype(jnp.bfloat16), keys[g]) + context_ref[g] * scales[g] for g in groups]
    context = [context[g] * (1.0 / totals[g]) for g in groups]

    head_of = lax.broadcasted_iota(jnp.int32, (1, inner), 1) // head_dim
    values = jnp.zeros((block_rows, inner), jnp.float32)
    for h in range(heads):
        w_value = jnp.where(head_of == h, w_att_ref[:, 2 * inner : 3 * inner], 0)
        rows = [
            context[g][(h * row_count + i) * tile : (h * row_count + i + 1) * tile]
            for i in range(row_count)
            for g in groups
        ]
        values = values + dot(jnp.concatenate(rows, 0).astype(jnp.bfloat16), w_value)
    gated = (values * gate_ref[...]).astype(jnp.bfloat16)
    mid = mid_ref[spot_of(block_rows, lax.axis_index("row") // 2)].astype(jnp.float32)
    out_ref[...] = (mid + dot(gated, w_out_ref[...])).astype(jnp.bfloat16).reshape(out_ref.shape)


def call(body, args, outs, cost_us, name, scratch=(), aliases=None, space=pltpu.VMEM):
    return pl.pallas_call(
        body,
        out_shape=[jax.ShapeDtypeStruct(shape, dtype) for shape, dtype in outs],
        in_specs=[pl.BlockSpec(memory_space=space)] * len(args),
        out_specs=[pl.BlockSpec(memory_space=pltpu.VMEM)] * len(outs),
        scratch_shapes=list(scratch),
        input_output_aliases=aliases or {},
        compiler_params=pltpu.CompilerParams(vmem_limit_bytes=24 * 2**20),
        cost_estimate=pl.CostEstimate(flops=int(cost_us * 1e9), bytes_accessed=2**18, transcendentals=0),
        name=name,
    )(*args)


def gathered(
    row_devices,
    pair_acts,
    res_mask,
    chain_id,
    in_gain,
    w_left,
    w_right,
    w_mult_gate,
    mult_gain,
    w_mult_out,
    att_gain,
    w_att,
    w_pair_bias,
    cross_bias,
    w_att_out,
):
    row_count, residues, channels = pair_acts.shape
    width = w_left.shape[1] // 2
    heads = w_pair_bias.shape[1]
    own_count = residues // 2
    pairs = own_count * residues
    block_rows = row_count * residues
    tile = 8
    wide = own_count * tile
    bf16, f32 = jnp.bfloat16, jnp.float32

    def swap(x, shift):
        return lax.ppermute(x, "row", [(i, i ^ shift) for i in range(row_devices)])

    base, held = [0], pair_acts
    far, near, side = 9, 5, 3

    def spread(shifts):
        return [o ^ s for s in shifts for o in base]

    shift = row_devices // 2
    while shift > far:
        held = jnp.concatenate([held, swap(held, shift + 1)], 0)
        base = base + [o ^ (shift + 1) for o in base]
        shift //= 2
    from_far = swap(held, far)
    from_side = swap(held, side)
    from_near = swap(held, near)
    from_corner = swap(held, near ^ side)

    weights = [
        in_gain[None],
        mult_gain[None],
        att_gain[None],
        w_right,
        w_left,
        w_mult_gate,
        w_mult_out,
        w_att,
        w_pair_bias.T,
        w_att_out,
        held,
    ]
    live, crossing, keep, far_crossing, far_keep, in_g, mult_g, att_g, w_r, w_l, w_g, w_m, w_a, w_b, w_o, held = call(
        functools.partial(stage_kernel, len(weights)),
        [
            pltpu.with_memory_space_constraint(x, pltpu.HBM)
            for x in (cross_bias, chain_id, res_mask[None], chain_id[None], *weights)
        ],
        [((residues, channels), f32)] + 2 * [((heads * row_count, wide), f32), ((residues // tile, wide), f32)]
        + [(w.shape, w.dtype) for w in weights],
        0.05,
        "stage",
        [
            pltpu.SMEM((heads,), f32),
            pltpu.SMEM((residues,), jnp.int32),
            pltpu.VMEM((1, residues), jnp.int32),
            pltpu.VMEM((1, residues), jnp.int32),
            pltpu.SemaphoreType.DMA((len(weights) + 4,)),
        ],
        space=pltpu.HBM,
    )
    from_far_near = swap(from_far, near)
    from_far_corner = swap(from_far, near ^ side)
    from_far_side = swap(from_far, side)

    sizes = [((pairs, channels), bf16), ((pairs, width), bf16), ((pairs, width), f32), ((pairs, channels), f32)]
    acts, right, left, gate = call(
        functools.partial(early_kernel, spread([0, far, side, near, near ^ side]), row_count),
        [live, in_g, w_r, w_l, w_g, held, from_far, from_side, from_near, from_corner],
        sizes,
        0.05,
        "early_edges",
    )
    late = spread([far ^ near ^ side, far ^ near, far ^ side])
    acts, right, normed = call(
        functools.partial(right_kernel, late, row_count),
        [live, in_g, w_r, from_far_corner, from_far_near, from_far_side, acts, right],
        [*sizes[:2], ((len(late) * block_rows, channels), bf16)],
        0.5,
        "right_edges",
        aliases={6: 0, 7: 1},
    )
    other = swap(right, 1)
    left, gate, near_product = call(
        functools.partial(left_kernel, late, row_count, residues),
        [normed, right, w_l, w_g, left, gate],
        [*sizes[2:], ((own_count * own_count, width), f32)],
        1.5,
        "left_edges",
        scratch=[pltpu.VMEM((pairs, width), f32)],
        aliases={4: 0, 5: 1},
    )
    mid, normed_mid = call(
        functools.partial(product_kernel, row_count, residues),
        [left, other, near_product, gate, acts, jnp.concatenate([in_g, mult_g, att_g], 0), w_m],
        [((pairs, channels), bf16), ((pairs, channels), bf16)],
        2.4,
        "product",
        scratch=[pltpu.VMEM((pairs, width), f32), pltpu.VMEM((pairs, width), f32)],
    )
    normed_other = swap(normed_mid, 1)
    groups, asked_rows = residues // tile, heads * row_count * tile
    asked, gate_att, top, total, context = call(
        functools.partial(near_attend_kernel, row_count, residues),
        [normed_mid, w_a, w_b, crossing, keep],
        [((groups, asked_rows, channels), bf16), ((block_rows, w_o.shape[0]), f32)]
        + 3 * [((groups, asked_rows, channels), f32)],
        1.2,
        "near_attend",
        scratch=[pltpu.VMEM((own_count, residues, channels), f32)],
    )
    (out,) = call(
        functools.partial(attend_kernel, row_count),
        [normed_other, mid, asked, gate_att, top, total, context, far_crossing, far_keep, w_a, w_b, w_o],
        [((row_count, residues, channels), bf16)],
        1.5,
        "attend",
        scratch=[pltpu.VMEM((own_count, residues, channels), f32)],
    )
    return out


def solution(mesh):
    placed = (
        P(("groups", "row"), None, None),
        P("groups"),
        P("groups"),
        P(),
        P(),
        P(),
        P(),
        P(),
        P(),
        P(),
        P(),
        P(),
        P(),
        P(),
    )
    row_devices = mesh.shape["row"]

    def whole(pair_acts, *others):
        row_count, residues, channels = pair_acts.shape
        in_vmem = 4 * residues * residues * channels <= vmem_share
        paired = row_devices % 16 == 0 and row_devices & (row_devices - 1) == 0 and residues % 8 == 0
        if in_vmem and paired:
            return gathered(row_devices, pair_acts, *others)
        return shards(pair_acts, *others)

    return jax.shard_map(
        whole,
        mesh=mesh,
        in_specs=placed,
        out_specs=P(("groups", "row"), None, None),
        check_vma=False,
    )
```

```python
import functools

import jax
import jax.numpy as jnp
from jax import lax
from jax.experimental import pallas as pl
from jax.experimental.pallas import tpu as pltpu
from jax.sharding import PartitionSpec as P

norm_eps = 1e-05
vmem_share = 4 * 2**20


def layer_norm(tensor, norm_axis):
    tensor = tensor.astype(jnp.float32)
    average = jnp.mean(tensor, axis=norm_axis, keepdims=True)
    spread = jnp.mean(jnp.square(tensor - average), axis=norm_axis, keepdims=True)
    return (tensor - average) * lax.rsqrt(spread + norm_eps)


def edges_of(normed, weight, row_mask, mult_width):
    gate_part = jnp.einsum(
        "ikc,cm->mik", normed, weight[:, :mult_width], preferred_element_type=jnp.float32
    )
    value_part = jnp.einsum(
        "ikc,cm->mik", normed, weight[:, mult_width:], preferred_element_type=jnp.float32
    )
    return (row_mask[None] * jax.nn.sigmoid(gate_part) * value_part).astype(jnp.bfloat16)


def attend(normed_cols, bias_table, mask_float, chain_id, cross_bias, w_att, first_col):
    residues, col_count, _ = normed_cols.shape
    inner_dim = w_att.shape[1] // 4
    head_count = cross_bias.shape[0]
    head_dim = inner_dim // head_count

    def project(slot_idx):
        return jnp.einsum(
            "ijc,ce->ije",
            normed_cols,
            w_att[:, slot_idx * inner_dim : (slot_idx + 1) * inner_dim],
            preferred_element_type=jnp.float32,
        )

    query_all = (
        (project(0) * head_dim ** (-0.5))
        .astype(jnp.bfloat16)
        .reshape(residues, col_count, head_count, head_dim)
    )
    key_all = project(1).astype(jnp.bfloat16).reshape(residues, col_count, head_count, head_dim)
    value_all = project(2).astype(jnp.bfloat16).reshape(residues, col_count, head_count, head_dim)
    gate_att = jax.nn.sigmoid(project(3))
    crossing = (chain_id[:, None] != chain_id[None, :]).astype(jnp.float32)
    half_rows = residues // 2

    def column(col_index):
        query = lax.dynamic_index_in_dim(query_all, col_index, 1, keepdims=False)
        key_col = lax.dynamic_index_in_dim(key_all, col_index, 1, keepdims=False)
        value_col = lax.dynamic_index_in_dim(value_all, col_index, 1, keepdims=False)
        own_live = lax.dynamic_index_in_dim(mask_float, first_col + col_index, 0, keepdims=False)
        key_live = mask_float * own_live > 0
        pieces_out = []
        for block_idx in range(2):
            lower_row = block_idx * half_rows
            query_block = query[lower_row : lower_row + half_rows]
            scores = jnp.einsum(
                "ihd,khd->hki", query_block, key_col, preferred_element_type=jnp.float32
            )
            scores = scores + (
                bias_table[:, :, lower_row : lower_row + half_rows].astype(jnp.float32)
                + cross_bias[:, None, None] * crossing[None, :, lower_row : lower_row + half_rows]
            )
            scores = jnp.where(key_live[None, :, None], scores, -1000000000.0)
            weights = jax.nn.softmax(scores, axis=1).astype(jnp.bfloat16)
            pieces_out.append(
                jnp.einsum("hki,khd->ihd", weights, value_col, preferred_element_type=jnp.float32)
            )
        return jnp.concatenate(pieces_out, 0)

    outputs = lax.map(column, jnp.arange(col_count, dtype=jnp.int32))
    outputs = jnp.transpose(outputs, (1, 0, 2, 3)).reshape(residues, col_count, inner_dim)
    return (outputs * gate_att).astype(jnp.bfloat16)


def shards(
    pair_acts,
    res_mask,
    chain_id,
    in_gain,
    w_left,
    w_right,
    w_mult_gate,
    mult_gain,
    w_mult_out,
    att_gain,
    w_att,
    w_pair_bias,
    cross_bias,
    w_att_out,
):
    row_count = pair_acts.shape[0]
    mult_width = w_left.shape[1] // 2
    first_row = lax.axis_index("row") * row_count
    mask_float = res_mask.astype(jnp.float32)
    own_mask = lax.dynamic_slice_in_dim(mask_float, first_row, row_count)
    row_mask = own_mask[:, None] * mask_float[None, :]
    normed = (layer_norm(pair_acts, -1) * in_gain).astype(jnp.bfloat16)
    left_edges = edges_of(normed, w_left, row_mask, mult_width)
    right_edges = edges_of(normed, w_right, row_mask, mult_width)
    left_chan, right_chan = (
        lax.all_to_all(left_edges, "row", split_axis=0, concat_axis=1, tiled=True),
        lax.all_to_all(right_edges, "row", split_axis=0, concat_axis=1, tiled=True),
    )
    product = jnp.einsum(
        "cik,cjk->cij", left_chan, right_chan, preferred_element_type=jnp.float32
    ).astype(jnp.bfloat16)
    product_own = lax.all_to_all(product, "row", split_axis=1, concat_axis=0, tiled=True)
    product_norm = (layer_norm(product_own, 0) * mult_gain[:, None, None]).astype(jnp.bfloat16)
    gate_mult = jax.nn.sigmoid(
        jnp.einsum("ijc,cd->ijd", normed, w_mult_gate, preferred_element_type=jnp.float32)
    )
    update = jnp.einsum("mij,mc->ijc", product_norm, w_mult_out, preferred_element_type=jnp.float32)
    pair_mid = (pair_acts.astype(jnp.float32) + gate_mult * update).astype(jnp.bfloat16)
    normed_mid = (layer_norm(pair_mid, -1) * att_gain).astype(jnp.bfloat16)
    bias_piece = jnp.einsum(
        "kic,ch->hki", normed_mid, w_pair_bias, preferred_element_type=jnp.float32
    ).astype(jnp.bfloat16)
    bias_table = lax.all_gather(bias_piece, "row", axis=1, tiled=True)
    normed_cols = lax.all_to_all(normed_mid, "row", split_axis=1, concat_axis=0, tiled=True)
    gated = attend(normed_cols, bias_table, mask_float, chain_id, cross_bias, w_att, first_row)
    gated_rows = lax.all_to_all(gated, "row", split_axis=0, concat_axis=1, tiled=True)
    pair_out = pair_mid.astype(jnp.float32) + jnp.einsum(
        "ije,ec->ijc", gated_rows, w_att_out, preferred_element_type=jnp.float32
    )
    return pair_out.astype(jnp.bfloat16)


def dot(a, b):
    return jnp.dot(a, b, preferred_element_type=jnp.float32)


def dot_t(a, b):
    return lax.dot_general(a, b, (((1,), (1,)), ((), ())), preferred_element_type=jnp.float32)


def sigmoid(x):
    return 0.5 * jnp.tanh(0.5 * x) + 0.5


def norm_rows(x, gain):
    average = jnp.mean(x, axis=-1, keepdims=True)
    centred = x - average
    spread = jnp.mean(centred * centred, axis=-1, keepdims=True)
    return centred * lax.rsqrt(spread + norm_eps) * gain


def norm_all(pieces, gain):
    width = pieces[0].shape[-1]
    ones = jnp.ones((width, width), jnp.bfloat16)
    sums = [dot(x, ones) for x in pieces]
    centred = [x.astype(jnp.float32) - s * (1.0 / width) for x, s in zip(pieces, sums, strict=True)]
    spreads = [jnp.mean(c * c, axis=-1, keepdims=True) for c in centred]
    return [
        (c * lax.rsqrt(s + norm_eps) * gain).astype(jnp.bfloat16) for c, s in zip(centred, spreads, strict=True)
    ]


def gated_edges(normed, weight):
    both = dot(normed, weight)
    width = both.shape[1] // 2
    return (sigmoid(both[:, :width]) * both[:, width:]).astype(jnp.bfloat16)


def odd_bits(number):
    return bin(number).count("1") % 2


def parity(number):
    bits = lax.axis_size("row").bit_length() - 1
    return functools.reduce(jnp.bitwise_xor, [number >> b for b in range(bits)]) & 1


def own_side():
    return parity(lax.axis_index("row"))


def stage_kernel(copied, *refs):
    sources, refs = refs[: copied + 4], refs[copied + 4 :]
    (live_ref, *half_refs), copies = refs[:5], refs[5 : copied + 5]
    *early, done = refs[copied + 5 :]
    cross_ref, chain_ref, mask_row_ref, chain_row_ref = early
    moves = [
        pltpu.make_async_copy(source, target, done.at[at])
        for at, (source, target) in enumerate(zip(sources, (*early, *copies), strict=True))
    ]
    for move in moves:
        move.start()
    for move in moves[: len(early)]:
        move.wait()
    residues = live_ref.shape[0]
    blocks, wide = half_refs[1].shape
    tile = 2 * wide // residues
    heads = cross_ref.shape[0]
    row_count = half_refs[0].shape[0] // heads
    mask_row = mask_row_ref[...].astype(jnp.float32)
    chain_row = chain_row_ref[...].astype(jnp.float32)

    line = lax.broadcasted_iota(jnp.int32, (residues, residues), 0)
    spot = lax.broadcasted_iota(jnp.int32, (residues, residues), 1)
    diagonal = jnp.where(line == spot, mask_row, 0.0)
    live_ref[...] = dot(diagonal, jnp.ones((residues, live_ref.shape[1]), jnp.float32))

    line = lax.broadcasted_iota(jnp.int32, (residues, wide), 0)
    lane = lax.broadcasted_iota(jnp.int32, (residues, wide), 1)
    by_column = (lane % tile == line % tile).astype(jnp.float32)
    local = lane // tile
    chip = local // row_count
    block = lax.broadcasted_iota(jnp.int32, (blocks, residues), 0)
    spot = lax.broadcasted_iota(jnp.int32, (blocks, residues), 1)
    column_mask = dot(jnp.where(spot // tile == block, mask_row, 0.0), by_column)
    first = lax.axis_index("row") * row_count
    for half, side in enumerate((own_side(), 1 - own_side())):
        key = (2 * chip + jnp.bitwise_xor(parity(chip), side)) * row_count + local % row_count
        by_key = (key == line).astype(jnp.float32)
        crossing_ref, keep_ref = half_refs[2 * half : 2 * half + 2]
        keep_ref[...] = column_mask * dot(mask_row, by_key)
        chain_wide = dot(chain_row, by_key)
        for i in range(row_count):
            crossing = (chain_wide != chain_ref[first + i].astype(jnp.float32)).astype(jnp.float32)
            for h in range(heads):
                crossing_ref[h * row_count + i : h * row_count + i + 1, :] = cross_ref[h] * crossing
    for move in moves[len(early) :]:
        move.wait()


def spot_of(block_rows, place):
    return pl.ds(pl.multiple_of(place * block_rows, block_rows), block_rows)


def take_blocks(pieces, offsets, row_count, residues, live_ref, gain_ref):
    me = lax.axis_index("row")
    block_rows = row_count * residues
    blocks = [(ref, at) for ref in pieces for at in range(ref.shape[0] // row_count)]
    for (ref, at), offset in zip(blocks, offsets, strict=True):
        device = jnp.bitwise_xor(me, offset)
        acts = ref[at * row_count : (at + 1) * row_count]
        normed = norm_rows(acts.astype(jnp.float32), gain_ref[0:1])
        live_all = live_ref[...]
        rows = [normed[r] * (live_all * live_ref[pl.ds(device * row_count + r, 1), :]) for r in range(row_count)]
        normed = jnp.concatenate(rows, 0).astype(jnp.bfloat16)
        yield spot_of(block_rows, device // 2), acts.reshape(block_rows, acts.shape[-1]), normed


def early_kernel(offsets, row_count, live_ref, gain_ref, w_right_ref, w_left_ref, w_gate_ref, *refs):
    pieces, (acts_ref, right_ref, left_ref, gate_ref) = refs[:-4], refs[-4:]
    residues = live_ref.shape[0]
    for spot, acts, normed in take_blocks(pieces, offsets, row_count, residues, live_ref, gain_ref):
        acts_ref[spot] = acts
        right_ref[spot] = gated_edges(normed, w_right_ref[...])
        left_ref[spot] = gated_edges(normed, w_left_ref[...]).astype(jnp.float32)
        gate_ref[spot] = sigmoid(dot(normed, w_gate_ref[...]))


def right_kernel(offsets, row_count, live_ref, gain_ref, w_right_ref, *refs):
    pieces, (_, _, acts_ref, right_ref, normed_ref) = refs[:-5], refs[-5:]
    residues = live_ref.shape[0]
    block_rows = row_count * residues
    blocks = take_blocks(pieces, offsets, row_count, residues, live_ref, gain_ref)
    for t, (spot, acts, normed) in enumerate(blocks):
        acts_ref[spot] = acts
        right_ref[spot] = gated_edges(normed, w_right_ref[...])
        normed_ref[t * block_rows : (t + 1) * block_rows] = normed


def turn(source, turned_ref, row_count, residues):
    chips = source.shape[0] // (row_count * residues)
    own_count = chips * row_count
    for chip in range(chips):
        for r in range(row_count):
            lower = (chip * row_count + r) * residues
            turned_ref[pl.ds(r * chips + chip, residues, stride=own_count), :] = source[
                lower : lower + residues
            ].astype(jnp.float32)


def multiply(left_ref, turned_ref, residues, store):
    row_block, tile = 8, 8
    count = turned_ref.shape[0] // residues
    own_count = left_ref.shape[0] // residues
    tiles = count // tile

    def rows_of(block, carry):
        first = block * row_block

        def add(k, totals):
            ahead = [
                turned_ref[pl.ds(pl.multiple_of(k * count + t * tile, tile), tile), :] for t in range(tiles)
            ]
            out = []
            for a in range(row_block):
                one = left_ref[pl.ds((first + a) * residues + k, 1), :]
                out.extend(totals[a * tiles + t] + one * ahead[t] for t in range(tiles))
            return tuple(out)

        zeros = tuple(jnp.zeros((tile, left_ref.shape[1]), jnp.float32) for _ in range(row_block * tiles))
        totals = lax.fori_loop(0, residues, add, zeros, unroll=16)
        for a in range(row_block):
            for t in range(tiles):
                store(first + a, t, totals[a * tiles + t])
        return carry

    lax.fori_loop(0, own_count // row_block, rows_of, 0)


def left_kernel(
    offsets, row_count, residues, normed_ref, right_ref, w_left_ref, w_gate_ref, _, __, left_ref, gate_ref, near_ref, turned_ref
):
    me = lax.axis_index("row")
    block_rows = row_count * residues
    for t, offset in enumerate(offsets):
        spot = spot_of(block_rows, jnp.bitwise_xor(me, offset) // 2)
        normed = normed_ref[t * block_rows : (t + 1) * block_rows]
        left_ref[spot] = gated_edges(normed, w_left_ref[...]).astype(jnp.float32)
        gate_ref[spot] = sigmoid(dot(normed, w_gate_ref[...]))
    turn(right_ref, turned_ref, row_count, residues)
    count = turned_ref.shape[0] // residues

    def store(i, t, values):
        near_ref[pl.ds(pl.multiple_of(i * count + t * 8, 8), 8), :] = values

    multiply(left_ref, turned_ref, residues, store)


def product_kernel(
    row_count,
    residues,
    left_ref,
    other_ref,
    near_ref,
    gate_ref,
    acts_ref,
    gain_ref,
    w_out_ref,
    mid_ref,
    normed_mid_ref,
    turned_ref,
    product_ref,
):
    core = own_side()
    turn(other_ref, turned_ref, row_count, residues)
    count = turned_ref.shape[0] // residues
    chips = count // row_count
    part = chips // 8

    line = lax.broadcasted_iota(jnp.int32, (8, 1), 0)
    odd_line = (line ^ (line >> 1) ^ (line >> 2)) & 1

    def store(i, t, values):
        r, eighth = t // part, t % part
        near = near_ref[pl.ds(pl.multiple_of(i * count + t * 8, 8), 8), :]
        near_first = odd_line == (core ^ odd_bits(eighth))
        for side, rows in ((0, jnp.where(near_first, near, values)), (1, jnp.where(near_first, values, near))):
            start = i * residues + (eighth * 16 + side) * row_count + r
            product_ref[pl.ds(start, 8, stride=2 * row_count), :] = rows

    multiply(left_ref, turned_ref, residues, store)

    step = 2 * row_count * residues
    spots = [slice(lower, lower + step) for lower in range(0, acts_ref.shape[0], step)]
    normed = norm_all([product_ref[at].astype(jnp.bfloat16) for at in spots], gain_ref[1:2])
    updates = [gate_ref[at] * dot(rows, w_out_ref[...]) for at, rows in zip(spots, normed, strict=True)]
    mids = [
        (acts_ref[at].astype(jnp.float32) + update).astype(jnp.bfloat16)
        for at, update in zip(spots, updates, strict=True)
    ]
    for at, mid in zip(spots, mids, strict=True):
        mid_ref[at] = mid
    for at, rows in zip(spots, norm_all(mids, gain_ref[2:3]), strict=True):
        normed_mid_ref[at] = rows


def half_attention(rows_ref, pair_ref, asked, w_bias, crossing_ref, keep_ref):
    count, residues, channels = pair_ref.shape
    heads = w_bias.shape[0]
    row_count = crossing_ref.shape[0] // heads
    tile = 8
    wide = count * tile
    for local in range(count):
        pair_ref[local] = rows_ref[local * residues : (local + 1) * residues].astype(jnp.float32)
    first = lax.axis_index("row") * row_count
    pieces = []
    for i in range(row_count):
        column = pair_ref[:, pl.ds(first + i, 1), :]
        spread = jnp.broadcast_to(column, (count, tile, channels)).reshape(wide, channels)
        pieces.append(dot_t(w_bias, spread.astype(jnp.bfloat16)).astype(jnp.bfloat16).astype(jnp.float32))
    extra = jnp.concatenate(
        [
            jnp.broadcast_to(pieces[i][h : h + 1] + crossing_ref[h * row_count + i : h * row_count + i + 1], (tile, wide))
            for h in range(heads)
            for i in range(row_count)
        ],
        0,
    )
    shape = extra.shape
    same = lax.broadcasted_iota(jnp.int32, shape, 0) % tile == lax.broadcasted_iota(jnp.int32, shape, 1) % tile
    low = jnp.where(same, -1000000000.0, -1e30)
    groups = range(residues // tile)
    keys = [
        pair_ref[:, g * tile : (g + 1) * tile, :].reshape(wide, channels).astype(jnp.bfloat16) for g in groups
    ]
    scores = [dot_t(asked[g], keys[g]) for g in groups]
    scores = [
        jnp.where(jnp.logical_and(same, keep_ref[g : g + 1, :] > 0), scores[g] + extra, low) for g in groups
    ]
    return scores, keys


def near_attend_kernel(
    row_count, residues, own_ref, w_att_ref, w_bias_ref, crossing_ref, keep_ref, asked_ref, gate_ref, top_ref, total_ref, context_ref, pair_ref
):
    block_rows = row_count * residues
    heads = w_bias_ref.shape[0]
    inner = w_att_ref.shape[1] // 4
    head_dim = inner // heads
    tile = 8
    groups = range(residues // tile)
    mine = own_ref[spot_of(block_rows, lax.axis_index("row") // 2)]
    query = (dot(mine, w_att_ref[:, :inner]) * head_dim ** (-0.5)).astype(jnp.bfloat16)
    gate_ref[...] = sigmoid(dot(mine, w_att_ref[:, 3 * inner :]))
    head_of = lax.broadcasted_iota(jnp.int32, (1, inner), 1) // head_dim
    w_key = w_att_ref[:, inner : 2 * inner]
    w_key = jnp.concatenate([jnp.where(head_of == h, w_key, 0) for h in range(heads)], 0)
    by_head = jnp.split(dot_t(query, w_key), heads, 1)
    asked = [
        jnp.concatenate(
            [
                by_head[h][i * residues + g * tile : i * residues + (g + 1) * tile]
                for h in range(heads)
                for i in range(row_count)
            ],
            0,
        ).astype(jnp.bfloat16)
        for g in groups
    ]
    for g in groups:
        asked_ref[g] = asked[g]
    scores, keys = half_attention(own_ref, pair_ref, asked, w_bias_ref[...], crossing_ref, keep_ref)
    tops = [jnp.max(s, axis=-1, keepdims=True) for s in scores]
    scores = [jnp.exp(s - top) for s, top in zip(scores, tops, strict=True)]
    totals = [jnp.sum(s, axis=-1, keepdims=True) for s in scores]
    for g in groups:
        context_ref[g] = dot(scores[g].astype(jnp.bfloat16), keys[g])
        top_ref[g] = jnp.broadcast_to(tops[g], top_ref.shape[1:])
        total_ref[g] = jnp.broadcast_to(totals[g], total_ref.shape[1:])


def attend_kernel(
    row_count,
    other_ref,
    mid_ref,
    asked_ref,
    gate_ref,
    top_ref,
    total_ref,
    context_ref,
    crossing_ref,
    keep_ref,
    w_att_ref,
    w_bias_ref,
    w_out_ref,
    out_ref,
    pair_ref,
):
    residues = pair_ref.shape[1]
    heads = w_bias_ref.shape[0]
    inner = w_out_ref.shape[0]
    head_dim = inner // heads
    block_rows = row_count * residues
    tile = 8
    groups = range(residues // tile)
    asked = [asked_ref[g] for g in groups]
    scores, keys = half_attention(other_ref, pair_ref, asked, w_bias_ref[...], crossing_ref, keep_ref)
    tops = [jnp.maximum(jnp.max(scores[g], axis=-1, keepdims=True), top_ref[g]) for g in groups]
    scales = [jnp.exp(top_ref[g] - tops[g]) for g in groups]
    copies = pl.cdiv(scores[0].shape[1], tops[0].shape[1])
    scores = [jnp.exp(s - jnp.concatenate([top] * copies, 1)[:, : s.shape[1]]) for s, top in zip(scores, tops, strict=True)]
    totals = [jnp.sum(scores[g], axis=-1, keepdims=True) + total_ref[g] * scales[g] for g in groups]
    context = [dot(scores[g].astype(jnp.bfloat16), keys[g]) + context_ref[g] * scales[g] for g in groups]
    context = [context[g] * (1.0 / totals[g]) for g in groups]

    head_of = lax.broadcasted_iota(jnp.int32, (1, inner), 1) // head_dim
    by_head = [
        jnp.concatenate(
            [
                context[g][(h * row_count + i) * tile : (h * row_count + i + 1) * tile]
                for i in range(row_count)
                for g in groups
            ],
            0,
        ).astype(jnp.bfloat16)
        for h in range(heads)
    ]
    w_value = w_att_ref[:, 2 * inner : 3 * inner]
    w_value = jnp.concatenate([jnp.where(head_of == h, w_value, 0) for h in range(heads)], 0)
    values = dot(jnp.concatenate(by_head, 1), w_value)
    gated = (values * gate_ref[...]).astype(jnp.bfloat16)
    mid = mid_ref[spot_of(block_rows, lax.axis_index("row") // 2)].astype(jnp.float32)
    out_ref[...] = (mid + dot(gated, w_out_ref[...])).astype(jnp.bfloat16).reshape(out_ref.shape)


def call(body, args, outs, cost_us, name, scratch=(), aliases=None, space=pltpu.VMEM):
    return pl.pallas_call(
        body,
        out_shape=[jax.ShapeDtypeStruct(shape, dtype) for shape, dtype in outs],
        in_specs=[pl.BlockSpec(memory_space=space)] * len(args),
        out_specs=[pl.BlockSpec(memory_space=pltpu.VMEM)] * len(outs),
        scratch_shapes=list(scratch),
        input_output_aliases=aliases or {},
        compiler_params=pltpu.CompilerParams(vmem_limit_bytes=24 * 2**20),
        cost_estimate=pl.CostEstimate(flops=int(cost_us * 1e9), bytes_accessed=2**18, transcendentals=0),
        name=name,
    )(*args)


def gathered(
    row_devices,
    pair_acts,
    res_mask,
    chain_id,
    in_gain,
    w_left,
    w_right,
    w_mult_gate,
    mult_gain,
    w_mult_out,
    att_gain,
    w_att,
    w_pair_bias,
    cross_bias,
    w_att_out,
):
    row_count, residues, channels = pair_acts.shape
    width = w_left.shape[1] // 2
    heads = w_pair_bias.shape[1]
    own_count = residues // 2
    pairs = own_count * residues
    block_rows = row_count * residues
    tile = 8
    wide = own_count * tile
    bf16, f32 = jnp.bfloat16, jnp.float32

    def swap(x, shift):
        return lax.ppermute(x, "row", [(i, i ^ shift) for i in range(row_devices)])

    base, held = [0], pair_acts
    far, near, side = 9, 5, 3

    def spread(shifts):
        return [o ^ s for s in shifts for o in base]

    shift = row_devices // 2
    while shift > far:
        held = jnp.concatenate([held, swap(held, shift + 1)], 0)
        base = base + [o ^ (shift + 1) for o in base]
        shift //= 2
    from_far = swap(held, far)
    from_side = swap(held, side)
    from_near = swap(held, near)
    from_corner = swap(held, near ^ side)

    weights = [
        in_gain[None],
        mult_gain[None],
        att_gain[None],
        w_right,
        w_left,
        w_mult_gate,
        w_mult_out,
        w_att,
        w_pair_bias.T,
        w_att_out,
        held,
    ]
    live, crossing, keep, far_crossing, far_keep, in_g, mult_g, att_g, w_r, w_l, w_g, w_m, w_a, w_b, w_o, held = call(
        functools.partial(stage_kernel, len(weights)),
        [
            pltpu.with_memory_space_constraint(x, pltpu.HBM)
            for x in (cross_bias, chain_id, res_mask[None], chain_id[None], *weights)
        ],
        [((residues, channels), f32)] + 2 * [((heads * row_count, wide), f32), ((residues // tile, wide), f32)]
        + [(w.shape, w.dtype) for w in weights],
        0.05,
        "stage",
        [
            pltpu.SMEM((heads,), f32),
            pltpu.SMEM((residues,), jnp.int32),
            pltpu.VMEM((1, residues), jnp.int32),
            pltpu.VMEM((1, residues), jnp.int32),
            pltpu.SemaphoreType.DMA((len(weights) + 4,)),
        ],
        space=pltpu.HBM,
    )
    from_far_near = swap(from_far, near)
    from_far_corner = swap(from_far, near ^ side)
    from_far_side = swap(from_far, side)

    sizes = [((pairs, channels), bf16), ((pairs, width), bf16), ((pairs, width), f32), ((pairs, channels), f32)]
    acts, right, left, gate = call(
        functools.partial(early_kernel, spread([0, far, side, near, near ^ side]), row_count),
        [live, in_g, w_r, w_l, w_g, held, from_far, from_side, from_near, from_corner],
        sizes,
        0.05,
        "early_edges",
    )
    late = spread([far ^ near ^ side, far ^ near, far ^ side])
    acts, right, normed = call(
        functools.partial(right_kernel, late, row_count),
        [live, in_g, w_r, from_far_corner, from_far_near, from_far_side, acts, right],
        [*sizes[:2], ((len(late) * block_rows, channels), bf16)],
        0.5,
        "right_edges",
        aliases={6: 0, 7: 1},
    )
    other = swap(right, 1)
    left, gate, near_product = call(
        functools.partial(left_kernel, late, row_count, residues),
        [normed, right, w_l, w_g, left, gate],
        [*sizes[2:], ((own_count * own_count, width), f32)],
        1.5,
        "left_edges",
        scratch=[pltpu.VMEM((pairs, width), f32)],
        aliases={4: 0, 5: 1},
    )
    mid, normed_mid = call(
        functools.partial(product_kernel, row_count, residues),
        [left, other, near_product, gate, acts, jnp.concatenate([in_g, mult_g, att_g], 0), w_m],
        [((pairs, channels), bf16), ((pairs, channels), bf16)],
        2.4,
        "product",
        scratch=[pltpu.VMEM((pairs, width), f32), pltpu.VMEM((pairs, width), f32)],
    )
    normed_other = swap(normed_mid, 1)
    groups, asked_rows = residues // tile, heads * row_count * tile
    asked, gate_att, top, total, context = call(
        functools.partial(near_attend_kernel, row_count, residues),
        [normed_mid, w_a, w_b, crossing, keep],
        [((groups, asked_rows, channels), bf16), ((block_rows, w_o.shape[0]), f32)]
        + 3 * [((groups, asked_rows, channels), f32)],
        1.2,
        "near_attend",
        scratch=[pltpu.VMEM((own_count, residues, channels), f32)],
    )
    (out,) = call(
        functools.partial(attend_kernel, row_count),
        [normed_other, mid, asked, gate_att, top, total, context, far_crossing, far_keep, w_a, w_b, w_o],
        [((row_count, residues, channels), bf16)],
        1.5,
        "attend",
        scratch=[pltpu.VMEM((own_count, residues, channels), f32)],
    )
    return out


def solution(mesh):
    placed = (
        P(("groups", "row"), None, None),
        P("groups"),
        P("groups"),
        P(),
        P(),
        P(),
        P(),
        P(),
        P(),
        P(),
        P(),
        P(),
        P(),
        P(),
    )
    row_devices = mesh.shape["row"]

    def whole(pair_acts, *others):
        row_count, residues, channels = pair_acts.shape
        in_vmem = 4 * residues * residues * channels <= vmem_share
        paired = row_devices % 16 == 0 and row_devices & (row_devices - 1) == 0 and residues % 8 == 0
        if in_vmem and paired:
            return gathered(row_devices, pair_acts, *others)
        return shards(pair_acts, *others)

    return jax.shard_map(
        whole,
        mesh=mesh,
        in_specs=placed,
        out_specs=P(("groups", "row"), None, None),
        check_vma=False,
    )
```

```python
import functools

import jax
import jax.numpy as jnp
from jax import lax
from jax.experimental import pallas as pl
from jax.experimental.pallas import tpu as pltpu
from jax.sharding import PartitionSpec as P

norm_eps = 1e-05
vmem_share = 4 * 2**20


def layer_norm(tensor, norm_axis):
    tensor = tensor.astype(jnp.float32)
    average = jnp.mean(tensor, axis=norm_axis, keepdims=True)
    spread = jnp.mean(jnp.square(tensor - average), axis=norm_axis, keepdims=True)
    return (tensor - average) * lax.rsqrt(spread + norm_eps)


def edges_of(normed, weight, row_mask, mult_width):
    gate_part = jnp.einsum(
        "ikc,cm->mik", normed, weight[:, :mult_width], preferred_element_type=jnp.float32
    )
    value_part = jnp.einsum(
        "ikc,cm->mik", normed, weight[:, mult_width:], preferred_element_type=jnp.float32
    )
    return (row_mask[None] * jax.nn.sigmoid(gate_part) * value_part).astype(jnp.bfloat16)


def attend(normed_cols, bias_table, mask_float, chain_id, cross_bias, w_att, first_col):
    residues, col_count, _ = normed_cols.shape
    inner_dim = w_att.shape[1] // 4
    head_count = cross_bias.shape[0]
    head_dim = inner_dim // head_count

    def project(slot_idx):
        return jnp.einsum(
            "ijc,ce->ije",
            normed_cols,
            w_att[:, slot_idx * inner_dim : (slot_idx + 1) * inner_dim],
            preferred_element_type=jnp.float32,
        )

    query_all = (
        (project(0) * head_dim ** (-0.5))
        .astype(jnp.bfloat16)
        .reshape(residues, col_count, head_count, head_dim)
    )
    key_all = project(1).astype(jnp.bfloat16).reshape(residues, col_count, head_count, head_dim)
    value_all = project(2).astype(jnp.bfloat16).reshape(residues, col_count, head_count, head_dim)
    gate_att = jax.nn.sigmoid(project(3))
    crossing = (chain_id[:, None] != chain_id[None, :]).astype(jnp.float32)
    half_rows = residues // 2

    def column(col_index):
        query = lax.dynamic_index_in_dim(query_all, col_index, 1, keepdims=False)
        key_col = lax.dynamic_index_in_dim(key_all, col_index, 1, keepdims=False)
        value_col = lax.dynamic_index_in_dim(value_all, col_index, 1, keepdims=False)
        own_live = lax.dynamic_index_in_dim(mask_float, first_col + col_index, 0, keepdims=False)
        key_live = mask_float * own_live > 0
        pieces_out = []
        for block_idx in range(2):
            lower_row = block_idx * half_rows
            query_block = query[lower_row : lower_row + half_rows]
            scores = jnp.einsum(
                "ihd,khd->hki", query_block, key_col, preferred_element_type=jnp.float32
            )
            scores = scores + (
                bias_table[:, :, lower_row : lower_row + half_rows].astype(jnp.float32)
                + cross_bias[:, None, None] * crossing[None, :, lower_row : lower_row + half_rows]
            )
            scores = jnp.where(key_live[None, :, None], scores, -1000000000.0)
            weights = jax.nn.softmax(scores, axis=1).astype(jnp.bfloat16)
            pieces_out.append(
                jnp.einsum("hki,khd->ihd", weights, value_col, preferred_element_type=jnp.float32)
            )
        return jnp.concatenate(pieces_out, 0)

    outputs = lax.map(column, jnp.arange(col_count, dtype=jnp.int32))
    outputs = jnp.transpose(outputs, (1, 0, 2, 3)).reshape(residues, col_count, inner_dim)
    return (outputs * gate_att).astype(jnp.bfloat16)


def shards(
    pair_acts,
    res_mask,
    chain_id,
    in_gain,
    w_left,
    w_right,
    w_mult_gate,
    mult_gain,
    w_mult_out,
    att_gain,
    w_att,
    w_pair_bias,
    cross_bias,
    w_att_out,
):
    row_count = pair_acts.shape[0]
    mult_width = w_left.shape[1] // 2
    first_row = lax.axis_index("row") * row_count
    mask_float = res_mask.astype(jnp.float32)
    own_mask = lax.dynamic_slice_in_dim(mask_float, first_row, row_count)
    row_mask = own_mask[:, None] * mask_float[None, :]
    normed = (layer_norm(pair_acts, -1) * in_gain).astype(jnp.bfloat16)
    left_edges = edges_of(normed, w_left, row_mask, mult_width)
    right_edges = edges_of(normed, w_right, row_mask, mult_width)
    left_chan, right_chan = (
        lax.all_to_all(left_edges, "row", split_axis=0, concat_axis=1, tiled=True),
        lax.all_to_all(right_edges, "row", split_axis=0, concat_axis=1, tiled=True),
    )
    product = jnp.einsum(
        "cik,cjk->cij", left_chan, right_chan, preferred_element_type=jnp.float32
    ).astype(jnp.bfloat16)
    product_own = lax.all_to_all(product, "row", split_axis=1, concat_axis=0, tiled=True)
    product_norm = (layer_norm(product_own, 0) * mult_gain[:, None, None]).astype(jnp.bfloat16)
    gate_mult = jax.nn.sigmoid(
        jnp.einsum("ijc,cd->ijd", normed, w_mult_gate, preferred_element_type=jnp.float32)
    )
    update = jnp.einsum("mij,mc->ijc", product_norm, w_mult_out, preferred_element_type=jnp.float32)
    pair_mid = (pair_acts.astype(jnp.float32) + gate_mult * update).astype(jnp.bfloat16)
    normed_mid = (layer_norm(pair_mid, -1) * att_gain).astype(jnp.bfloat16)
    bias_piece = jnp.einsum(
        "kic,ch->hki", normed_mid, w_pair_bias, preferred_element_type=jnp.float32
    ).astype(jnp.bfloat16)
    bias_table = lax.all_gather(bias_piece, "row", axis=1, tiled=True)
    normed_cols = lax.all_to_all(normed_mid, "row", split_axis=1, concat_axis=0, tiled=True)
    gated = attend(normed_cols, bias_table, mask_float, chain_id, cross_bias, w_att, first_row)
    gated_rows = lax.all_to_all(gated, "row", split_axis=0, concat_axis=1, tiled=True)
    pair_out = pair_mid.astype(jnp.float32) + jnp.einsum(
        "ije,ec->ijc", gated_rows, w_att_out, preferred_element_type=jnp.float32
    )
    return pair_out.astype(jnp.bfloat16)


def dot(a, b):
    return jnp.dot(a, b, preferred_element_type=jnp.float32)


def dot_t(a, b):
    return lax.dot_general(a, b, (((1,), (1,)), ((), ())), preferred_element_type=jnp.float32)


def sigmoid(x):
    return 0.5 * jnp.tanh(0.5 * x) + 0.5


def norm_rows(x, gain):
    average = jnp.mean(x, axis=-1, keepdims=True)
    centred = x - average
    spread = jnp.mean(centred * centred, axis=-1, keepdims=True)
    return centred * lax.rsqrt(spread + norm_eps) * gain


def norm_all(pieces, gain):
    width = pieces[0].shape[-1]
    ones = jnp.ones((width, width), jnp.bfloat16)
    sums = [dot(x, ones) for x in pieces]
    centred = [x.astype(jnp.float32) - s * (1.0 / width) for x, s in zip(pieces, sums, strict=True)]
    spreads = [jnp.mean(c * c, axis=-1, keepdims=True) for c in centred]
    return [
        (c * lax.rsqrt(s + norm_eps) * gain).astype(jnp.bfloat16) for c, s in zip(centred, spreads, strict=True)
    ]


def gated_edges(normed, weight):
    both = dot(normed, weight)
    width = both.shape[1] // 2
    return (sigmoid(both[:, :width]) * both[:, width:]).astype(jnp.bfloat16)


def odd_bits(number):
    return bin(number).count("1") % 2


def parity(number):
    bits = lax.axis_size("row").bit_length() - 1
    return functools.reduce(jnp.bitwise_xor, [number >> b for b in range(bits)]) & 1


def own_side():
    return parity(lax.axis_index("row"))


def stage_kernel(copied, *refs):
    sources, refs = refs[: copied + 4], refs[copied + 4 :]
    (live_ref, *half_refs), copies = refs[:5], refs[5 : copied + 5]
    *early, done = refs[copied + 5 :]
    cross_ref, chain_ref, mask_row_ref, chain_row_ref = early
    moves = [
        pltpu.make_async_copy(source, target, done.at[at])
        for at, (source, target) in enumerate(zip(sources, (*early, *copies), strict=True))
    ]
    for move in moves:
        move.start()
    for move in moves[: len(early)]:
        move.wait()
    residues = live_ref.shape[0]
    blocks, wide = half_refs[1].shape
    tile = 2 * wide // residues
    heads = cross_ref.shape[0]
    row_count = half_refs[0].shape[0] // heads
    mask_row = mask_row_ref[...].astype(jnp.float32)
    chain_row = chain_row_ref[...].astype(jnp.float32)

    line = lax.broadcasted_iota(jnp.int32, (residues, residues), 0)
    spot = lax.broadcasted_iota(jnp.int32, (residues, residues), 1)
    diagonal = jnp.where(line == spot, mask_row, 0.0)
    live_ref[...] = dot(diagonal, jnp.ones((residues, live_ref.shape[1]), jnp.float32))

    line = lax.broadcasted_iota(jnp.int32, (residues, wide), 0)
    lane = lax.broadcasted_iota(jnp.int32, (residues, wide), 1)
    by_column = (lane % tile == line % tile).astype(jnp.float32)
    local = lane // tile
    chip = local // row_count
    block = lax.broadcasted_iota(jnp.int32, (blocks, residues), 0)
    spot = lax.broadcasted_iota(jnp.int32, (blocks, residues), 1)
    column_mask = dot(jnp.where(spot // tile == block, mask_row, 0.0), by_column)
    first = lax.axis_index("row") * row_count
    for half, side in enumerate((own_side(), 1 - own_side())):
        key = (2 * chip + jnp.bitwise_xor(parity(chip), side)) * row_count + local % row_count
        by_key = (key == line).astype(jnp.float32)
        crossing_ref, keep_ref = half_refs[2 * half : 2 * half + 2]
        keep_ref[...] = column_mask * dot(mask_row, by_key)
        chain_wide = dot(chain_row, by_key)
        for i in range(row_count):
            crossing = (chain_wide != chain_ref[first + i].astype(jnp.float32)).astype(jnp.float32)
            for h in range(heads):
                crossing_ref[h * row_count + i : h * row_count + i + 1, :] = cross_ref[h] * crossing
    for move in moves[len(early) :]:
        move.wait()


def spot_of(block_rows, place):
    return pl.ds(pl.multiple_of(place * block_rows, block_rows), block_rows)


def take_blocks(pieces, offsets, row_count, residues, live_ref, gain_ref):
    me = lax.axis_index("row")
    block_rows = row_count * residues
    blocks = [(ref, at) for ref in pieces for at in range(ref.shape[0] // row_count)]
    for (ref, at), offset in zip(blocks, offsets, strict=True):
        device = jnp.bitwise_xor(me, offset)
        acts = ref[at * row_count : (at + 1) * row_count]
        normed = norm_rows(acts.astype(jnp.float32), gain_ref[0:1])
        live_all = live_ref[...]
        rows = [normed[r] * (live_all * live_ref[pl.ds(device * row_count + r, 1), :]) for r in range(row_count)]
        normed = jnp.concatenate(rows, 0).astype(jnp.bfloat16)
        yield spot_of(block_rows, device // 2), acts.reshape(block_rows, acts.shape[-1]), normed


def early_kernel(offsets, row_count, live_ref, gain_ref, w_right_ref, w_left_ref, w_gate_ref, *refs):
    pieces, (acts_ref, right_ref, left_ref, gate_ref) = refs[:-4], refs[-4:]
    residues = live_ref.shape[0]
    for spot, acts, normed in take_blocks(pieces, offsets, row_count, residues, live_ref, gain_ref):
        acts_ref[spot] = acts
        right_ref[spot] = gated_edges(normed, w_right_ref[...])
        left_ref[spot] = gated_edges(normed, w_left_ref[...]).astype(jnp.float32)
        gate_ref[spot] = sigmoid(dot(normed, w_gate_ref[...]))


def right_kernel(offsets, row_count, live_ref, gain_ref, w_right_ref, *refs):
    pieces, (_, _, acts_ref, right_ref, normed_ref) = refs[:-5], refs[-5:]
    residues = live_ref.shape[0]
    block_rows = row_count * residues
    blocks = take_blocks(pieces, offsets, row_count, residues, live_ref, gain_ref)
    for t, (spot, acts, normed) in enumerate(blocks):
        acts_ref[spot] = acts
        right_ref[spot] = gated_edges(normed, w_right_ref[...])
        normed_ref[t * block_rows : (t + 1) * block_rows] = normed


def turn(source, turned_ref, row_count, residues):
    chips = source.shape[0] // (row_count * residues)
    own_count = chips * row_count
    for chip in range(chips):
        for r in range(row_count):
            lower = (chip * row_count + r) * residues
            turned_ref[pl.ds(r * chips + chip, residues, stride=own_count), :] = source[
                lower : lower + residues
            ].astype(jnp.float32)


def multiply(left_ref, turned_ref, residues, store):
    row_block, tile = 8, 8
    count = turned_ref.shape[0] // residues
    own_count = left_ref.shape[0] // residues
    tiles = count // tile

    def rows_of(block, carry):
        first = block * row_block

        def add(k, totals):
            ahead = [
                turned_ref[pl.ds(pl.multiple_of(k * count + t * tile, tile), tile), :] for t in range(tiles)
            ]
            out = []
            for a in range(row_block):
                one = left_ref[pl.ds((first + a) * residues + k, 1), :]
                out.extend(totals[a * tiles + t] + one * ahead[t] for t in range(tiles))
            return tuple(out)

        zeros = tuple(jnp.zeros((tile, left_ref.shape[1]), jnp.float32) for _ in range(row_block * tiles))
        totals = lax.fori_loop(0, residues, add, zeros, unroll=16)
        for a in range(row_block):
            for t in range(tiles):
                store(first + a, t, totals[a * tiles + t])
        return carry

    lax.fori_loop(0, own_count // row_block, rows_of, 0)


def left_kernel(late, row_count, residues, *refs):
    *normed_refs, right_ref, w_left_ref, w_gate_ref, _, _, left_ref, gate_ref, near_ref, turned_ref = refs
    me = lax.axis_index("row")
    block_rows = row_count * residues
    for offsets, normed_ref in zip(late, normed_refs, strict=True):
        for t, offset in enumerate(offsets):
            spot = spot_of(block_rows, jnp.bitwise_xor(me, offset) // 2)
            normed = normed_ref[t * block_rows : (t + 1) * block_rows]
            left_ref[spot] = gated_edges(normed, w_left_ref[...]).astype(jnp.float32)
            gate_ref[spot] = sigmoid(dot(normed, w_gate_ref[...]))
    turn(right_ref, turned_ref, row_count, residues)
    count = turned_ref.shape[0] // residues

    def store(i, t, values):
        near_ref[pl.ds(pl.multiple_of(i * count + t * 8, 8), 8), :] = values

    multiply(left_ref, turned_ref, residues, store)


def product_kernel(
    row_count,
    residues,
    left_ref,
    other_ref,
    near_ref,
    gate_ref,
    acts_ref,
    gain_ref,
    w_out_ref,
    mid_ref,
    normed_mid_ref,
    turned_ref,
    product_ref,
):
    core = own_side()
    turn(other_ref, turned_ref, row_count, residues)
    count = turned_ref.shape[0] // residues
    chips = count // row_count
    part = chips // 8

    line = lax.broadcasted_iota(jnp.int32, (8, 1), 0)
    odd_line = (line ^ (line >> 1) ^ (line >> 2)) & 1

    def store(i, t, values):
        r, eighth = t // part, t % part
        near = near_ref[pl.ds(pl.multiple_of(i * count + t * 8, 8), 8), :]
        near_first = odd_line == (core ^ odd_bits(eighth))
        for side, rows in ((0, jnp.where(near_first, near, values)), (1, jnp.where(near_first, values, near))):
            start = i * residues + (eighth * 16 + side) * row_count + r
            product_ref[pl.ds(start, 8, stride=2 * row_count), :] = rows

    multiply(left_ref, turned_ref, residues, store)

    step = 2 * row_count * residues
    spots = [slice(lower, lower + step) for lower in range(0, acts_ref.shape[0], step)]
    normed = norm_all([product_ref[at].astype(jnp.bfloat16) for at in spots], gain_ref[1:2])
    updates = [gate_ref[at] * dot(rows, w_out_ref[...]) for at, rows in zip(spots, normed, strict=True)]
    mids = [
        (acts_ref[at].astype(jnp.float32) + update).astype(jnp.bfloat16)
        for at, update in zip(spots, updates, strict=True)
    ]
    for at, mid in zip(spots, mids, strict=True):
        mid_ref[at] = mid
    for at, rows in zip(spots, norm_all(mids, gain_ref[2:3]), strict=True):
        normed_mid_ref[at] = rows


def half_attention(rows_ref, pair_ref, asked, w_bias, crossing_ref, keep_ref):
    count, residues, channels = pair_ref.shape
    heads = w_bias.shape[0]
    row_count = crossing_ref.shape[0] // heads
    tile = 8
    wide = count * tile
    for local in range(count):
        pair_ref[local] = rows_ref[local * residues : (local + 1) * residues].astype(jnp.float32)
    first = lax.axis_index("row") * row_count
    pieces = []
    for i in range(row_count):
        column = pair_ref[:, pl.ds(first + i, 1), :]
        spread = jnp.broadcast_to(column, (count, tile, channels)).reshape(wide, channels)
        pieces.append(dot_t(w_bias, spread.astype(jnp.bfloat16)).astype(jnp.bfloat16).astype(jnp.float32))
    extra = jnp.concatenate(
        [
            jnp.broadcast_to(pieces[i][h : h + 1] + crossing_ref[h * row_count + i : h * row_count + i + 1], (tile, wide))
            for h in range(heads)
            for i in range(row_count)
        ],
        0,
    )
    shape = extra.shape
    same = lax.broadcasted_iota(jnp.int32, shape, 0) % tile == lax.broadcasted_iota(jnp.int32, shape, 1) % tile
    low = jnp.where(same, -1000000000.0, -1e30)
    groups = range(residues // tile)
    keys = [
        pair_ref[:, g * tile : (g + 1) * tile, :].reshape(wide, channels).astype(jnp.bfloat16) for g in groups
    ]
    scores = [dot_t(asked[g], keys[g]) for g in groups]
    scores = [
        jnp.where(jnp.logical_and(same, keep_ref[g : g + 1, :] > 0), scores[g] + extra, low) for g in groups
    ]
    return scores, keys


def near_attend_kernel(
    row_count, residues, own_ref, w_att_ref, w_bias_ref, crossing_ref, keep_ref, asked_ref, gate_ref, top_ref, total_ref, context_ref, pair_ref
):
    block_rows = row_count * residues
    heads = w_bias_ref.shape[0]
    inner = w_att_ref.shape[1] // 4
    head_dim = inner // heads
    tile = 8
    groups = range(residues // tile)
    mine = own_ref[spot_of(block_rows, lax.axis_index("row") // 2)]
    query = (dot(mine, w_att_ref[:, :inner]) * head_dim ** (-0.5)).astype(jnp.bfloat16)
    gate_ref[...] = sigmoid(dot(mine, w_att_ref[:, 3 * inner :]))
    head_of = lax.broadcasted_iota(jnp.int32, (1, inner), 1) // head_dim
    w_key = w_att_ref[:, inner : 2 * inner]
    w_key = jnp.concatenate([jnp.where(head_of == h, w_key, 0) for h in range(heads)], 0)
    by_head = jnp.split(dot_t(query, w_key), heads, 1)
    asked = [
        jnp.concatenate(
            [
                by_head[h][i * residues + g * tile : i * residues + (g + 1) * tile]
                for h in range(heads)
                for i in range(row_count)
            ],
            0,
        ).astype(jnp.bfloat16)
        for g in groups
    ]
    for g in groups:
        asked_ref[g] = asked[g]
    scores, keys = half_attention(own_ref, pair_ref, asked, w_bias_ref[...], crossing_ref, keep_ref)
    tops = [jnp.max(s, axis=-1, keepdims=True) for s in scores]
    scores = [jnp.exp(s - top) for s, top in zip(scores, tops, strict=True)]
    totals = [jnp.sum(s, axis=-1, keepdims=True) for s in scores]
    for g in groups:
        context_ref[g] = dot(scores[g].astype(jnp.bfloat16), keys[g])
        top_ref[g] = jnp.broadcast_to(tops[g], top_ref.shape[1:])
        total_ref[g] = jnp.broadcast_to(totals[g], total_ref.shape[1:])


def attend_kernel(
    row_count,
    other_ref,
    mid_ref,
    asked_ref,
    gate_ref,
    top_ref,
    total_ref,
    context_ref,
    crossing_ref,
    keep_ref,
    w_att_ref,
    w_bias_ref,
    w_out_ref,
    out_ref,
    pair_ref,
):
    residues = pair_ref.shape[1]
    heads = w_bias_ref.shape[0]
    inner = w_out_ref.shape[0]
    head_dim = inner // heads
    block_rows = row_count * residues
    tile = 8
    groups = range(residues // tile)
    asked = [asked_ref[g] for g in groups]
    scores, keys = half_attention(other_ref, pair_ref, asked, w_bias_ref[...], crossing_ref, keep_ref)
    tops = [jnp.maximum(jnp.max(scores[g], axis=-1, keepdims=True), top_ref[g]) for g in groups]
    scales = [jnp.exp(top_ref[g] - tops[g]) for g in groups]
    copies = pl.cdiv(scores[0].shape[1], tops[0].shape[1])
    scores = [jnp.exp(s - jnp.concatenate([top] * copies, 1)[:, : s.shape[1]]) for s, top in zip(scores, tops, strict=True)]
    totals = [jnp.sum(scores[g], axis=-1, keepdims=True) + total_ref[g] * scales[g] for g in groups]
    context = [dot(scores[g].astype(jnp.bfloat16), keys[g]) + context_ref[g] * scales[g] for g in groups]
    context = [context[g] * (1.0 / totals[g]) for g in groups]

    head_of = lax.broadcasted_iota(jnp.int32, (1, inner), 1) // head_dim
    by_head = [
        jnp.concatenate(
            [
                context[g][(h * row_count + i) * tile : (h * row_count + i + 1) * tile]
                for i in range(row_count)
                for g in groups
            ],
            0,
        ).astype(jnp.bfloat16)
        for h in range(heads)
    ]
    w_value = w_att_ref[:, 2 * inner : 3 * inner]
    w_value = jnp.concatenate([jnp.where(head_of == h, w_value, 0) for h in range(heads)], 0)
    values = dot(jnp.concatenate(by_head, 1), w_value)
    gated = (values * gate_ref[...]).astype(jnp.bfloat16)
    mid = mid_ref[spot_of(block_rows, lax.axis_index("row") // 2)].astype(jnp.float32)
    out_ref[...] = (mid + dot(gated, w_out_ref[...])).astype(jnp.bfloat16).reshape(out_ref.shape)


def call(body, args, outs, cost_us, name, scratch=(), aliases=None, space=pltpu.VMEM):
    return pl.pallas_call(
        body,
        out_shape=[jax.ShapeDtypeStruct(shape, dtype) for shape, dtype in outs],
        in_specs=[pl.BlockSpec(memory_space=space)] * len(args),
        out_specs=[pl.BlockSpec(memory_space=pltpu.VMEM)] * len(outs),
        scratch_shapes=list(scratch),
        input_output_aliases=aliases or {},
        compiler_params=pltpu.CompilerParams(vmem_limit_bytes=24 * 2**20),
        cost_estimate=pl.CostEstimate(flops=int(cost_us * 1e9), bytes_accessed=2**18, transcendentals=0),
        name=name,
    )(*args)


def gathered(
    row_devices,
    pair_acts,
    res_mask,
    chain_id,
    in_gain,
    w_left,
    w_right,
    w_mult_gate,
    mult_gain,
    w_mult_out,
    att_gain,
    w_att,
    w_pair_bias,
    cross_bias,
    w_att_out,
):
    row_count, residues, channels = pair_acts.shape
    width = w_left.shape[1] // 2
    heads = w_pair_bias.shape[1]
    own_count = residues // 2
    pairs = own_count * residues
    block_rows = row_count * residues
    tile = 8
    wide = own_count * tile
    bf16, f32 = jnp.bfloat16, jnp.float32

    def swap(x, shift):
        return lax.ppermute(x, "row", [(i, i ^ shift) for i in range(row_devices)])

    base, held = [0], pair_acts
    far, near, side = 9, 5, 3

    def spread(shifts):
        return [o ^ s for s in shifts for o in base]

    shift = row_devices // 2
    while shift > far:
        held = jnp.concatenate([held, swap(held, shift + 1)], 0)
        base = base + [o ^ (shift + 1) for o in base]
        shift //= 2
    from_far = swap(held, far)
    from_side = swap(held, side)
    from_near = swap(held, near)
    from_corner = swap(held, near ^ side)

    weights = [
        in_gain[None],
        mult_gain[None],
        att_gain[None],
        w_right,
        w_left,
        w_mult_gate,
        w_mult_out,
        w_att,
        w_pair_bias.T,
        w_att_out,
        held,
    ]
    live, crossing, keep, far_crossing, far_keep, in_g, mult_g, att_g, w_r, w_l, w_g, w_m, w_a, w_b, w_o, held = call(
        functools.partial(stage_kernel, len(weights)),
        [
            pltpu.with_memory_space_constraint(x, pltpu.HBM)
            for x in (cross_bias, chain_id, res_mask[None], chain_id[None], *weights)
        ],
        [((residues, channels), f32)] + 2 * [((heads * row_count, wide), f32), ((residues // tile, wide), f32)]
        + [(w.shape, w.dtype) for w in weights],
        0.05,
        "stage",
        [
            pltpu.SMEM((heads,), f32),
            pltpu.SMEM((residues,), jnp.int32),
            pltpu.VMEM((1, residues), jnp.int32),
            pltpu.VMEM((1, residues), jnp.int32),
            pltpu.SemaphoreType.DMA((len(weights) + 4,)),
        ],
        space=pltpu.HBM,
    )
    from_far_near = swap(from_far, near)
    from_far_corner = swap(from_far, near ^ side)
    from_far_side = swap(from_far, side)

    sizes = [((pairs, channels), bf16), ((pairs, width), bf16), ((pairs, width), f32), ((pairs, channels), f32)]
    acts, right, left, gate = call(
        functools.partial(early_kernel, spread([0, far, side, near, near ^ side]), row_count),
        [live, in_g, w_r, w_l, w_g, held, from_far, from_side, from_near, from_corner],
        sizes,
        0.05,
        "early_edges",
    )
    late = [spread([far ^ near ^ side, far ^ near]), spread([far ^ side])]
    normed = []
    for offsets, pieces in zip(late, ([from_far_corner, from_far_near], [from_far_side]), strict=True):
        acts, right, rows = call(
            functools.partial(right_kernel, offsets, row_count),
            [live, in_g, w_r, *pieces, acts, right],
            [*sizes[:2], ((len(offsets) * block_rows, channels), bf16)],
            0.05,
            "right_edges",
            aliases={3 + len(pieces): 0, 4 + len(pieces): 1},
        )
        normed.append(rows)
    other = swap(right, 1)
    left, gate, near_product = call(
        functools.partial(left_kernel, late, row_count, residues),
        [*normed, right, w_l, w_g, left, gate],
        [*sizes[2:], ((own_count * own_count, width), f32)],
        1.5,
        "left_edges",
        scratch=[pltpu.VMEM((pairs, width), f32)],
        aliases={3 + len(normed): 0, 4 + len(normed): 1},
    )
    mid, normed_mid = call(
        functools.partial(product_kernel, row_count, residues),
        [left, other, near_product, gate, acts, jnp.concatenate([in_g, mult_g, att_g], 0), w_m],
        [((pairs, channels), bf16), ((pairs, channels), bf16)],
        2.4,
        "product",
        scratch=[pltpu.VMEM((pairs, width), f32), pltpu.VMEM((pairs, width), f32)],
    )
    normed_other = swap(normed_mid, 1)
    groups, asked_rows = residues // tile, heads * row_count * tile
    asked, gate_att, top, total, context = call(
        functools.partial(near_attend_kernel, row_count, residues),
        [normed_mid, w_a, w_b, crossing, keep],
        [((groups, asked_rows, channels), bf16), ((block_rows, w_o.shape[0]), f32)]
        + 3 * [((groups, asked_rows, channels), f32)],
        1.2,
        "near_attend",
        scratch=[pltpu.VMEM((own_count, residues, channels), f32)],
    )
    (out,) = call(
        functools.partial(attend_kernel, row_count),
        [normed_other, mid, asked, gate_att, top, total, context, far_crossing, far_keep, w_a, w_b, w_o],
        [((row_count, residues, channels), bf16)],
        1.5,
        "attend",
        scratch=[pltpu.VMEM((own_count, residues, channels), f32)],
    )
    return out


def solution(mesh):
    placed = (
        P(("groups", "row"), None, None),
        P("groups"),
        P("groups"),
        P(),
        P(),
        P(),
        P(),
        P(),
        P(),
        P(),
        P(),
        P(),
        P(),
        P(),
    )
    row_devices = mesh.shape["row"]

    def whole(pair_acts, *others):
        row_count, residues, channels = pair_acts.shape
        in_vmem = 4 * residues * residues * channels <= vmem_share
        paired = row_devices % 16 == 0 and row_devices & (row_devices - 1) == 0 and residues % 8 == 0
        if in_vmem and paired:
            return gathered(row_devices, pair_acts, *others)
        return shards(pair_acts, *others)

    return jax.shard_map(
        whole,
        mesh=mesh,
        in_specs=placed,
        out_specs=P(("groups", "row"), None, None),
        check_vma=False,
    )
```

```python
import functools

import jax
import jax.numpy as jnp
from jax import lax
from jax.experimental import pallas as pl
from jax.experimental.pallas import tpu as pltpu
from jax.sharding import PartitionSpec as P

norm_eps = 1e-05
vmem_share = 4 * 2**20


def layer_norm(tensor, norm_axis):
    tensor = tensor.astype(jnp.float32)
    average = jnp.mean(tensor, axis=norm_axis, keepdims=True)
    spread = jnp.mean(jnp.square(tensor - average), axis=norm_axis, keepdims=True)
    return (tensor - average) * lax.rsqrt(spread + norm_eps)


def edges_of(normed, weight, row_mask, mult_width):
    gate_part = jnp.einsum(
        "ikc,cm->mik", normed, weight[:, :mult_width], preferred_element_type=jnp.float32
    )
    value_part = jnp.einsum(
        "ikc,cm->mik", normed, weight[:, mult_width:], preferred_element_type=jnp.float32
    )
    return (row_mask[None] * jax.nn.sigmoid(gate_part) * value_part).astype(jnp.bfloat16)


def attend(normed_cols, bias_table, mask_float, chain_id, cross_bias, w_att, first_col):
    residues, col_count, _ = normed_cols.shape
    inner_dim = w_att.shape[1] // 4
    head_count = cross_bias.shape[0]
    head_dim = inner_dim // head_count

    def project(slot_idx):
        return jnp.einsum(
            "ijc,ce->ije",
            normed_cols,
            w_att[:, slot_idx * inner_dim : (slot_idx + 1) * inner_dim],
            preferred_element_type=jnp.float32,
        )

    query_all = (
        (project(0) * head_dim ** (-0.5))
        .astype(jnp.bfloat16)
        .reshape(residues, col_count, head_count, head_dim)
    )
    key_all = project(1).astype(jnp.bfloat16).reshape(residues, col_count, head_count, head_dim)
    value_all = project(2).astype(jnp.bfloat16).reshape(residues, col_count, head_count, head_dim)
    gate_att = jax.nn.sigmoid(project(3))
    crossing = (chain_id[:, None] != chain_id[None, :]).astype(jnp.float32)
    half_rows = residues // 2

    def column(col_index):
        query = lax.dynamic_index_in_dim(query_all, col_index, 1, keepdims=False)
        key_col = lax.dynamic_index_in_dim(key_all, col_index, 1, keepdims=False)
        value_col = lax.dynamic_index_in_dim(value_all, col_index, 1, keepdims=False)
        own_live = lax.dynamic_index_in_dim(mask_float, first_col + col_index, 0, keepdims=False)
        key_live = mask_float * own_live > 0
        pieces_out = []
        for block_idx in range(2):
            lower_row = block_idx * half_rows
            query_block = query[lower_row : lower_row + half_rows]
            scores = jnp.einsum(
                "ihd,khd->hki", query_block, key_col, preferred_element_type=jnp.float32
            )
            scores = scores + (
                bias_table[:, :, lower_row : lower_row + half_rows].astype(jnp.float32)
                + cross_bias[:, None, None] * crossing[None, :, lower_row : lower_row + half_rows]
            )
            scores = jnp.where(key_live[None, :, None], scores, -1000000000.0)
            weights = jax.nn.softmax(scores, axis=1).astype(jnp.bfloat16)
            pieces_out.append(
                jnp.einsum("hki,khd->ihd", weights, value_col, preferred_element_type=jnp.float32)
            )
        return jnp.concatenate(pieces_out, 0)

    outputs = lax.map(column, jnp.arange(col_count, dtype=jnp.int32))
    outputs = jnp.transpose(outputs, (1, 0, 2, 3)).reshape(residues, col_count, inner_dim)
    return (outputs * gate_att).astype(jnp.bfloat16)


def shards(
    pair_acts,
    res_mask,
    chain_id,
    in_gain,
    w_left,
    w_right,
    w_mult_gate,
    mult_gain,
    w_mult_out,
    att_gain,
    w_att,
    w_pair_bias,
    cross_bias,
    w_att_out,
):
    row_count = pair_acts.shape[0]
    mult_width = w_left.shape[1] // 2
    first_row = lax.axis_index("row") * row_count
    mask_float = res_mask.astype(jnp.float32)
    own_mask = lax.dynamic_slice_in_dim(mask_float, first_row, row_count)
    row_mask = own_mask[:, None] * mask_float[None, :]
    normed = (layer_norm(pair_acts, -1) * in_gain).astype(jnp.bfloat16)
    left_edges = edges_of(normed, w_left, row_mask, mult_width)
    right_edges = edges_of(normed, w_right, row_mask, mult_width)
    left_chan, right_chan = (
        lax.all_to_all(left_edges, "row", split_axis=0, concat_axis=1, tiled=True),
        lax.all_to_all(right_edges, "row", split_axis=0, concat_axis=1, tiled=True),
    )
    product = jnp.einsum(
        "cik,cjk->cij", left_chan, right_chan, preferred_element_type=jnp.float32
    ).astype(jnp.bfloat16)
    product_own = lax.all_to_all(product, "row", split_axis=1, concat_axis=0, tiled=True)
    product_norm = (layer_norm(product_own, 0) * mult_gain[:, None, None]).astype(jnp.bfloat16)
    gate_mult = jax.nn.sigmoid(
        jnp.einsum("ijc,cd->ijd", normed, w_mult_gate, preferred_element_type=jnp.float32)
    )
    update = jnp.einsum("mij,mc->ijc", product_norm, w_mult_out, preferred_element_type=jnp.float32)
    pair_mid = (pair_acts.astype(jnp.float32) + gate_mult * update).astype(jnp.bfloat16)
    normed_mid = (layer_norm(pair_mid, -1) * att_gain).astype(jnp.bfloat16)
    bias_piece = jnp.einsum(
        "kic,ch->hki", normed_mid, w_pair_bias, preferred_element_type=jnp.float32
    ).astype(jnp.bfloat16)
    bias_table = lax.all_gather(bias_piece, "row", axis=1, tiled=True)
    normed_cols = lax.all_to_all(normed_mid, "row", split_axis=1, concat_axis=0, tiled=True)
    gated = attend(normed_cols, bias_table, mask_float, chain_id, cross_bias, w_att, first_row)
    gated_rows = lax.all_to_all(gated, "row", split_axis=0, concat_axis=1, tiled=True)
    pair_out = pair_mid.astype(jnp.float32) + jnp.einsum(
        "ije,ec->ijc", gated_rows, w_att_out, preferred_element_type=jnp.float32
    )
    return pair_out.astype(jnp.bfloat16)


def dot(a, b):
    return jnp.dot(a, b, preferred_element_type=jnp.float32)


def dot_t(a, b):
    return lax.dot_general(a, b, (((1,), (1,)), ((), ())), preferred_element_type=jnp.float32)


def sigmoid(x):
    return 0.5 * jnp.tanh(0.5 * x) + 0.5


def norm_rows(x, gain):
    average = jnp.mean(x, axis=-1, keepdims=True)
    centred = x - average
    spread = jnp.mean(centred * centred, axis=-1, keepdims=True)
    return centred * lax.rsqrt(spread + norm_eps) * gain


def norm_all(pieces, gain):
    width = pieces[0].shape[-1]
    ones = jnp.ones((width, width), jnp.bfloat16)
    sums = [dot(x, ones) for x in pieces]
    centred = [x.astype(jnp.float32) - s * (1.0 / width) for x, s in zip(pieces, sums, strict=True)]
    spreads = [jnp.mean(c * c, axis=-1, keepdims=True) for c in centred]
    return [
        (c * lax.rsqrt(s + norm_eps) * gain).astype(jnp.bfloat16) for c, s in zip(centred, spreads, strict=True)
    ]


def gated_edges(normed, weight):
    both = dot(normed, weight)
    width = both.shape[1] // 2
    return (sigmoid(both[:, :width]) * both[:, width:]).astype(jnp.bfloat16)


def odd_bits(number):
    return bin(number).count("1") % 2


def parity(number):
    bits = lax.axis_size("row").bit_length() - 1
    return functools.reduce(jnp.bitwise_xor, [number >> b for b in range(bits)]) & 1


def own_side():
    return parity(lax.axis_index("row"))


def stage_kernel(copied, *refs):
    sources, refs = refs[: copied + 4], refs[copied + 4 :]
    (live_ref, *half_refs), copies = refs[:5], refs[5 : copied + 5]
    *early, done = refs[copied + 5 :]
    cross_ref, chain_ref, mask_row_ref, chain_row_ref = early
    moves = [
        pltpu.make_async_copy(source, target, done.at[at])
        for at, (source, target) in enumerate(zip(sources, (*early, *copies), strict=True))
    ]
    for move in moves:
        move.start()
    for move in moves[: len(early)]:
        move.wait()
    residues = live_ref.shape[0]
    blocks, wide = half_refs[1].shape
    tile = 2 * wide // residues
    heads = cross_ref.shape[0]
    row_count = half_refs[0].shape[0] // heads
    mask_row = mask_row_ref[...].astype(jnp.float32)
    chain_row = chain_row_ref[...].astype(jnp.float32)

    line = lax.broadcasted_iota(jnp.int32, (residues, residues), 0)
    spot = lax.broadcasted_iota(jnp.int32, (residues, residues), 1)
    diagonal = jnp.where(line == spot, mask_row, 0.0)
    live_ref[...] = dot(diagonal, jnp.ones((residues, live_ref.shape[1]), jnp.float32))

    line = lax.broadcasted_iota(jnp.int32, (residues, wide), 0)
    lane = lax.broadcasted_iota(jnp.int32, (residues, wide), 1)
    by_column = (lane % tile == line % tile).astype(jnp.float32)
    local = lane // tile
    chip = local // row_count
    block = lax.broadcasted_iota(jnp.int32, (blocks, residues), 0)
    spot = lax.broadcasted_iota(jnp.int32, (blocks, residues), 1)
    column_mask = dot(jnp.where(spot // tile == block, mask_row, 0.0), by_column)
    first = lax.axis_index("row") * row_count
    for half, side in enumerate((own_side(), 1 - own_side())):
        key = (2 * chip + jnp.bitwise_xor(parity(chip), side)) * row_count + local % row_count
        by_key = (key == line).astype(jnp.float32)
        crossing_ref, keep_ref = half_refs[2 * half : 2 * half + 2]
        keep_ref[...] = column_mask * dot(mask_row, by_key)
        chain_wide = dot(chain_row, by_key)
        for i in range(row_count):
            crossing = (chain_wide != chain_ref[first + i].astype(jnp.float32)).astype(jnp.float32)
            for h in range(heads):
                crossing_ref[h * row_count + i : h * row_count + i + 1, :] = cross_ref[h] * crossing
    for move in moves[len(early) :]:
        move.wait()


def spot_of(block_rows, place):
    return pl.ds(pl.multiple_of(place * block_rows, block_rows), block_rows)


def blocks_of(pieces, row_count):
    return [ref[at : at + row_count] for ref in pieces for at in range(0, ref.shape[0], row_count)]


def masked_norms(pieces, offsets, row_count, live_ref, gain_ref):
    me = lax.axis_index("row")
    for acts, offset in zip(blocks_of(pieces, row_count), offsets, strict=True):
        device = jnp.bitwise_xor(me, offset)
        normed = norm_rows(acts.astype(jnp.float32), gain_ref[0:1])
        live_all = live_ref[...]
        rows = [normed[r] * (live_all * live_ref[pl.ds(device * row_count + r, 1), :]) for r in range(row_count)]
        yield jnp.concatenate(rows, 0).astype(jnp.bfloat16)


def parts_of(ref, count):
    step = ref.shape[0] // count
    return [ref[at : at + step] for at in range(0, ref.shape[0], step)]


def spots_of(offsets, block_rows):
    me = lax.axis_index("row")
    return [spot_of(block_rows, jnp.bitwise_xor(me, offset) // 2) for offset in offsets]


def early_kernel(offsets, row_count, live_ref, gain_ref, w_right_ref, w_left_ref, w_gate_ref, *refs):
    pieces, (right_ref, left_ref, gate_ref) = refs[:-3], refs[-3:]
    block_rows = row_count * live_ref.shape[0]
    for t, normed in enumerate(masked_norms(pieces, offsets, row_count, live_ref, gain_ref)):
        at = slice(t * block_rows, (t + 1) * block_rows)
        right_ref[at] = gated_edges(normed, w_right_ref[...])
        left_ref[at] = gated_edges(normed, w_left_ref[...]).astype(jnp.float32)
        gate_ref[at] = sigmoid(dot(normed, w_gate_ref[...]))


def middle_kernel(offsets, row_count, live_ref, gain_ref, w_right_ref, *refs):
    pieces, (right_ref, normed_ref) = refs[:-2], refs[-2:]
    block_rows = row_count * live_ref.shape[0]
    for t, normed in enumerate(masked_norms(pieces, offsets, row_count, live_ref, gain_ref)):
        at = slice(t * block_rows, (t + 1) * block_rows)
        right_ref[at] = gated_edges(normed, w_right_ref[...])
        normed_ref[at] = normed


def right_kernel(done_offsets, offsets, row_count, live_ref, gain_ref, w_right_ref, *refs):
    done_refs, pieces = refs[: len(done_offsets)], refs[len(done_offsets) : -2]
    right_ref, normed_ref = refs[-2:]
    block_rows = row_count * live_ref.shape[0]
    for ref, held in zip(done_refs, done_offsets, strict=True):
        for spot, edges in zip(spots_of(held, block_rows), parts_of(ref, len(held)), strict=True):
            right_ref[spot] = edges
    normed_blocks = masked_norms(pieces, offsets, row_count, live_ref, gain_ref)
    for t, (spot, normed) in enumerate(zip(spots_of(offsets, block_rows), normed_blocks, strict=True)):
        right_ref[spot] = gated_edges(normed, w_right_ref[...])
        normed_ref[t * block_rows : (t + 1) * block_rows] = normed


def turn(source, turned_ref, row_count, residues):
    chips = source.shape[0] // (row_count * residues)
    own_count = chips * row_count
    for chip in range(chips):
        for r in range(row_count):
            lower = (chip * row_count + r) * residues
            turned_ref[pl.ds(r * chips + chip, residues, stride=own_count), :] = source[
                lower : lower + residues
            ].astype(jnp.float32)


def multiply(left_ref, turned_ref, residues, store):
    row_block, tile = 8, 8
    count = turned_ref.shape[0] // residues
    own_count = left_ref.shape[0] // residues
    tiles = count // tile

    def rows_of(block, carry):
        first = block * row_block

        def add(k, totals):
            ahead = [
                turned_ref[pl.ds(pl.multiple_of(k * count + t * tile, tile), tile), :] for t in range(tiles)
            ]
            out = []
            for a in range(row_block):
                one = left_ref[pl.ds((first + a) * residues + k, 1), :]
                out.extend(totals[a * tiles + t] + one * ahead[t] for t in range(tiles))
            return tuple(out)

        zeros = tuple(jnp.zeros((tile, left_ref.shape[1]), jnp.float32) for _ in range(row_block * tiles))
        totals = lax.fori_loop(0, residues, add, zeros, unroll=16)
        for a in range(row_block):
            for t in range(tiles):
                store(first + a, t, totals[a * tiles + t])
        return carry

    lax.fori_loop(0, own_count // row_block, rows_of, 0)


def left_kernel(early, late, row_count, residues, right_ref, w_left_ref, w_gate_ref, early_left_ref, early_gate_ref, *refs):
    normed_refs, pieces = refs[: len(late)], refs[len(late) : -5]
    left_ref, gate_ref, acts_ref, near_ref, turned_ref = refs[-5:]
    block_rows = row_count * residues
    blocks = zip(
        spots_of(early, block_rows),
        parts_of(early_left_ref, len(early)),
        parts_of(early_gate_ref, len(early)),
        strict=True,
    )
    for spot, edges, gate in blocks:
        left_ref[spot] = edges
        gate_ref[spot] = gate
    for offsets, normed_ref in zip(late, normed_refs, strict=True):
        for spot, normed in zip(spots_of(offsets, block_rows), parts_of(normed_ref, len(offsets)), strict=True):
            left_ref[spot] = gated_edges(normed, w_left_ref[...]).astype(jnp.float32)
            gate_ref[spot] = sigmoid(dot(normed, w_gate_ref[...]))
    order = early + [offset for offsets in late for offset in offsets]
    for spot, acts in zip(spots_of(order, block_rows), blocks_of(pieces, row_count), strict=True):
        acts_ref[spot] = acts.reshape(block_rows, acts.shape[-1])
    turn(right_ref, turned_ref, row_count, residues)
    count = turned_ref.shape[0] // residues

    def store(i, t, values):
        near_ref[pl.ds(pl.multiple_of(i * count + t * 8, 8), 8), :] = values

    multiply(left_ref, turned_ref, residues, store)


def product_kernel(
    row_count,
    residues,
    left_ref,
    other_ref,
    near_ref,
    gate_ref,
    acts_ref,
    gain_ref,
    w_out_ref,
    mid_ref,
    normed_mid_ref,
    turned_ref,
    product_ref,
):
    core = own_side()
    turn(other_ref, turned_ref, row_count, residues)
    count = turned_ref.shape[0] // residues
    chips = count // row_count
    part = chips // 8

    line = lax.broadcasted_iota(jnp.int32, (8, 1), 0)
    odd_line = (line ^ (line >> 1) ^ (line >> 2)) & 1

    def store(i, t, values):
        r, eighth = t // part, t % part
        near = near_ref[pl.ds(pl.multiple_of(i * count + t * 8, 8), 8), :]
        near_first = odd_line == (core ^ odd_bits(eighth))
        for side, rows in ((0, jnp.where(near_first, near, values)), (1, jnp.where(near_first, values, near))):
            start = i * residues + (eighth * 16 + side) * row_count + r
            product_ref[pl.ds(start, 8, stride=2 * row_count), :] = rows

    multiply(left_ref, turned_ref, residues, store)

    step = 2 * row_count * residues
    spots = [slice(lower, lower + step) for lower in range(0, acts_ref.shape[0], step)]
    normed = norm_all([product_ref[at].astype(jnp.bfloat16) for at in spots], gain_ref[1:2])
    updates = [gate_ref[at] * dot(rows, w_out_ref[...]) for at, rows in zip(spots, normed, strict=True)]
    mids = [
        (acts_ref[at].astype(jnp.float32) + update).astype(jnp.bfloat16)
        for at, update in zip(spots, updates, strict=True)
    ]
    for at, mid in zip(spots, mids, strict=True):
        mid_ref[at] = mid
    for at, rows in zip(spots, norm_all(mids, gain_ref[2:3]), strict=True):
        normed_mid_ref[at] = rows


def half_attention(rows_ref, pair_ref, asked, w_bias, crossing_ref, keep_ref):
    count, residues, channels = pair_ref.shape
    heads = w_bias.shape[0]
    row_count = crossing_ref.shape[0] // heads
    tile = 8
    wide = count * tile
    for local in range(count):
        pair_ref[local] = rows_ref[local * residues : (local + 1) * residues].astype(jnp.float32)
    first = lax.axis_index("row") * row_count
    pieces = []
    for i in range(row_count):
        column = pair_ref[:, pl.ds(first + i, 1), :]
        spread = jnp.broadcast_to(column, (count, tile, channels)).reshape(wide, channels)
        pieces.append(dot_t(w_bias, spread.astype(jnp.bfloat16)).astype(jnp.bfloat16).astype(jnp.float32))
    extra = jnp.concatenate(
        [
            jnp.broadcast_to(pieces[i][h : h + 1] + crossing_ref[h * row_count + i : h * row_count + i + 1], (tile, wide))
            for h in range(heads)
            for i in range(row_count)
        ],
        0,
    )
    shape = extra.shape
    same = lax.broadcasted_iota(jnp.int32, shape, 0) % tile == lax.broadcasted_iota(jnp.int32, shape, 1) % tile
    low = jnp.where(same, -1000000000.0, -1e30)
    groups = range(residues // tile)
    keys = [
        pair_ref[:, g * tile : (g + 1) * tile, :].reshape(wide, channels).astype(jnp.bfloat16) for g in groups
    ]
    scores = [dot_t(asked[g], keys[g]) for g in groups]
    scores = [
        jnp.where(jnp.logical_and(same, keep_ref[g : g + 1, :] > 0), scores[g] + extra, low) for g in groups
    ]
    return scores, keys


def near_attend_kernel(
    row_count, residues, own_ref, w_att_ref, w_bias_ref, crossing_ref, keep_ref, asked_ref, gate_ref, top_ref, total_ref, context_ref, pair_ref
):
    block_rows = row_count * residues
    heads = w_bias_ref.shape[0]
    inner = w_att_ref.shape[1] // 4
    head_dim = inner // heads
    tile = 8
    groups = range(residues // tile)
    mine = own_ref[spot_of(block_rows, lax.axis_index("row") // 2)]
    query = (dot(mine, w_att_ref[:, :inner]) * head_dim ** (-0.5)).astype(jnp.bfloat16)
    gate_ref[...] = sigmoid(dot(mine, w_att_ref[:, 3 * inner :]))
    head_of = lax.broadcasted_iota(jnp.int32, (1, inner), 1) // head_dim
    w_key = w_att_ref[:, inner : 2 * inner]
    w_key = jnp.concatenate([jnp.where(head_of == h, w_key, 0) for h in range(heads)], 0)
    by_head = jnp.split(dot_t(query, w_key), heads, 1)
    asked = [
        jnp.concatenate(
            [
                by_head[h][i * residues + g * tile : i * residues + (g + 1) * tile]
                for h in range(heads)
                for i in range(row_count)
            ],
            0,
        ).astype(jnp.bfloat16)
        for g in groups
    ]
    for g in groups:
        asked_ref[g] = asked[g]
    scores, keys = half_attention(own_ref, pair_ref, asked, w_bias_ref[...], crossing_ref, keep_ref)
    tops = [jnp.max(s, axis=-1, keepdims=True) for s in scores]
    scores = [jnp.exp(s - top) for s, top in zip(scores, tops, strict=True)]
    totals = [jnp.sum(s, axis=-1, keepdims=True) for s in scores]
    for g in groups:
        context_ref[g] = dot(scores[g].astype(jnp.bfloat16), keys[g])
        top_ref[g] = jnp.broadcast_to(tops[g], top_ref.shape[1:])
        total_ref[g] = jnp.broadcast_to(totals[g], total_ref.shape[1:])


def attend_kernel(
    row_count,
    other_ref,
    mid_ref,
    asked_ref,
    gate_ref,
    top_ref,
    total_ref,
    context_ref,
    crossing_ref,
    keep_ref,
    w_att_ref,
    w_bias_ref,
    w_out_ref,
    out_ref,
    pair_ref,
):
    residues = pair_ref.shape[1]
    heads = w_bias_ref.shape[0]
    inner = w_out_ref.shape[0]
    head_dim = inner // heads
    block_rows = row_count * residues
    tile = 8
    groups = range(residues // tile)
    asked = [asked_ref[g] for g in groups]
    scores, keys = half_attention(other_ref, pair_ref, asked, w_bias_ref[...], crossing_ref, keep_ref)
    tops = [jnp.maximum(jnp.max(scores[g], axis=-1, keepdims=True), top_ref[g]) for g in groups]
    scales = [jnp.exp(top_ref[g] - tops[g]) for g in groups]
    copies = pl.cdiv(scores[0].shape[1], tops[0].shape[1])
    scores = [jnp.exp(s - jnp.concatenate([top] * copies, 1)[:, : s.shape[1]]) for s, top in zip(scores, tops, strict=True)]
    totals = [jnp.sum(scores[g], axis=-1, keepdims=True) + total_ref[g] * scales[g] for g in groups]
    context = [dot(scores[g].astype(jnp.bfloat16), keys[g]) + context_ref[g] * scales[g] for g in groups]
    context = [context[g] * (1.0 / totals[g]) for g in groups]

    head_of = lax.broadcasted_iota(jnp.int32, (1, inner), 1) // head_dim
    by_head = [
        jnp.concatenate(
            [
                context[g][(h * row_count + i) * tile : (h * row_count + i + 1) * tile]
                for i in range(row_count)
                for g in groups
            ],
            0,
        ).astype(jnp.bfloat16)
        for h in range(heads)
    ]
    w_value = w_att_ref[:, 2 * inner : 3 * inner]
    w_value = jnp.concatenate([jnp.where(head_of == h, w_value, 0) for h in range(heads)], 0)
    values = dot(jnp.concatenate(by_head, 1), w_value)
    gated = (values * gate_ref[...]).astype(jnp.bfloat16)
    mid = mid_ref[spot_of(block_rows, lax.axis_index("row") // 2)].astype(jnp.float32)
    out_ref[...] = (mid + dot(gated, w_out_ref[...])).astype(jnp.bfloat16).reshape(out_ref.shape)


def call(body, args, outs, cost_us, name, scratch=(), space=pltpu.VMEM):
    return pl.pallas_call(
        body,
        out_shape=[jax.ShapeDtypeStruct(shape, dtype) for shape, dtype in outs],
        in_specs=[pl.BlockSpec(memory_space=space)] * len(args),
        out_specs=[pl.BlockSpec(memory_space=pltpu.VMEM)] * len(outs),
        scratch_shapes=list(scratch),
        compiler_params=pltpu.CompilerParams(vmem_limit_bytes=24 * 2**20),
        cost_estimate=pl.CostEstimate(flops=int(cost_us * 1e9), bytes_accessed=2**18, transcendentals=0),
        name=name,
    )(*args)


def gathered(
    row_devices,
    pair_acts,
    res_mask,
    chain_id,
    in_gain,
    w_left,
    w_right,
    w_mult_gate,
    mult_gain,
    w_mult_out,
    att_gain,
    w_att,
    w_pair_bias,
    cross_bias,
    w_att_out,
):
    row_count, residues, channels = pair_acts.shape
    width = w_left.shape[1] // 2
    heads = w_pair_bias.shape[1]
    own_count = residues // 2
    pairs = own_count * residues
    block_rows = row_count * residues
    tile = 8
    wide = own_count * tile
    bf16, f32 = jnp.bfloat16, jnp.float32

    def swap(x, shift):
        return lax.ppermute(x, "row", [(i, i ^ shift) for i in range(row_devices)])

    base, held = [0], pair_acts
    far, near, side = 9, 5, 3

    def spread(shifts):
        return [o ^ s for s in shifts for o in base]

    shift = row_devices // 2
    while shift > far:
        held = jnp.concatenate([held, swap(held, shift + 1)], 0)
        base = base + [o ^ (shift + 1) for o in base]
        shift //= 2
    from_far = swap(held, far)
    from_side = swap(held, side)
    from_near = swap(held, near)
    from_corner = swap(held, near ^ side)

    weights = [
        in_gain[None],
        mult_gain[None],
        att_gain[None],
        w_right,
        w_left,
        w_mult_gate,
        w_mult_out,
        w_att,
        w_pair_bias.T,
        w_att_out,
        held,
    ]
    live, crossing, keep, far_crossing, far_keep, in_g, mult_g, att_g, w_r, w_l, w_g, w_m, w_a, w_b, w_o, held = call(
        functools.partial(stage_kernel, len(weights)),
        [
            pltpu.with_memory_space_constraint(x, pltpu.HBM)
            for x in (cross_bias, chain_id, res_mask[None], chain_id[None], *weights)
        ],
        [((residues, channels), f32)] + 2 * [((heads * row_count, wide), f32), ((residues // tile, wide), f32)]
        + [(w.shape, w.dtype) for w in weights],
        0.05,
        "stage",
        [
            pltpu.SMEM((heads,), f32),
            pltpu.SMEM((residues,), jnp.int32),
            pltpu.VMEM((1, residues), jnp.int32),
            pltpu.VMEM((1, residues), jnp.int32),
            pltpu.SemaphoreType.DMA((len(weights) + 4,)),
        ],
        space=pltpu.HBM,
    )
    from_far_near = swap(from_far, near)
    from_far_corner = swap(from_far, near ^ side)
    from_far_side = swap(from_far, side)

    early = spread([0, far, side, near, near ^ side])
    early_pieces = [held, from_far, from_side, from_near, from_corner]

    def rows_like(count, dtype, blocks=None):
        return (((blocks or own_count // row_count) * block_rows, count), dtype)

    early_right, early_left, early_gate = call(
        functools.partial(early_kernel, early, row_count),
        [live, in_g, w_r, w_l, w_g, *early_pieces],
        [rows_like(width, bf16, len(early)), rows_like(width, f32, len(early)), rows_like(channels, f32, len(early))],
        0.05,
        "early_edges",
    )
    middle, last = spread([far ^ near ^ side, far ^ near]), spread([far ^ side])
    middle_pieces, last_pieces = [from_far_corner, from_far_near], [from_far_side]
    middle_right, middle_normed = call(
        functools.partial(middle_kernel, middle, row_count),
        [live, in_g, w_r, *middle_pieces],
        [rows_like(width, bf16, len(middle)), rows_like(channels, bf16, len(middle))],
        0.05,
        "middle_edges",
    )
    right, last_normed = call(
        functools.partial(right_kernel, [early, middle], last, row_count),
        [live, in_g, w_r, early_right, middle_right, *last_pieces],
        [rows_like(width, bf16), rows_like(channels, bf16, len(last))],
        0.05,
        "right_edges",
    )
    other = swap(right, 1)
    left, gate, acts, near_product = call(
        functools.partial(left_kernel, early, [middle, last], row_count, residues),
        [right, w_l, w_g, early_left, early_gate, middle_normed, last_normed]
        + early_pieces
        + middle_pieces
        + last_pieces,
        [rows_like(width, f32), rows_like(channels, f32), rows_like(channels, bf16)]
        + [((own_count * own_count, width), f32)],
        1.5,
        "left_edges",
        scratch=[pltpu.VMEM((pairs + own_count, width), f32)],
    )
    mid, normed_mid = call(
        functools.partial(product_kernel, row_count, residues),
        [left, other, near_product, gate, acts, jnp.concatenate([in_g, mult_g, att_g], 0), w_m],
        [((pairs, channels), bf16), ((pairs, channels), bf16)],
        2.4,
        "product",
        scratch=[pltpu.VMEM((pairs + own_count, width), f32), pltpu.VMEM((pairs + 2 * row_count, width), f32)],
    )
    normed_other = swap(normed_mid, 1)
    groups, asked_rows = residues // tile, heads * row_count * tile
    asked, gate_att, top, total, context = call(
        functools.partial(near_attend_kernel, row_count, residues),
        [normed_mid, w_a, w_b, crossing, keep],
        [((groups, asked_rows, channels), bf16), ((block_rows, w_o.shape[0]), f32)]
        + 3 * [((groups, asked_rows, channels), f32)],
        1.2,
        "near_attend",
        scratch=[pltpu.VMEM((own_count, residues, channels), f32)],
    )
    (out,) = call(
        functools.partial(attend_kernel, row_count),
        [normed_other, mid, asked, gate_att, top, total, context, far_crossing, far_keep, w_a, w_b, w_o],
        [((row_count, residues, channels), bf16)],
        1.5,
        "attend",
        scratch=[pltpu.VMEM((own_count, residues, channels), f32)],
    )
    return out


def solution(mesh):
    placed = (
        P(("groups", "row"), None, None),
        P("groups"),
        P("groups"),
        P(),
        P(),
        P(),
        P(),
        P(),
        P(),
        P(),
        P(),
        P(),
        P(),
        P(),
    )
    row_devices = mesh.shape["row"]

    def whole(pair_acts, *others):
        row_count, residues, channels = pair_acts.shape
        in_vmem = 4 * residues * residues * channels <= vmem_share
        paired = row_devices % 16 == 0 and row_devices & (row_devices - 1) == 0 and residues % 8 == 0
        if in_vmem and paired:
            return gathered(row_devices, pair_acts, *others)
        return shards(pair_acts, *others)

    return jax.shard_map(
        whole,
        mesh=mesh,
        in_specs=placed,
        out_specs=P(("groups", "row"), None, None),
        check_vma=False,
    )
```

```python
import functools

import jax
import jax.numpy as jnp
from jax import lax
from jax.experimental import pallas as pl
from jax.experimental.pallas import tpu as pltpu
from jax.sharding import PartitionSpec as P

norm_eps = 1e-05
vmem_share = 4 * 2**20


def layer_norm(tensor, norm_axis):
    tensor = tensor.astype(jnp.float32)
    average = jnp.mean(tensor, axis=norm_axis, keepdims=True)
    spread = jnp.mean(jnp.square(tensor - average), axis=norm_axis, keepdims=True)
    return (tensor - average) * lax.rsqrt(spread + norm_eps)


def edges_of(normed, weight, row_mask, mult_width):
    gate_part = jnp.einsum(
        "ikc,cm->mik", normed, weight[:, :mult_width], preferred_element_type=jnp.float32
    )
    value_part = jnp.einsum(
        "ikc,cm->mik", normed, weight[:, mult_width:], preferred_element_type=jnp.float32
    )
    return (row_mask[None] * jax.nn.sigmoid(gate_part) * value_part).astype(jnp.bfloat16)


def attend(normed_cols, bias_table, mask_float, chain_id, cross_bias, w_att, first_col):
    residues, col_count, _ = normed_cols.shape
    inner_dim = w_att.shape[1] // 4
    head_count = cross_bias.shape[0]
    head_dim = inner_dim // head_count

    def project(slot_idx):
        return jnp.einsum(
            "ijc,ce->ije",
            normed_cols,
            w_att[:, slot_idx * inner_dim : (slot_idx + 1) * inner_dim],
            preferred_element_type=jnp.float32,
        )

    query_all = (
        (project(0) * head_dim ** (-0.5))
        .astype(jnp.bfloat16)
        .reshape(residues, col_count, head_count, head_dim)
    )
    key_all = project(1).astype(jnp.bfloat16).reshape(residues, col_count, head_count, head_dim)
    value_all = project(2).astype(jnp.bfloat16).reshape(residues, col_count, head_count, head_dim)
    gate_att = jax.nn.sigmoid(project(3))
    crossing = (chain_id[:, None] != chain_id[None, :]).astype(jnp.float32)
    half_rows = residues // 2

    def column(col_index):
        query = lax.dynamic_index_in_dim(query_all, col_index, 1, keepdims=False)
        key_col = lax.dynamic_index_in_dim(key_all, col_index, 1, keepdims=False)
        value_col = lax.dynamic_index_in_dim(value_all, col_index, 1, keepdims=False)
        own_live = lax.dynamic_index_in_dim(mask_float, first_col + col_index, 0, keepdims=False)
        key_live = mask_float * own_live > 0
        pieces_out = []
        for block_idx in range(2):
            lower_row = block_idx * half_rows
            query_block = query[lower_row : lower_row + half_rows]
            scores = jnp.einsum(
                "ihd,khd->hki", query_block, key_col, preferred_element_type=jnp.float32
            )
            scores = scores + (
                bias_table[:, :, lower_row : lower_row + half_rows].astype(jnp.float32)
                + cross_bias[:, None, None] * crossing[None, :, lower_row : lower_row + half_rows]
            )
            scores = jnp.where(key_live[None, :, None], scores, -1000000000.0)
            weights = jax.nn.softmax(scores, axis=1).astype(jnp.bfloat16)
            pieces_out.append(
                jnp.einsum("hki,khd->ihd", weights, value_col, preferred_element_type=jnp.float32)
            )
        return jnp.concatenate(pieces_out, 0)

    outputs = lax.map(column, jnp.arange(col_count, dtype=jnp.int32))
    outputs = jnp.transpose(outputs, (1, 0, 2, 3)).reshape(residues, col_count, inner_dim)
    return (outputs * gate_att).astype(jnp.bfloat16)


def shards(
    pair_acts,
    res_mask,
    chain_id,
    in_gain,
    w_left,
    w_right,
    w_mult_gate,
    mult_gain,
    w_mult_out,
    att_gain,
    w_att,
    w_pair_bias,
    cross_bias,
    w_att_out,
):
    row_count = pair_acts.shape[0]
    mult_width = w_left.shape[1] // 2
    first_row = lax.axis_index("row") * row_count
    mask_float = res_mask.astype(jnp.float32)
    own_mask = lax.dynamic_slice_in_dim(mask_float, first_row, row_count)
    row_mask = own_mask[:, None] * mask_float[None, :]
    normed = (layer_norm(pair_acts, -1) * in_gain).astype(jnp.bfloat16)
    left_edges = edges_of(normed, w_left, row_mask, mult_width)
    right_edges = edges_of(normed, w_right, row_mask, mult_width)
    left_chan, right_chan = (
        lax.all_to_all(left_edges, "row", split_axis=0, concat_axis=1, tiled=True),
        lax.all_to_all(right_edges, "row", split_axis=0, concat_axis=1, tiled=True),
    )
    product = jnp.einsum(
        "cik,cjk->cij", left_chan, right_chan, preferred_element_type=jnp.float32
    ).astype(jnp.bfloat16)
    product_own = lax.all_to_all(product, "row", split_axis=1, concat_axis=0, tiled=True)
    product_norm = (layer_norm(product_own, 0) * mult_gain[:, None, None]).astype(jnp.bfloat16)
    gate_mult = jax.nn.sigmoid(
        jnp.einsum("ijc,cd->ijd", normed, w_mult_gate, preferred_element_type=jnp.float32)
    )
    update = jnp.einsum("mij,mc->ijc", product_norm, w_mult_out, preferred_element_type=jnp.float32)
    pair_mid = (pair_acts.astype(jnp.float32) + gate_mult * update).astype(jnp.bfloat16)
    normed_mid = (layer_norm(pair_mid, -1) * att_gain).astype(jnp.bfloat16)
    bias_piece = jnp.einsum(
        "kic,ch->hki", normed_mid, w_pair_bias, preferred_element_type=jnp.float32
    ).astype(jnp.bfloat16)
    bias_table = lax.all_gather(bias_piece, "row", axis=1, tiled=True)
    normed_cols = lax.all_to_all(normed_mid, "row", split_axis=1, concat_axis=0, tiled=True)
    gated = attend(normed_cols, bias_table, mask_float, chain_id, cross_bias, w_att, first_row)
    gated_rows = lax.all_to_all(gated, "row", split_axis=0, concat_axis=1, tiled=True)
    pair_out = pair_mid.astype(jnp.float32) + jnp.einsum(
        "ije,ec->ijc", gated_rows, w_att_out, preferred_element_type=jnp.float32
    )
    return pair_out.astype(jnp.bfloat16)


def dot(a, b):
    return jnp.dot(a, b, preferred_element_type=jnp.float32)


def dot_t(a, b):
    return lax.dot_general(a, b, (((1,), (1,)), ((), ())), preferred_element_type=jnp.float32)


def sigmoid(x):
    return 0.5 * jnp.tanh(0.5 * x) + 0.5


def norm_rows(x, gain):
    average = jnp.mean(x, axis=-1, keepdims=True)
    centred = x - average
    spread = jnp.mean(centred * centred, axis=-1, keepdims=True)
    return centred * lax.rsqrt(spread + norm_eps) * gain


def norm_all(pieces, gain):
    width = pieces[0].shape[-1]
    ones = jnp.ones((width, width), jnp.bfloat16)
    sums = [dot(x, ones) for x in pieces]
    centred = [x.astype(jnp.float32) - s * (1.0 / width) for x, s in zip(pieces, sums, strict=True)]
    spreads = [jnp.mean(c * c, axis=-1, keepdims=True) for c in centred]
    return [
        (c * lax.rsqrt(s + norm_eps) * gain).astype(jnp.bfloat16) for c, s in zip(centred, spreads, strict=True)
    ]


def gated_edges(normed, weight):
    both = dot(normed, weight)
    width = both.shape[1] // 2
    return (sigmoid(both[:, :width]) * both[:, width:]).astype(jnp.bfloat16)


def odd_bits(number):
    return bin(number).count("1") % 2


def parity(number):
    bits = lax.axis_size("row").bit_length() - 1
    return functools.reduce(jnp.bitwise_xor, [number >> b for b in range(bits)]) & 1


def own_side():
    return parity(lax.axis_index("row"))


def stage_kernel(copied, *refs):
    sources, refs = refs[: copied + 4], refs[copied + 4 :]
    (live_ref, *half_refs), copies = refs[:5], refs[5 : copied + 5]
    *early, done = refs[copied + 5 :]
    cross_ref, chain_ref, mask_row_ref, chain_row_ref = early
    moves = [
        pltpu.make_async_copy(source, target, done.at[at])
        for at, (source, target) in enumerate(zip(sources, (*early, *copies), strict=True))
    ]
    for move in moves:
        move.start()
    for move in moves[: len(early)]:
        move.wait()
    residues = live_ref.shape[0]
    blocks, wide = half_refs[1].shape
    tile = 2 * wide // residues
    heads = cross_ref.shape[0]
    row_count = half_refs[0].shape[0] // heads
    mask_row = mask_row_ref[...].astype(jnp.float32)
    chain_row = chain_row_ref[...].astype(jnp.float32)

    line = lax.broadcasted_iota(jnp.int32, (residues, residues), 0)
    spot = lax.broadcasted_iota(jnp.int32, (residues, residues), 1)
    diagonal = jnp.where(line == spot, mask_row, 0.0)
    live_ref[...] = dot(diagonal, jnp.ones((residues, live_ref.shape[1]), jnp.float32))

    line = lax.broadcasted_iota(jnp.int32, (residues, wide), 0)
    lane = lax.broadcasted_iota(jnp.int32, (residues, wide), 1)
    by_column = (lane % tile == line % tile).astype(jnp.float32)
    local = lane // tile
    chip = local // row_count
    block = lax.broadcasted_iota(jnp.int32, (blocks, residues), 0)
    spot = lax.broadcasted_iota(jnp.int32, (blocks, residues), 1)
    column_mask = dot(jnp.where(spot // tile == block, mask_row, 0.0), by_column)
    first = lax.axis_index("row") * row_count
    for half, side in enumerate((own_side(), 1 - own_side())):
        key = (2 * chip + jnp.bitwise_xor(parity(chip), side)) * row_count + local % row_count
        by_key = (key == line).astype(jnp.float32)
        crossing_ref, keep_ref = half_refs[2 * half : 2 * half + 2]
        keep_ref[...] = column_mask * dot(mask_row, by_key)
        chain_wide = dot(chain_row, by_key)
        for i in range(row_count):
            crossing = (chain_wide != chain_ref[first + i].astype(jnp.float32)).astype(jnp.float32)
            for h in range(heads):
                crossing_ref[h * row_count + i : h * row_count + i + 1, :] = cross_ref[h] * crossing
    for move in moves[len(early) :]:
        move.wait()


def spot_of(block_rows, place):
    return pl.ds(pl.multiple_of(place * block_rows, block_rows), block_rows)


def blocks_of(pieces, row_count):
    return [ref[at : at + row_count] for ref in pieces for at in range(0, ref.shape[0], row_count)]


def masked_norms(pieces, offsets, row_count, live_ref, gain_ref):
    me = lax.axis_index("row")
    for acts, offset in zip(blocks_of(pieces, row_count), offsets, strict=True):
        device = jnp.bitwise_xor(me, offset)
        normed = norm_rows(acts.astype(jnp.float32), gain_ref[0:1])
        live_all = live_ref[...]
        rows = [normed[r] * (live_all * live_ref[pl.ds(device * row_count + r, 1), :]) for r in range(row_count)]
        yield jnp.concatenate(rows, 0).astype(jnp.bfloat16)


def parts_of(ref, count):
    step = ref.shape[0] // count
    return [ref[at : at + step] for at in range(0, ref.shape[0], step)]


def spots_of(offsets, block_rows):
    me = lax.axis_index("row")
    return [spot_of(block_rows, jnp.bitwise_xor(me, offset) // 2) for offset in offsets]


def early_kernel(offsets, row_count, live_ref, gain_ref, w_right_ref, w_left_ref, w_gate_ref, *refs):
    pieces, (right_ref, left_ref, gate_ref) = refs[:-3], refs[-3:]
    block_rows = row_count * live_ref.shape[0]
    for t, normed in enumerate(masked_norms(pieces, offsets, row_count, live_ref, gain_ref)):
        at = slice(t * block_rows, (t + 1) * block_rows)
        right_ref[at] = gated_edges(normed, w_right_ref[...])
        left_ref[at] = gated_edges(normed, w_left_ref[...]).astype(jnp.float32)
        gate_ref[at] = sigmoid(dot(normed, w_gate_ref[...]))


def middle_kernel(offsets, row_count, live_ref, gain_ref, w_right_ref, *refs):
    pieces, (right_ref, normed_ref) = refs[:-2], refs[-2:]
    block_rows = row_count * live_ref.shape[0]
    for t, normed in enumerate(masked_norms(pieces, offsets, row_count, live_ref, gain_ref)):
        at = slice(t * block_rows, (t + 1) * block_rows)
        right_ref[at] = gated_edges(normed, w_right_ref[...])
        normed_ref[at] = normed


def right_kernel(done_offsets, offsets, row_count, live_ref, gain_ref, w_right_ref, *refs):
    done_refs, pieces = refs[: len(done_offsets)], refs[len(done_offsets) : -2]
    right_ref, normed_ref = refs[-2:]
    block_rows = row_count * live_ref.shape[0]
    for ref, held in zip(done_refs, done_offsets, strict=True):
        for spot, edges in zip(spots_of(held, block_rows), parts_of(ref, len(held)), strict=True):
            right_ref[spot] = edges
    normed_blocks = masked_norms(pieces, offsets, row_count, live_ref, gain_ref)
    for t, (spot, normed) in enumerate(zip(spots_of(offsets, block_rows), normed_blocks, strict=True)):
        right_ref[spot] = gated_edges(normed, w_right_ref[...])
        normed_ref[t * block_rows : (t + 1) * block_rows] = normed


def turn(source, turned_ref, row_count, residues):
    chips = source.shape[0] // (row_count * residues)
    own_count = chips * row_count
    for chip in range(chips):
        for r in range(row_count):
            lower = (chip * row_count + r) * residues
            turned_ref[pl.ds(r * chips + chip, residues, stride=own_count), :] = source[
                lower : lower + residues
            ].astype(jnp.float32)


def multiply(left_ref, turned_ref, residues, store):
    row_block, tile = 8, 8
    count = turned_ref.shape[0] // residues
    own_count = left_ref.shape[0] // residues
    tiles = count // tile

    def rows_of(block, carry):
        first = block * row_block

        def add(k, totals):
            ahead = [
                turned_ref[pl.ds(pl.multiple_of(k * count + t * tile, tile), tile), :] for t in range(tiles)
            ]
            out = []
            for a in range(row_block):
                one = left_ref[pl.ds((first + a) * residues + k, 1), :]
                out.extend(totals[a * tiles + t] + one * ahead[t] for t in range(tiles))
            return tuple(out)

        zeros = tuple(jnp.zeros((tile, left_ref.shape[1]), jnp.float32) for _ in range(row_block * tiles))
        totals = lax.fori_loop(0, residues, add, zeros, unroll=16)
        for a in range(row_block):
            for t in range(tiles):
                store(first + a, t, totals[a * tiles + t])
        return carry

    lax.fori_loop(0, own_count // row_block, rows_of, 0)


def left_kernel(early, late, row_count, residues, right_ref, w_left_ref, w_gate_ref, early_left_ref, early_gate_ref, *refs):
    normed_refs, pieces = refs[: len(late)], refs[len(late) : -5]
    left_ref, gate_ref, acts_ref, near_ref, turned_ref = refs[-5:]
    block_rows = row_count * residues
    blocks = zip(
        spots_of(early, block_rows),
        parts_of(early_left_ref, len(early)),
        parts_of(early_gate_ref, len(early)),
        strict=True,
    )
    for spot, edges, gate in blocks:
        left_ref[spot] = edges
        gate_ref[spot] = gate
    for offsets, normed_ref in zip(late, normed_refs, strict=True):
        for spot, normed in zip(spots_of(offsets, block_rows), parts_of(normed_ref, len(offsets)), strict=True):
            left_ref[spot] = gated_edges(normed, w_left_ref[...]).astype(jnp.float32)
            gate_ref[spot] = sigmoid(dot(normed, w_gate_ref[...]))
    order = early + [offset for offsets in late for offset in offsets]
    for spot, acts in zip(spots_of(order, block_rows), blocks_of(pieces, row_count), strict=True):
        acts_ref[spot] = acts.reshape(block_rows, acts.shape[-1])
    turn(right_ref, turned_ref, row_count, residues)
    count = turned_ref.shape[0] // residues

    def store(i, t, values):
        near_ref[pl.ds(pl.multiple_of(i * count + t * 8, 8), 8), :] = values

    multiply(left_ref, turned_ref, residues, store)


def product_kernel(
    row_count,
    residues,
    left_ref,
    other_ref,
    near_ref,
    gate_ref,
    acts_ref,
    gain_ref,
    w_out_ref,
    mid_ref,
    normed_mid_ref,
    turned_ref,
    product_ref,
):
    core = own_side()
    turn(other_ref, turned_ref, row_count, residues)
    count = turned_ref.shape[0] // residues
    chips = count // row_count
    part = chips // 8

    line = lax.broadcasted_iota(jnp.int32, (8, 1), 0)
    odd_line = (line ^ (line >> 1) ^ (line >> 2)) & 1

    def store(i, t, values):
        r, eighth = t // part, t % part
        near = near_ref[pl.ds(pl.multiple_of(i * count + t * 8, 8), 8), :]
        near_first = odd_line == (core ^ odd_bits(eighth))
        for side, rows in ((0, jnp.where(near_first, near, values)), (1, jnp.where(near_first, values, near))):
            start = i * residues + (eighth * 16 + side) * row_count + r
            product_ref[pl.ds(start, 8, stride=2 * row_count), :] = rows

    multiply(left_ref, turned_ref, residues, store)

    step = 2 * row_count * residues
    spots = [slice(lower, lower + step) for lower in range(0, acts_ref.shape[0], step)]
    normed = norm_all([product_ref[at].astype(jnp.bfloat16) for at in spots], gain_ref[1:2])
    updates = [gate_ref[at] * dot(rows, w_out_ref[...]) for at, rows in zip(spots, normed, strict=True)]
    mids = [
        (acts_ref[at].astype(jnp.float32) + update).astype(jnp.bfloat16)
        for at, update in zip(spots, updates, strict=True)
    ]
    for at, mid in zip(spots, mids, strict=True):
        mid_ref[at] = mid
    for at, rows in zip(spots, norm_all(mids, gain_ref[2:3]), strict=True):
        normed_mid_ref[at] = rows


def half_attention(rows_ref, pair_ref, asked, w_bias, crossing_ref, keep_ref):
    count, residues, channels = pair_ref.shape
    heads = w_bias.shape[0]
    row_count = crossing_ref.shape[0] // heads
    tile = 8
    wide = count * tile
    for local in range(count):
        pair_ref[local] = rows_ref[local * residues : (local + 1) * residues].astype(jnp.float32)
    first = lax.axis_index("row") * row_count
    pieces = []
    for i in range(row_count):
        column = pair_ref[:, pl.ds(first + i, 1), :]
        spread = jnp.broadcast_to(column, (count, tile, channels)).reshape(wide, channels)
        pieces.append(dot_t(w_bias, spread.astype(jnp.bfloat16)).astype(jnp.bfloat16).astype(jnp.float32))
    extra = jnp.concatenate(
        [
            jnp.broadcast_to(pieces[i][h : h + 1] + crossing_ref[h * row_count + i : h * row_count + i + 1], (tile, wide))
            for h in range(heads)
            for i in range(row_count)
        ],
        0,
    )
    shape = extra.shape
    same = lax.broadcasted_iota(jnp.int32, shape, 0) % tile == lax.broadcasted_iota(jnp.int32, shape, 1) % tile
    low = jnp.where(same, -1000000000.0, -1e30)
    groups = range(residues // tile)
    keys = [
        pair_ref[:, g * tile : (g + 1) * tile, :].reshape(wide, channels).astype(jnp.bfloat16) for g in groups
    ]
    scores = [dot_t(asked[g], keys[g]) for g in groups]
    scores = [
        jnp.where(jnp.logical_and(same, keep_ref[g : g + 1, :] > 0), scores[g] + extra, low) for g in groups
    ]
    return scores, keys


def near_attend_kernel(
    row_count, residues, own_ref, w_att_ref, w_bias_ref, crossing_ref, keep_ref, asked_ref, gate_ref, top_ref, total_ref, context_ref, pair_ref
):
    block_rows = row_count * residues
    heads = w_bias_ref.shape[0]
    inner = w_att_ref.shape[1] // 4
    head_dim = inner // heads
    tile = 8
    groups = range(residues // tile)
    mine = own_ref[spot_of(block_rows, lax.axis_index("row") // 2)]
    query = (dot(mine, w_att_ref[:, :inner]) * head_dim ** (-0.5)).astype(jnp.bfloat16)
    gate_ref[...] = sigmoid(dot(mine, w_att_ref[:, 3 * inner :]))
    head_of = lax.broadcasted_iota(jnp.int32, (1, inner), 1) // head_dim
    w_key = w_att_ref[:, inner : 2 * inner]
    w_key = jnp.concatenate([jnp.where(head_of == h, w_key, 0) for h in range(heads)], 0)
    by_head = jnp.split(dot_t(query, w_key), heads, 1)
    asked = [
        jnp.concatenate(
            [
                by_head[h][i * residues + g * tile : i * residues + (g + 1) * tile]
                for h in range(heads)
                for i in range(row_count)
            ],
            0,
        ).astype(jnp.bfloat16)
        for g in groups
    ]
    for g in groups:
        asked_ref[g] = asked[g]
    scores, keys = half_attention(own_ref, pair_ref, asked, w_bias_ref[...], crossing_ref, keep_ref)
    tops = [jnp.max(s, axis=-1, keepdims=True) for s in scores]
    scores = [jnp.exp(s - top) for s, top in zip(scores, tops, strict=True)]
    totals = [jnp.sum(s, axis=-1, keepdims=True) for s in scores]
    for g in groups:
        context_ref[g] = dot(scores[g].astype(jnp.bfloat16), keys[g])
        top_ref[g] = jnp.broadcast_to(tops[g], top_ref.shape[1:])
        total_ref[g] = jnp.broadcast_to(totals[g], total_ref.shape[1:])


def attend_kernel(
    row_count,
    other_ref,
    mid_ref,
    asked_ref,
    gate_ref,
    top_ref,
    total_ref,
    context_ref,
    crossing_ref,
    keep_ref,
    w_att_ref,
    w_bias_ref,
    w_out_ref,
    out_ref,
    pair_ref,
):
    residues = pair_ref.shape[1]
    heads = w_bias_ref.shape[0]
    inner = w_out_ref.shape[0]
    head_dim = inner // heads
    block_rows = row_count * residues
    tile = 8
    groups = range(residues // tile)
    asked = [asked_ref[g] for g in groups]
    scores, keys = half_attention(other_ref, pair_ref, asked, w_bias_ref[...], crossing_ref, keep_ref)
    tops = [jnp.maximum(jnp.max(scores[g], axis=-1, keepdims=True), top_ref[g]) for g in groups]
    scales = [jnp.exp(top_ref[g] - tops[g]) for g in groups]
    copies = pl.cdiv(scores[0].shape[1], tops[0].shape[1])
    scores = [jnp.exp(s - jnp.concatenate([top] * copies, 1)[:, : s.shape[1]]) for s, top in zip(scores, tops, strict=True)]
    totals = [jnp.sum(scores[g], axis=-1, keepdims=True) + total_ref[g] * scales[g] for g in groups]
    context = [dot(scores[g].astype(jnp.bfloat16), keys[g]) + context_ref[g] * scales[g] for g in groups]
    context = [context[g] * (1.0 / totals[g]) for g in groups]

    head_of = lax.broadcasted_iota(jnp.int32, (1, inner), 1) // head_dim
    by_head = [
        jnp.concatenate(
            [
                context[g][(h * row_count + i) * tile : (h * row_count + i + 1) * tile]
                for i in range(row_count)
                for g in groups
            ],
            0,
        ).astype(jnp.bfloat16)
        for h in range(heads)
    ]
    w_value = w_att_ref[:, 2 * inner : 3 * inner]
    w_value = jnp.concatenate([jnp.where(head_of == h, w_value, 0) for h in range(heads)], 0)
    values = dot(jnp.concatenate(by_head, 1), w_value)
    gated = (values * gate_ref[...]).astype(jnp.bfloat16)
    mid = mid_ref[spot_of(block_rows, lax.axis_index("row") // 2)].astype(jnp.float32)
    out_ref[...] = (mid + dot(gated, w_out_ref[...])).astype(jnp.bfloat16).reshape(out_ref.shape)


def call(body, args, outs, cost_us, name, scratch=(), space=pltpu.VMEM):
    return pl.pallas_call(
        body,
        out_shape=[jax.ShapeDtypeStruct(shape, dtype) for shape, dtype in outs],
        in_specs=[pl.BlockSpec(memory_space=space)] * len(args),
        out_specs=[pl.BlockSpec(memory_space=pltpu.VMEM)] * len(outs),
        scratch_shapes=list(scratch),
        compiler_params=pltpu.CompilerParams(vmem_limit_bytes=24 * 2**20),
        cost_estimate=pl.CostEstimate(flops=int(cost_us * 1e9), bytes_accessed=2**18, transcendentals=0),
        name=name,
    )(*args)


def gathered(
    row_devices,
    pair_acts,
    res_mask,
    chain_id,
    in_gain,
    w_left,
    w_right,
    w_mult_gate,
    mult_gain,
    w_mult_out,
    att_gain,
    w_att,
    w_pair_bias,
    cross_bias,
    w_att_out,
):
    row_count, residues, channels = pair_acts.shape
    width = w_left.shape[1] // 2
    heads = w_pair_bias.shape[1]
    own_count = residues // 2
    pairs = own_count * residues
    block_rows = row_count * residues
    tile = 8
    wide = own_count * tile
    bf16, f32 = jnp.bfloat16, jnp.float32

    def swap(x, shift):
        return lax.ppermute(x, "row", [(i, i ^ shift) for i in range(row_devices)])

    base, held = [0], pair_acts
    far, near, side = 9, 5, 3

    def spread(shifts):
        return [o ^ s for s in shifts for o in base]

    shift = row_devices // 2
    while shift > far:
        held = jnp.concatenate([held, swap(held, shift + 1)], 0)
        base = base + [o ^ (shift + 1) for o in base]
        shift //= 2
    from_far = swap(held, far)
    from_corner = swap(held, near ^ side)
    from_near = swap(held, near)
    from_side = swap(held, side)

    weights = [
        in_gain[None],
        mult_gain[None],
        att_gain[None],
        w_right,
        w_left,
        w_mult_gate,
        w_mult_out,
        w_att,
        w_pair_bias.T,
        w_att_out,
        held,
    ]
    live, crossing, keep, far_crossing, far_keep, in_g, mult_g, att_g, w_r, w_l, w_g, w_m, w_a, w_b, w_o, held = call(
        functools.partial(stage_kernel, len(weights)),
        [
            pltpu.with_memory_space_constraint(x, pltpu.HBM)
            for x in (cross_bias, chain_id, res_mask[None], chain_id[None], *weights)
        ],
        [((residues, channels), f32)] + 2 * [((heads * row_count, wide), f32), ((residues // tile, wide), f32)]
        + [(w.shape, w.dtype) for w in weights],
        0.05,
        "stage",
        [
            pltpu.SMEM((heads,), f32),
            pltpu.SMEM((residues,), jnp.int32),
            pltpu.VMEM((1, residues), jnp.int32),
            pltpu.VMEM((1, residues), jnp.int32),
            pltpu.SemaphoreType.DMA((len(weights) + 4,)),
        ],
        space=pltpu.HBM,
    )
    from_far_near = swap(from_far, near)
    from_far_corner = swap(from_far, near ^ side)
    from_far_side = swap(from_far, side)

    early = spread([0, far, near ^ side, near, side])
    early_pieces = [held, from_far, from_corner, from_near, from_side]

    def rows_like(count, dtype, blocks=None):
        return (((blocks or own_count // row_count) * block_rows, count), dtype)

    early_right, early_left, early_gate = call(
        functools.partial(early_kernel, early, row_count),
        [live, in_g, w_r, w_l, w_g, *early_pieces],
        [rows_like(width, bf16, len(early)), rows_like(width, f32, len(early)), rows_like(channels, f32, len(early))],
        0.05,
        "early_edges",
    )
    middle, last = spread([far ^ near ^ side]), spread([far ^ near, far ^ side])
    middle_pieces, last_pieces = [from_far_corner], [from_far_near, from_far_side]
    middle_right, middle_normed = call(
        functools.partial(middle_kernel, middle, row_count),
        [live, in_g, w_r, *middle_pieces],
        [rows_like(width, bf16, len(middle)), rows_like(channels, bf16, len(middle))],
        0.05,
        "middle_edges",
    )
    right, last_normed = call(
        functools.partial(right_kernel, [early, middle], last, row_count),
        [live, in_g, w_r, early_right, middle_right, *last_pieces],
        [rows_like(width, bf16), rows_like(channels, bf16, len(last))],
        0.05,
        "right_edges",
    )
    other = swap(right, 1)
    left, gate, acts, near_product = call(
        functools.partial(left_kernel, early, [middle, last], row_count, residues),
        [right, w_l, w_g, early_left, early_gate, middle_normed, last_normed]
        + early_pieces
        + middle_pieces
        + last_pieces,
        [rows_like(width, f32), rows_like(channels, f32), rows_like(channels, bf16)]
        + [((own_count * own_count, width), f32)],
        1.5,
        "left_edges",
        scratch=[pltpu.VMEM((pairs + own_count, width), f32)],
    )
    mid, normed_mid = call(
        functools.partial(product_kernel, row_count, residues),
        [left, other, near_product, gate, acts, jnp.concatenate([in_g, mult_g, att_g], 0), w_m],
        [((pairs, channels), bf16), ((pairs, channels), bf16)],
        2.4,
        "product",
        scratch=[pltpu.VMEM((pairs + own_count, width), f32), pltpu.VMEM((pairs + 2 * row_count, width), f32)],
    )
    normed_other = swap(normed_mid, 1)
    groups, asked_rows = residues // tile, heads * row_count * tile
    asked, gate_att, top, total, context = call(
        functools.partial(near_attend_kernel, row_count, residues),
        [normed_mid, w_a, w_b, crossing, keep],
        [((groups, asked_rows, channels), bf16), ((block_rows, w_o.shape[0]), f32)]
        + 3 * [((groups, asked_rows, channels), f32)],
        1.2,
        "near_attend",
        scratch=[pltpu.VMEM((own_count, residues, channels), f32)],
    )
    (out,) = call(
        functools.partial(attend_kernel, row_count),
        [normed_other, mid, asked, gate_att, top, total, context, far_crossing, far_keep, w_a, w_b, w_o],
        [((row_count, residues, channels), bf16)],
        1.5,
        "attend",
        scratch=[pltpu.VMEM((own_count, residues, channels), f32)],
    )
    return out


def solution(mesh):
    placed = (
        P(("groups", "row"), None, None),
        P("groups"),
        P("groups"),
        P(),
        P(),
        P(),
        P(),
        P(),
        P(),
        P(),
        P(),
        P(),
        P(),
        P(),
    )
    row_devices = mesh.shape["row"]

    def whole(pair_acts, *others):
        row_count, residues, channels = pair_acts.shape
        in_vmem = 4 * residues * residues * channels <= vmem_share
        paired = row_devices % 16 == 0 and row_devices & (row_devices - 1) == 0 and residues % 8 == 0
        if in_vmem and paired:
            return gathered(row_devices, pair_acts, *others)
        return shards(pair_acts, *others)

    return jax.shard_map(
        whole,
        mesh=mesh,
        in_specs=placed,
        out_specs=P(("groups", "row"), None, None),
        check_vma=False,
    )
```

```python
import functools

import jax
import jax.numpy as jnp
from jax import lax
from jax.experimental import pallas as pl
from jax.experimental.pallas import tpu as pltpu
from jax.sharding import PartitionSpec as P

norm_eps = 1e-05
vmem_share = 4 * 2**20


def layer_norm(tensor, norm_axis):
    tensor = tensor.astype(jnp.float32)
    average = jnp.mean(tensor, axis=norm_axis, keepdims=True)
    spread = jnp.mean(jnp.square(tensor - average), axis=norm_axis, keepdims=True)
    return (tensor - average) * lax.rsqrt(spread + norm_eps)


def edges_of(normed, weight, row_mask, mult_width):
    gate_part = jnp.einsum(
        "ikc,cm->mik", normed, weight[:, :mult_width], preferred_element_type=jnp.float32
    )
    value_part = jnp.einsum(
        "ikc,cm->mik", normed, weight[:, mult_width:], preferred_element_type=jnp.float32
    )
    return (row_mask[None] * jax.nn.sigmoid(gate_part) * value_part).astype(jnp.bfloat16)


def attend(normed_cols, bias_table, mask_float, chain_id, cross_bias, w_att, first_col):
    residues, col_count, _ = normed_cols.shape
    inner_dim = w_att.shape[1] // 4
    head_count = cross_bias.shape[0]
    head_dim = inner_dim // head_count

    def project(slot_idx):
        return jnp.einsum(
            "ijc,ce->ije",
            normed_cols,
            w_att[:, slot_idx * inner_dim : (slot_idx + 1) * inner_dim],
            preferred_element_type=jnp.float32,
        )

    query_all = (
        (project(0) * head_dim ** (-0.5))
        .astype(jnp.bfloat16)
        .reshape(residues, col_count, head_count, head_dim)
    )
    key_all = project(1).astype(jnp.bfloat16).reshape(residues, col_count, head_count, head_dim)
    value_all = project(2).astype(jnp.bfloat16).reshape(residues, col_count, head_count, head_dim)
    gate_att = jax.nn.sigmoid(project(3))
    crossing = (chain_id[:, None] != chain_id[None, :]).astype(jnp.float32)
    half_rows = residues // 2

    def column(col_index):
        query = lax.dynamic_index_in_dim(query_all, col_index, 1, keepdims=False)
        key_col = lax.dynamic_index_in_dim(key_all, col_index, 1, keepdims=False)
        value_col = lax.dynamic_index_in_dim(value_all, col_index, 1, keepdims=False)
        own_live = lax.dynamic_index_in_dim(mask_float, first_col + col_index, 0, keepdims=False)
        key_live = mask_float * own_live > 0
        pieces_out = []
        for block_idx in range(2):
            lower_row = block_idx * half_rows
            query_block = query[lower_row : lower_row + half_rows]
            scores = jnp.einsum(
                "ihd,khd->hki", query_block, key_col, preferred_element_type=jnp.float32
            )
            scores = scores + (
                bias_table[:, :, lower_row : lower_row + half_rows].astype(jnp.float32)
                + cross_bias[:, None, None] * crossing[None, :, lower_row : lower_row + half_rows]
            )
            scores = jnp.where(key_live[None, :, None], scores, -1000000000.0)
            weights = jax.nn.softmax(scores, axis=1).astype(jnp.bfloat16)
            pieces_out.append(
                jnp.einsum("hki,khd->ihd", weights, value_col, preferred_element_type=jnp.float32)
            )
        return jnp.concatenate(pieces_out, 0)

    outputs = lax.map(column, jnp.arange(col_count, dtype=jnp.int32))
    outputs = jnp.transpose(outputs, (1, 0, 2, 3)).reshape(residues, col_count, inner_dim)
    return (outputs * gate_att).astype(jnp.bfloat16)


def shards(
    pair_acts,
    res_mask,
    chain_id,
    in_gain,
    w_left,
    w_right,
    w_mult_gate,
    mult_gain,
    w_mult_out,
    att_gain,
    w_att,
    w_pair_bias,
    cross_bias,
    w_att_out,
):
    row_count = pair_acts.shape[0]
    mult_width = w_left.shape[1] // 2
    first_row = lax.axis_index("row") * row_count
    mask_float = res_mask.astype(jnp.float32)
    own_mask = lax.dynamic_slice_in_dim(mask_float, first_row, row_count)
    row_mask = own_mask[:, None] * mask_float[None, :]
    normed = (layer_norm(pair_acts, -1) * in_gain).astype(jnp.bfloat16)
    left_edges = edges_of(normed, w_left, row_mask, mult_width)
    right_edges = edges_of(normed, w_right, row_mask, mult_width)
    left_chan, right_chan = (
        lax.all_to_all(left_edges, "row", split_axis=0, concat_axis=1, tiled=True),
        lax.all_to_all(right_edges, "row", split_axis=0, concat_axis=1, tiled=True),
    )
    product = jnp.einsum(
        "cik,cjk->cij", left_chan, right_chan, preferred_element_type=jnp.float32
    ).astype(jnp.bfloat16)
    product_own = lax.all_to_all(product, "row", split_axis=1, concat_axis=0, tiled=True)
    product_norm = (layer_norm(product_own, 0) * mult_gain[:, None, None]).astype(jnp.bfloat16)
    gate_mult = jax.nn.sigmoid(
        jnp.einsum("ijc,cd->ijd", normed, w_mult_gate, preferred_element_type=jnp.float32)
    )
    update = jnp.einsum("mij,mc->ijc", product_norm, w_mult_out, preferred_element_type=jnp.float32)
    pair_mid = (pair_acts.astype(jnp.float32) + gate_mult * update).astype(jnp.bfloat16)
    normed_mid = (layer_norm(pair_mid, -1) * att_gain).astype(jnp.bfloat16)
    bias_piece = jnp.einsum(
        "kic,ch->hki", normed_mid, w_pair_bias, preferred_element_type=jnp.float32
    ).astype(jnp.bfloat16)
    bias_table = lax.all_gather(bias_piece, "row", axis=1, tiled=True)
    normed_cols = lax.all_to_all(normed_mid, "row", split_axis=1, concat_axis=0, tiled=True)
    gated = attend(normed_cols, bias_table, mask_float, chain_id, cross_bias, w_att, first_row)
    gated_rows = lax.all_to_all(gated, "row", split_axis=0, concat_axis=1, tiled=True)
    pair_out = pair_mid.astype(jnp.float32) + jnp.einsum(
        "ije,ec->ijc", gated_rows, w_att_out, preferred_element_type=jnp.float32
    )
    return pair_out.astype(jnp.bfloat16)


def dot(a, b):
    return jnp.dot(a, b, preferred_element_type=jnp.float32)


def dot_t(a, b):
    return lax.dot_general(a, b, (((1,), (1,)), ((), ())), preferred_element_type=jnp.float32)


def sigmoid(x):
    return 0.5 * jnp.tanh(0.5 * x) + 0.5


def norm_rows(x, gain):
    average = jnp.mean(x, axis=-1, keepdims=True)
    centred = x - average
    spread = jnp.mean(centred * centred, axis=-1, keepdims=True)
    return centred * lax.rsqrt(spread + norm_eps) * gain


def norm_all(pieces, gain):
    width = pieces[0].shape[-1]
    ones = jnp.ones((width, width), jnp.bfloat16)
    sums = [dot(x, ones) for x in pieces]
    centred = [x.astype(jnp.float32) - s * (1.0 / width) for x, s in zip(pieces, sums, strict=True)]
    spreads = [jnp.mean(c * c, axis=-1, keepdims=True) for c in centred]
    return [
        (c * lax.rsqrt(s + norm_eps) * gain).astype(jnp.bfloat16) for c, s in zip(centred, spreads, strict=True)
    ]


def gated_edges(normed, weight):
    both = dot(normed, weight)
    width = both.shape[1] // 2
    return (sigmoid(both[:, :width]) * both[:, width:]).astype(jnp.bfloat16)


def odd_bits(number):
    return bin(number).count("1") % 2


def parity(number):
    bits = lax.axis_size("row").bit_length() - 1
    return functools.reduce(jnp.bitwise_xor, [number >> b for b in range(bits)]) & 1


def own_side():
    return parity(lax.axis_index("row"))


def stage_kernel(copied, *refs):
    sources, refs = refs[: copied + 4], refs[copied + 4 :]
    (live_ref, *half_refs), copies = refs[:5], refs[5 : copied + 5]
    *early, done = refs[copied + 5 :]
    cross_ref, chain_ref, mask_row_ref, chain_row_ref = early
    moves = [
        pltpu.make_async_copy(source, target, done.at[at])
        for at, (source, target) in enumerate(zip(sources, (*early, *copies), strict=True))
    ]
    for move in moves:
        move.start()
    for move in moves[: len(early)]:
        move.wait()
    residues = live_ref.shape[0]
    blocks, wide = half_refs[1].shape
    tile = 2 * wide // residues
    heads = cross_ref.shape[0]
    row_count = half_refs[0].shape[0] // heads
    mask_row = mask_row_ref[...].astype(jnp.float32)
    chain_row = chain_row_ref[...].astype(jnp.float32)

    line = lax.broadcasted_iota(jnp.int32, (residues, residues), 0)
    spot = lax.broadcasted_iota(jnp.int32, (residues, residues), 1)
    diagonal = jnp.where(line == spot, mask_row, 0.0)
    live_ref[...] = dot(diagonal, jnp.ones((residues, live_ref.shape[1]), jnp.float32))

    line = lax.broadcasted_iota(jnp.int32, (residues, wide), 0)
    lane = lax.broadcasted_iota(jnp.int32, (residues, wide), 1)
    by_column = (lane % tile == line % tile).astype(jnp.float32)
    local = lane // tile
    chip = local // row_count
    block = lax.broadcasted_iota(jnp.int32, (blocks, residues), 0)
    spot = lax.broadcasted_iota(jnp.int32, (blocks, residues), 1)
    column_mask = dot(jnp.where(spot // tile == block, mask_row, 0.0), by_column)
    first = lax.axis_index("row") * row_count
    for half, side in enumerate((own_side(), 1 - own_side())):
        key = (2 * chip + jnp.bitwise_xor(parity(chip), side)) * row_count + local % row_count
        by_key = (key == line).astype(jnp.float32)
        crossing_ref, keep_ref = half_refs[2 * half : 2 * half + 2]
        keep_ref[...] = column_mask * dot(mask_row, by_key)
        chain_wide = dot(chain_row, by_key)
        for i in range(row_count):
            crossing = (chain_wide != chain_ref[first + i].astype(jnp.float32)).astype(jnp.float32)
            for h in range(heads):
                crossing_ref[h * row_count + i : h * row_count + i + 1, :] = cross_ref[h] * crossing
    for move in moves[len(early) :]:
        move.wait()


def spot_of(block_rows, place):
    return pl.ds(pl.multiple_of(place * block_rows, block_rows), block_rows)


def blocks_of(pieces, row_count):
    return [ref[at : at + row_count] for ref in pieces for at in range(0, ref.shape[0], row_count)]


def masked_norms(pieces, offsets, row_count, live_ref, gain_ref):
    me = lax.axis_index("row")
    for acts, offset in zip(blocks_of(pieces, row_count), offsets, strict=True):
        device = jnp.bitwise_xor(me, offset)
        normed = norm_rows(acts.astype(jnp.float32), gain_ref[0:1])
        live_all = live_ref[...]
        rows = [normed[r] * (live_all * live_ref[pl.ds(device * row_count + r, 1), :]) for r in range(row_count)]
        yield jnp.concatenate(rows, 0).astype(jnp.bfloat16)


def parts_of(ref, count):
    step = ref.shape[0] // count
    return [ref[at : at + step] for at in range(0, ref.shape[0], step)]


def spots_of(offsets, block_rows):
    me = lax.axis_index("row")
    return [spot_of(block_rows, jnp.bitwise_xor(me, offset) // 2) for offset in offsets]


def early_kernel(offsets, row_count, live_ref, gain_ref, w_right_ref, w_left_ref, w_gate_ref, *refs):
    pieces, (right_ref, left_ref, gate_ref) = refs[:-3], refs[-3:]
    block_rows = row_count * live_ref.shape[0]
    for t, normed in enumerate(masked_norms(pieces, offsets, row_count, live_ref, gain_ref)):
        at = slice(t * block_rows, (t + 1) * block_rows)
        right_ref[at] = gated_edges(normed, w_right_ref[...])
        left_ref[at] = gated_edges(normed, w_left_ref[...]).astype(jnp.float32)
        gate_ref[at] = sigmoid(dot(normed, w_gate_ref[...]))


def middle_kernel(offsets, row_count, live_ref, gain_ref, w_right_ref, *refs):
    pieces, (right_ref, normed_ref) = refs[:-2], refs[-2:]
    block_rows = row_count * live_ref.shape[0]
    for t, normed in enumerate(masked_norms(pieces, offsets, row_count, live_ref, gain_ref)):
        at = slice(t * block_rows, (t + 1) * block_rows)
        right_ref[at] = gated_edges(normed, w_right_ref[...])
        normed_ref[at] = normed


def right_kernel(done_offsets, offsets, row_count, live_ref, gain_ref, w_right_ref, *refs):
    done_refs, pieces = refs[: len(done_offsets)], refs[len(done_offsets) : -2]
    right_ref, normed_ref = refs[-2:]
    block_rows = row_count * live_ref.shape[0]
    for ref, held in zip(done_refs, done_offsets, strict=True):
        for spot, edges in zip(spots_of(held, block_rows), parts_of(ref, len(held)), strict=True):
            right_ref[spot] = edges
    normed_blocks = masked_norms(pieces, offsets, row_count, live_ref, gain_ref)
    for t, (spot, normed) in enumerate(zip(spots_of(offsets, block_rows), normed_blocks, strict=True)):
        right_ref[spot] = gated_edges(normed, w_right_ref[...])
        normed_ref[t * block_rows : (t + 1) * block_rows] = normed


def turn(source, turned_ref, row_count, residues):
    chips = source.shape[0] // (row_count * residues)
    own_count = chips * row_count
    for chip in range(chips):
        for r in range(row_count):
            lower = (chip * row_count + r) * residues
            turned_ref[pl.ds(r * chips + chip, residues, stride=own_count), :] = source[
                lower : lower + residues
            ].astype(jnp.float32)


def multiply(left_ref, turned_ref, residues, store):
    row_block, tile = 8, 8
    count = turned_ref.shape[0] // residues
    own_count = left_ref.shape[0] // residues
    tiles = count // tile

    def rows_of(block, carry):
        first = block * row_block

        def add(k, totals):
            ahead = [
                turned_ref[pl.ds(pl.multiple_of(k * count + t * tile, tile), tile), :] for t in range(tiles)
            ]
            out = []
            for a in range(row_block):
                one = left_ref[pl.ds((first + a) * residues + k, 1), :]
                out.extend(totals[a * tiles + t] + one * ahead[t] for t in range(tiles))
            return tuple(out)

        zeros = tuple(jnp.zeros((tile, left_ref.shape[1]), jnp.float32) for _ in range(row_block * tiles))
        totals = lax.fori_loop(0, residues, add, zeros, unroll=24)
        for a in range(row_block):
            for t in range(tiles):
                store(first + a, t, totals[a * tiles + t])
        return carry

    lax.fori_loop(0, own_count // row_block, rows_of, 0)


def left_kernel(early, late, row_count, residues, right_ref, w_left_ref, w_gate_ref, early_left_ref, early_gate_ref, *refs):
    normed_refs, pieces = refs[: len(late)], refs[len(late) : -5]
    left_ref, gate_ref, acts_ref, near_ref, turned_ref = refs[-5:]
    block_rows = row_count * residues
    blocks = zip(
        spots_of(early, block_rows),
        parts_of(early_left_ref, len(early)),
        parts_of(early_gate_ref, len(early)),
        strict=True,
    )
    for spot, edges, gate in blocks:
        left_ref[spot] = edges
        gate_ref[spot] = gate
    for offsets, normed_ref in zip(late, normed_refs, strict=True):
        for spot, normed in zip(spots_of(offsets, block_rows), parts_of(normed_ref, len(offsets)), strict=True):
            left_ref[spot] = gated_edges(normed, w_left_ref[...]).astype(jnp.float32)
            gate_ref[spot] = sigmoid(dot(normed, w_gate_ref[...]))
    order = early + [offset for offsets in late for offset in offsets]
    for spot, acts in zip(spots_of(order, block_rows), blocks_of(pieces, row_count), strict=True):
        acts_ref[spot] = acts.reshape(block_rows, acts.shape[-1])
    turn(right_ref, turned_ref, row_count, residues)
    count = turned_ref.shape[0] // residues

    def store(i, t, values):
        near_ref[pl.ds(pl.multiple_of(i * count + t * 8, 8), 8), :] = values

    multiply(left_ref, turned_ref, residues, store)


def product_kernel(
    row_count,
    residues,
    left_ref,
    other_ref,
    near_ref,
    gate_ref,
    acts_ref,
    gain_ref,
    w_out_ref,
    mid_ref,
    normed_mid_ref,
    turned_ref,
    product_ref,
):
    core = own_side()
    turn(other_ref, turned_ref, row_count, residues)
    count = turned_ref.shape[0] // residues
    chips = count // row_count
    part = chips // 8

    line = lax.broadcasted_iota(jnp.int32, (8, 1), 0)
    odd_line = (line ^ (line >> 1) ^ (line >> 2)) & 1

    def store(i, t, values):
        r, eighth = t // part, t % part
        near = near_ref[pl.ds(pl.multiple_of(i * count + t * 8, 8), 8), :]
        near_first = odd_line == (core ^ odd_bits(eighth))
        for side, rows in ((0, jnp.where(near_first, near, values)), (1, jnp.where(near_first, values, near))):
            start = i * residues + (eighth * 16 + side) * row_count + r
            product_ref[pl.ds(start, 8, stride=2 * row_count), :] = rows

    multiply(left_ref, turned_ref, residues, store)

    step = 2 * row_count * residues
    spots = [slice(lower, lower + step) for lower in range(0, acts_ref.shape[0], step)]
    normed = norm_all([product_ref[at].astype(jnp.bfloat16) for at in spots], gain_ref[1:2])
    updates = [gate_ref[at] * dot(rows, w_out_ref[...]) for at, rows in zip(spots, normed, strict=True)]
    mids = [
        (acts_ref[at].astype(jnp.float32) + update).astype(jnp.bfloat16)
        for at, update in zip(spots, updates, strict=True)
    ]
    for at, mid in zip(spots, mids, strict=True):
        mid_ref[at] = mid
    for at, rows in zip(spots, norm_all(mids, gain_ref[2:3]), strict=True):
        normed_mid_ref[at] = rows


def half_attention(rows_ref, pair_ref, asked, w_bias, crossing_ref, keep_ref):
    count, residues, channels = pair_ref.shape
    heads = w_bias.shape[0]
    row_count = crossing_ref.shape[0] // heads
    tile = 8
    wide = count * tile
    for local in range(count):
        pair_ref[local] = rows_ref[local * residues : (local + 1) * residues].astype(jnp.float32)
    first = lax.axis_index("row") * row_count
    pieces = []
    for i in range(row_count):
        column = pair_ref[:, pl.ds(first + i, 1), :]
        spread = jnp.broadcast_to(column, (count, tile, channels)).reshape(wide, channels)
        pieces.append(dot_t(w_bias, spread.astype(jnp.bfloat16)).astype(jnp.bfloat16).astype(jnp.float32))
    extra = jnp.concatenate(
        [
            jnp.broadcast_to(pieces[i][h : h + 1] + crossing_ref[h * row_count + i : h * row_count + i + 1], (tile, wide))
            for h in range(heads)
            for i in range(row_count)
        ],
        0,
    )
    shape = extra.shape
    same = lax.broadcasted_iota(jnp.int32, shape, 0) % tile == lax.broadcasted_iota(jnp.int32, shape, 1) % tile
    low = jnp.where(same, -1000000000.0, -1e30)
    groups = range(residues // tile)
    keys = [
        pair_ref[:, g * tile : (g + 1) * tile, :].reshape(wide, channels).astype(jnp.bfloat16) for g in groups
    ]
    scores = [dot_t(asked[g], keys[g]) for g in groups]
    scores = [
        jnp.where(jnp.logical_and(same, keep_ref[g : g + 1, :] > 0), scores[g] + extra, low) for g in groups
    ]
    return scores, keys


def near_attend_kernel(
    row_count, residues, own_ref, w_att_ref, w_bias_ref, crossing_ref, keep_ref, asked_ref, gate_ref, top_ref, total_ref, context_ref, pair_ref
):
    block_rows = row_count * residues
    heads = w_bias_ref.shape[0]
    inner = w_att_ref.shape[1] // 4
    head_dim = inner // heads
    tile = 8
    groups = range(residues // tile)
    mine = own_ref[spot_of(block_rows, lax.axis_index("row") // 2)]
    query = (dot(mine, w_att_ref[:, :inner]) * head_dim ** (-0.5)).astype(jnp.bfloat16)
    gate_ref[...] = sigmoid(dot(mine, w_att_ref[:, 3 * inner :]))
    head_of = lax.broadcasted_iota(jnp.int32, (1, inner), 1) // head_dim
    w_key = w_att_ref[:, inner : 2 * inner]
    w_key = jnp.concatenate([jnp.where(head_of == h, w_key, 0) for h in range(heads)], 0)
    by_head = jnp.split(dot_t(query, w_key), heads, 1)
    asked = [
        jnp.concatenate(
            [
                by_head[h][i * residues + g * tile : i * residues + (g + 1) * tile]
                for h in range(heads)
                for i in range(row_count)
            ],
            0,
        ).astype(jnp.bfloat16)
        for g in groups
    ]
    for g in groups:
        asked_ref[g] = asked[g]
    scores, keys = half_attention(own_ref, pair_ref, asked, w_bias_ref[...], crossing_ref, keep_ref)
    tops = [jnp.max(s, axis=-1, keepdims=True) for s in scores]
    scores = [jnp.exp(s - top) for s, top in zip(scores, tops, strict=True)]
    totals = [jnp.sum(s, axis=-1, keepdims=True) for s in scores]
    for g in groups:
        context_ref[g] = dot(scores[g].astype(jnp.bfloat16), keys[g])
        top_ref[g] = jnp.broadcast_to(tops[g], top_ref.shape[1:])
        total_ref[g] = jnp.broadcast_to(totals[g], total_ref.shape[1:])


def attend_kernel(
    row_count,
    other_ref,
    mid_ref,
    asked_ref,
    gate_ref,
    top_ref,
    total_ref,
    context_ref,
    crossing_ref,
    keep_ref,
    w_att_ref,
    w_bias_ref,
    w_out_ref,
    out_ref,
    pair_ref,
):
    residues = pair_ref.shape[1]
    heads = w_bias_ref.shape[0]
    inner = w_out_ref.shape[0]
    head_dim = inner // heads
    block_rows = row_count * residues
    tile = 8
    groups = range(residues // tile)
    asked = [asked_ref[g] for g in groups]
    scores, keys = half_attention(other_ref, pair_ref, asked, w_bias_ref[...], crossing_ref, keep_ref)
    tops = [jnp.maximum(jnp.max(scores[g], axis=-1, keepdims=True), top_ref[g]) for g in groups]
    scales = [jnp.exp(top_ref[g] - tops[g]) for g in groups]
    copies = pl.cdiv(scores[0].shape[1], tops[0].shape[1])
    scores = [jnp.exp(s - jnp.concatenate([top] * copies, 1)[:, : s.shape[1]]) for s, top in zip(scores, tops, strict=True)]
    totals = [jnp.sum(scores[g], axis=-1, keepdims=True) + total_ref[g] * scales[g] for g in groups]
    context = [dot(scores[g].astype(jnp.bfloat16), keys[g]) + context_ref[g] * scales[g] for g in groups]
    context = [context[g] * (1.0 / totals[g]) for g in groups]

    head_of = lax.broadcasted_iota(jnp.int32, (1, inner), 1) // head_dim
    by_head = [
        jnp.concatenate(
            [
                context[g][(h * row_count + i) * tile : (h * row_count + i + 1) * tile]
                for i in range(row_count)
                for g in groups
            ],
            0,
        ).astype(jnp.bfloat16)
        for h in range(heads)
    ]
    w_value = w_att_ref[:, 2 * inner : 3 * inner]
    w_value = jnp.concatenate([jnp.where(head_of == h, w_value, 0) for h in range(heads)], 0)
    values = dot(jnp.concatenate(by_head, 1), w_value)
    gated = (values * gate_ref[...]).astype(jnp.bfloat16)
    mid = mid_ref[spot_of(block_rows, lax.axis_index("row") // 2)].astype(jnp.float32)
    out_ref[...] = (mid + dot(gated, w_out_ref[...])).astype(jnp.bfloat16).reshape(out_ref.shape)


def call(body, args, outs, cost_us, name, scratch=(), space=pltpu.VMEM):
    return pl.pallas_call(
        body,
        out_shape=[jax.ShapeDtypeStruct(shape, dtype) for shape, dtype in outs],
        in_specs=[pl.BlockSpec(memory_space=space)] * len(args),
        out_specs=[pl.BlockSpec(memory_space=pltpu.VMEM)] * len(outs),
        scratch_shapes=list(scratch),
        compiler_params=pltpu.CompilerParams(vmem_limit_bytes=24 * 2**20),
        cost_estimate=pl.CostEstimate(flops=int(cost_us * 1e9), bytes_accessed=2**18, transcendentals=0),
        name=name,
    )(*args)


def gathered(
    row_devices,
    pair_acts,
    res_mask,
    chain_id,
    in_gain,
    w_left,
    w_right,
    w_mult_gate,
    mult_gain,
    w_mult_out,
    att_gain,
    w_att,
    w_pair_bias,
    cross_bias,
    w_att_out,
):
    row_count, residues, channels = pair_acts.shape
    width = w_left.shape[1] // 2
    heads = w_pair_bias.shape[1]
    own_count = residues // 2
    pairs = own_count * residues
    block_rows = row_count * residues
    tile = 8
    wide = own_count * tile
    bf16, f32 = jnp.bfloat16, jnp.float32

    def swap(x, shift):
        return lax.ppermute(x, "row", [(i, i ^ shift) for i in range(row_devices)])

    base, held = [0], pair_acts
    far, near, side = 9, 5, 3

    def spread(shifts):
        return [o ^ s for s in shifts for o in base]

    shift = row_devices // 2
    while shift > far:
        held = jnp.concatenate([held, swap(held, shift + 1)], 0)
        base = base + [o ^ (shift + 1) for o in base]
        shift //= 2
    from_far = swap(held, far)
    from_corner = swap(held, near ^ side)
    from_near = swap(held, near)
    from_side = swap(held, side)

    weights = [
        in_gain[None],
        mult_gain[None],
        att_gain[None],
        w_right,
        w_left,
        w_mult_gate,
        w_mult_out,
        w_att,
        w_pair_bias.T,
        w_att_out,
        held,
    ]
    live, crossing, keep, far_crossing, far_keep, in_g, mult_g, att_g, w_r, w_l, w_g, w_m, w_a, w_b, w_o, held = call(
        functools.partial(stage_kernel, len(weights)),
        [
            pltpu.with_memory_space_constraint(x, pltpu.HBM)
            for x in (cross_bias, chain_id, res_mask[None], chain_id[None], *weights)
        ],
        [((residues, channels), f32)] + 2 * [((heads * row_count, wide), f32), ((residues // tile, wide), f32)]
        + [(w.shape, w.dtype) for w in weights],
        0.05,
        "stage",
        [
            pltpu.SMEM((heads,), f32),
            pltpu.SMEM((residues,), jnp.int32),
            pltpu.VMEM((1, residues), jnp.int32),
            pltpu.VMEM((1, residues), jnp.int32),
            pltpu.SemaphoreType.DMA((len(weights) + 4,)),
        ],
        space=pltpu.HBM,
    )
    from_far_near = swap(from_far, near)
    from_far_corner = swap(from_far, near ^ side)
    from_far_side = swap(from_far, side)

    early = spread([0, far, near ^ side, near, side])
    early_pieces = [held, from_far, from_corner, from_near, from_side]

    def rows_like(count, dtype, blocks=None):
        return (((blocks or own_count // row_count) * block_rows, count), dtype)

    early_right, early_left, early_gate = call(
        functools.partial(early_kernel, early, row_count),
        [live, in_g, w_r, w_l, w_g, *early_pieces],
        [rows_like(width, bf16, len(early)), rows_like(width, f32, len(early)), rows_like(channels, f32, len(early))],
        0.05,
        "early_edges",
    )
    middle, last = spread([far ^ near ^ side]), spread([far ^ near, far ^ side])
    middle_pieces, last_pieces = [from_far_corner], [from_far_near, from_far_side]
    middle_right, middle_normed = call(
        functools.partial(middle_kernel, middle, row_count),
        [live, in_g, w_r, *middle_pieces],
        [rows_like(width, bf16, len(middle)), rows_like(channels, bf16, len(middle))],
        0.05,
        "middle_edges",
    )
    right, last_normed = call(
        functools.partial(right_kernel, [early, middle], last, row_count),
        [live, in_g, w_r, early_right, middle_right, *last_pieces],
        [rows_like(width, bf16), rows_like(channels, bf16, len(last))],
        0.05,
        "right_edges",
    )
    other = swap(right, 1)
    left, gate, acts, near_product = call(
        functools.partial(left_kernel, early, [middle, last], row_count, residues),
        [right, w_l, w_g, early_left, early_gate, middle_normed, last_normed]
        + early_pieces
        + middle_pieces
        + last_pieces,
        [rows_like(width, f32), rows_like(channels, f32), rows_like(channels, bf16)]
        + [((own_count * own_count, width), f32)],
        1.5,
        "left_edges",
        scratch=[pltpu.VMEM((pairs + own_count, width), f32)],
    )
    mid, normed_mid = call(
        functools.partial(product_kernel, row_count, residues),
        [left, other, near_product, gate, acts, jnp.concatenate([in_g, mult_g, att_g], 0), w_m],
        [((pairs, channels), bf16), ((pairs, channels), bf16)],
        2.4,
        "product",
        scratch=[pltpu.VMEM((pairs + own_count, width), f32), pltpu.VMEM((pairs + 2 * row_count, width), f32)],
    )
    normed_other = swap(normed_mid, 1)
    groups, asked_rows = residues // tile, heads * row_count * tile
    asked, gate_att, top, total, context = call(
        functools.partial(near_attend_kernel, row_count, residues),
        [normed_mid, w_a, w_b, crossing, keep],
        [((groups, asked_rows, channels), bf16), ((block_rows, w_o.shape[0]), f32)]
        + 3 * [((groups, asked_rows, channels), f32)],
        1.2,
        "near_attend",
        scratch=[pltpu.VMEM((own_count, residues, channels), f32)],
    )
    (out,) = call(
        functools.partial(attend_kernel, row_count),
        [normed_other, mid, asked, gate_att, top, total, context, far_crossing, far_keep, w_a, w_b, w_o],
        [((row_count, residues, channels), bf16)],
        1.5,
        "attend",
        scratch=[pltpu.VMEM((own_count, residues, channels), f32)],
    )
    return out


def solution(mesh):
    placed = (
        P(("groups", "row"), None, None),
        P("groups"),
        P("groups"),
        P(),
        P(),
        P(),
        P(),
        P(),
        P(),
        P(),
        P(),
        P(),
        P(),
        P(),
    )
    row_devices = mesh.shape["row"]

    def whole(pair_acts, *others):
        row_count, residues, channels = pair_acts.shape
        in_vmem = 4 * residues * residues * channels <= vmem_share
        paired = row_devices % 16 == 0 and row_devices & (row_devices - 1) == 0 and residues % 8 == 0
        if in_vmem and paired:
            return gathered(row_devices, pair_acts, *others)
        return shards(pair_acts, *others)

    return jax.shard_map(
        whole,
        mesh=mesh,
        in_specs=placed,
        out_specs=P(("groups", "row"), None, None),
        check_vma=False,
    )
```
